32 devices in a mesh: section: 2 (over core), dp: 4 (over z), tensor: 4 (over y, x).
Axes of the slice: x: 2, y: 2, z: 4, core: 2. Of those that a mesh axis runs over, the one named last changes fastest.
Arguments:
- states: bfloat16 [2, 4096, 1024], P(None, ('dp', 'tensor')), may hold values from -6 to 6
- segment_ids: int32 [2, 4096], P(None, 'dp'), may hold values from 0 to 519, as said below
- cotangent: bfloat16 [2, 4096, 1024], P(None, ('dp', 'tensor')), may hold values from -6 to 6
- qkv_weight: bfloat16 [2, 1024, 3, 1024], P('section', None, None, 'tensor'), may hold values from -0.1875 to 0.1875
- out_weight: bfloat16 [2, 1024, 1024], P('section', 'tensor'), may hold values from -0.5 to 0.5
- up_weight: bfloat16 [2, 1024, 4096], P('section', None, 'tensor'), may hold values from -0.1875 to 0.1875
- up_bias: bfloat16 [2, 4096], P('section', 'tensor'), may hold values from -3 to 3
- down_weight: bfloat16 [2, 4096, 1024], P('section', 'tensor'), may hold values from -0.09375 to 0.09375
- norm_gain: bfloat16 [2, 2, 1024], P('section'), may hold values from 0.5 to 1.5
- shift_vec: bfloat16 [2, 4, 1024], P('section'), may hold values from -2 to 2
- prefix: bfloat16 [2, 2, 64, 1024], P('section', None, None, 'tensor'), may hold values from -6 to 6
Outputs:
- hidden_out: bfloat16 [2, 2, 4096, 1024], P('section', None, ('dp', 'tensor'))
- input_grads: float32 [2, 2, 4096, 1024], P('section', None, ('dp', 'tensor'))
- prefix_grads: float32 [2, 2, 64, 1024], P('section', None, None, 'tensor')
The draws below stay inside these ranges and needn't reach their ends.
Inputs may be any that keep to these rules, and one draw needn't show every extreme that they name: `segment_ids`: segment numbers never fall along a micro-batch; every sequence of 1024 tokens starts a new segment, so sequences share none; in every sequence one segment covers all of it but at most 32 tokens at each end. The k-th sequence of the whole batch (micro-batches in order) uses numbers from k * (65) to (k + 1) * 65 - 1, and its last token holds the highest of them.
All inputs are finite; a program needn't handle non-finite values.
Results may differ from the reference program's by a relative error of at most 0.03.
Values may be sent and summed in bfloat16 or wider, within the bound.
A program may use at most 192 MiB of HBM per device.

```python
import math
import jax
import jax.numpy as jnp
from jax import lax

D = 1024
FF = 4096
HEADS = 16
HEAD = 64
PREFIX = 64
LEN = 1024
MICRO = 2
ROWS = 4096


def draw_segment_ids(key, part):
    key = jax.random.fold_in(key, 7)
    key_front, key_back, key_rough = jax.random.split(key, 3)
    sequences = MICRO * ROWS // LEN
    edge_span = LEN // 32
    places = jnp.arange(LEN, dtype=jnp.int32)[None, :]
    front_edge = jax.random.randint(key_front, (sequences, 1), 1, edge_span + 1)
    tail_edge = LEN - jax.random.randint(key_back, (sequences, 1), 1, edge_span + 1)
    rough_starts = jax.random.randint(key_rough, (sequences, LEN), 0, 6) == 0
    outside = (places < front_edge) | (places > tail_edge)
    starts_all = (places == 0) | (places == front_edge) | (places == tail_edge) | rough_starts & outside
    starts_int = starts_all.astype(jnp.int32)
    counted = jnp.cumsum(starts_int, axis=1)
    before = counted - 1
    after = counted[:, -1:] - counted
    local_number = jnp.where(places < front_edge, before, jnp.where(places < tail_edge, edge_span, 2 * edge_span - after))
    block_start = jnp.arange(sequences, dtype=jnp.int32)[:, None] * (2 * edge_span + 1)
    numbers = block_start + local_number
    return numbers.reshape(MICRO, ROWS).astype(jnp.int32)


def levels(key, dims, shards, low, largest):
    level = 1.0
    for position, parts in shards:
        steps = jax.random.uniform(jax.random.fold_in(jax.random.fold_in(key, 6), position), (parts,), jnp.float32, low / len(shards), largest / len(shards))
        level = level * jnp.repeat(jnp.exp(steps), dims[position] // parts).reshape((-1,) + (1,) * (len(dims) - 1 - position))
    return level


def scatter_about(own_key, extent, scale, most, shards=(), held_as=jnp.bfloat16):
    entries = jax.random.normal(own_key, extent, jnp.float32) * scale
    if len(shards) > 0:
        entries = levels(own_key, extent, shards, -0.22, 0.18) * entries
    return jnp.clip(entries, min=-most, max=most).astype(held_as)


def setup_inputs(seed: int = 0) -> dict:
    key_list = jax.random.split(jax.random.key(seed), 12)
    return {
        "states": scatter_about(key_list[0], (MICRO, ROWS, D), 1.0, 6.0, ((1, 16),)),
        "segment_ids": draw_segment_ids(jax.random.fold_in(key_list[11], 71), 0),
        "cotangent": scatter_about(key_list[2], (MICRO, ROWS, D), 1.0, 6.0, ((1, 16),)),
        "qkv_weight": scatter_about(key_list[3], (2, D, 3, D), D ** -0.5, 0.1875, ((0, 2), (3, 4))),
        "out_weight": scatter_about(key_list[4], (2, D, D), (D // 8) ** -0.5, 0.5, ((0, 2), (1, 4))),
        "up_weight": scatter_about(key_list[5], (2, D, FF), D ** -0.5, 0.1875, ((0, 2), (2, 4))),
        "up_bias": scatter_about(key_list[6], (2, FF), 0.5, 3.0, ((0, 2), (1, 4))),
        "down_weight": scatter_about(key_list[7], (2, FF, D), FF ** -0.5, 0.09375, ((0, 2), (1, 4))),
        "norm_gain": jnp.clip(1.0 + 0.1 * jax.random.normal(key_list[8], (2, 2, D), jnp.float32), 0.5, 1.5).astype(jnp.bfloat16),
        "shift_vec": scatter_about(key_list[9], (2, 4, D), 0.3, 2.0, ((0, 2),)),
        "prefix": scatter_about(key_list[10], (2, 2, PREFIX, D), 1.0, 6.0, ((0, 2), (3, 4))),
    }


@jax.custom_vjp
def low(v):
    return lax.optimization_barrier(v.astype(jnp.bfloat16)).astype(jnp.float32)

@jax.custom_vjp
def lowered_backward(v):
    return v

def low_keep(v):
    return (low(v), None)

def low_pass(kept, grad):
    return (grad,)

def back_keep(v):
    return (v, None)

def back_low(kept, grad):
    return (low(grad),)
low.defvjp(low_keep, low_pass)
lowered_backward.defvjp(back_keep, back_low)

def rounded_pair(value):
    return low(lowered_backward(value))

def norm_rows(values, gain, bias):
    center = values - lax.optimization_barrier(jnp.mean(values, axis=-1, keepdims=True))
    spread = lax.optimization_barrier(jnp.mean(center * center, axis=-1, keepdims=True))
    return center * lax.rsqrt(spread + 1e-05) * gain + bias

def attend_one(sequence_item, keys_pre, values_pre):
    highest_precision = lax.Precision.HIGHEST
    queries, keys_seq, values_seq, segment = sequence_item
    keys_all = jnp.concatenate([keys_pre, keys_seq], 0)
    values_all = jnp.concatenate([values_pre, values_seq], 0)
    scores = jnp.einsum('qhe,khe->hqk', queries, keys_all, precision=highest_precision) * 0.125
    scores = lowered_backward(scores)
    visible = jnp.concatenate([jnp.full((LEN, PREFIX), True), segment[:, None] == segment[None, :]], 1)
    scores = jnp.where(visible[None], scores, -1e+30)
    weights_soft = low(jax.nn.softmax(scores, axis=-1))
    return jnp.einsum('hqk,khe->qhe', weights_soft, values_all, precision=highest_precision)

def layer(block_rows, segment, weight_set, prefix_pair):
    highest_precision = lax.Precision.HIGHEST
    query_key_value_matrix, output_matrix, up_matrix, up_offset_bias, down_matrix, gains, prefix_shifts = weight_set
    sequences = block_rows.shape[0]
    inner_width = lowered_backward(block_rows)
    projected_rows = rounded_pair(jnp.einsum('vhk,kuw->vhuw', inner_width, query_key_value_matrix, precision=highest_precision))
    heads_form = projected_rows.reshape(sequences, LEN, 3, HEADS, HEAD)
    keys_pre = prefix_pair[0].reshape(PREFIX, HEADS, HEAD)
    values_pre = prefix_pair[1].reshape(PREFIX, HEADS, HEAD)
    attend_fn = jax.checkpoint(lambda sequence_item: attend_one(sequence_item, keys_pre, values_pre))
    merged_heads = lax.map(attend_fn, (heads_form[:, :, 0], heads_form[:, :, 1], heads_form[:, :, 2], segment))
    merged_heads = rounded_pair(merged_heads.reshape(sequences, LEN, D))
    attended_rows = lowered_backward(jnp.einsum('wya,at->wyt', merged_heads, output_matrix, precision=highest_precision) + prefix_shifts[0])
    middle = norm_rows(block_rows + attended_rows, gains[0], prefix_shifts[1])
    middle_lowered = rounded_pair(middle)
    hidden_state = lowered_backward(jnp.einsum('pze,en->pzn', middle_lowered, up_matrix, precision=highest_precision) + up_offset_bias)
    active_units = low(jax.nn.gelu(hidden_state, approximate=False))
    branch_output = lowered_backward(jnp.einsum('unz,zc->unc', active_units, down_matrix, precision=highest_precision) + prefix_shifts[2])
    return norm_rows(middle + branch_output, gains[1], prefix_shifts[3])

def reference(states, segment_ids, cotangent, qkv_weight, out_weight, up_weight, up_bias, down_weight, norm_gain, shift_vec, prefix):
    sequences = MICRO * ROWS // LEN
    group_size = math.gcd(sequences, max(1, 4096 // LEN))
    groups = sequences // group_size

    def section_set(index):
        return (qkv_weight[index].astype(jnp.float32), out_weight[index].astype(jnp.float32), up_weight[index].astype(jnp.float32), up_bias[index].astype(jnp.float32), down_weight[index].astype(jnp.float32), norm_gain[index].astype(jnp.float32), shift_vec[index].astype(jnp.float32))
    first_set = section_set(0)
    second_set = section_set(1)
    prefix_first = prefix[0].astype(jnp.float32)
    prefix_second = prefix[1].astype(jnp.float32)
    block_all = states.astype(jnp.float32).reshape(groups, group_size, LEN, D)
    segment_all = segment_ids.reshape(groups, group_size, LEN)
    cotangent_all = cotangent.astype(jnp.float32).reshape(groups, group_size, LEN, D)

    def group_step(running, group_item):
        block_rows, segment, cotangent_part = group_item
        out_first, back_first = jax.vjp(lambda inputs, pair: layer(inputs, segment, first_set, pair), block_rows, prefix_first)
        passed, back_pass = jax.vjp(rounded_pair, out_first)
        out_second, back_second = jax.vjp(lambda inputs, pair: layer(inputs, segment, second_set, pair), passed, prefix_second)
        grad_passed, grad_pair_second = back_second(cotangent_part)
        grad_out_first, = back_pass(grad_passed)
        grad_inputs, grad_pair_first = back_first(grad_out_first)
        running = (running[0] + grad_pair_first, running[1] + grad_pair_second)
        return (running, (passed, out_second, grad_inputs, grad_passed))
    zero_grads = jnp.zeros((2, PREFIX, D), jnp.float32)
    (grad_first, grad_second), (out_zero, out_one, grads_zero, grads_one) = lax.scan(group_step, (zero_grads, zero_grads), (block_all, segment_all, cotangent_all))
    whole_shape = (MICRO, ROWS, D)
    hidden_out = jnp.stack([out_zero.reshape(whole_shape), out_one.reshape(whole_shape)]).astype(jnp.bfloat16)
    input_grads = jnp.stack([grads_zero.reshape(whole_shape), grads_one.reshape(whole_shape)])
    prefix_grads = jnp.stack([grad_first, grad_second])
    return (hidden_out, input_grads, prefix_grads)
```

```python
import functools

import jax
import jax.numpy as jnp
from jax import lax
from jax.experimental import pallas as pl
from jax.experimental.pallas import tpu as pltpu
from jax.sharding import PartitionSpec as P

D = 1024
HEAD = 64
PAIR = 2 * HEAD
PREFIX = 64
LEN = 1024
SPAN = LEN // 32
LABELS = 128
HIDDEN = -1e30
F32 = jnp.float32
BF16 = jnp.bfloat16


def dot(a, b):
    return jnp.dot(a, b, preferred_element_type=F32)


def dot_t(a, b):
    return lax.dot_general(a, b, (((1,), (1,)), ((), ())), preferred_element_type=F32)


def head_lanes(rows, head):
    lanes = lax.broadcasted_iota(jnp.int32, (rows, PAIR), 1)
    return (lanes >= head * HEAD) & (lanes < (head + 1) * HEAD)


def fill_keys(keys, own, sib, pre, own_lab, sib_lab):
    rows = own.shape[0]
    keys[:rows, :PAIR] = own[...]
    keys[rows : 2 * rows, :PAIR] = sib[...]
    keys[2 * rows :, :PAIR] = pre[...]
    keys[:rows, PAIR:] = own_lab[...]
    keys[rows : 2 * rows, PAIR:] = sib_lab[...]
    keys[2 * rows :, PAIR:] = jnp.zeros((PREFIX, LABELS), BF16)


def attend_kernel(block, q, ko, vo, ks, vs, kp, vp, lab_q, lab_o, lab_s, out, lse, keys, vals_t):
    rows = q.shape[0]
    fill_keys(keys, ko, ks, kp, lab_o, lab_s)
    vals_t[:, :rows] = vo[...].T
    vals_t[:, rows : 2 * rows] = vs[...].T
    vals_t[:, 2 * rows :] = vp[...].T
    for start in range(0, rows, block):
        part = pl.ds(start, block)
        query = q[part, :] * 0.125
        label = lab_q[part, :]
        results = []
        for head in range(2):
            mine = jnp.where(head_lanes(block, head), query, 0)
            scores = dot_t(keys[...], jnp.concatenate([mine, label], 1))
            peak = jnp.max(scores, axis=0, keepdims=True)
            weights = jnp.exp(scores - peak)
            total = jnp.sum(weights, axis=0, keepdims=True)
            merged = dot(vals_t[head * HEAD : (head + 1) * HEAD, :], weights.astype(BF16))
            results.append(merged / total)
            lse[0, head : head + 1, part] = peak + jnp.log(total)
        out[part, :] = jnp.concatenate(results, 0).T.astype(BF16)


def attend_back_kernel(
    block, q, ko, vo, ks, vs, kp, vp, lab_q, lab_o, lab_s, out, lse, grad,
    dq, dko, dvo, dks, dvs, dkp, dvp, keys, vals, keys_t, dk_sum, dv_sum,
):
    rows = q.shape[0]
    fill_keys(keys, ko, ks, kp, lab_o, lab_s)
    vals[:rows, :] = vo[...]
    vals[rows : 2 * rows, :] = vs[...]
    vals[2 * rows :, :] = vp[...]
    keys_t[:, :rows] = ko[...].T
    keys_t[:, rows : 2 * rows] = ks[...].T
    keys_t[:, 2 * rows :] = kp[...].T
    for start in range(0, rows, block):
        part = pl.ds(start, block)
        query = q[part, :] * 0.125
        label = lab_q[part, :]
        grad_part = grad[part, :]
        product = (grad_part.astype(F32) * out[part, :].astype(F32)).T
        queries, grads, weights_all, scores_all, results = [], [], [], [], []
        for head in range(2):
            span = slice(head * HEAD, (head + 1) * HEAD)
            mine = jnp.where(head_lanes(block, head), query, 0)
            mine_grad = jnp.where(head_lanes(block, head), grad_part, 0)
            scores = dot_t(keys[...], jnp.concatenate([mine, label], 1))
            weights = jnp.exp(scores - lse[0, head : head + 1, part])
            delta = jnp.sum(product[span], axis=0, keepdims=True)
            grad_scores = (weights * (dot_t(vals[...], mine_grad) - delta)).astype(BF16)
            results.append(dot(keys_t[span, :], grad_scores))
            queries.append(mine)
            grads.append(mine_grad)
            weights_all.append(weights.astype(BF16))
            scores_all.append(grad_scores)
        dq[part, :] = (jnp.concatenate(results, 0).T * 0.125).astype(BF16)
        dv_part = dot(jnp.concatenate(weights_all, 1), jnp.concatenate(grads, 0))
        dk_part = dot(jnp.concatenate(scores_all, 1), jnp.concatenate(queries, 0))
        if start == 0:
            dv_sum[...] = dv_part
            dk_sum[...] = dk_part
        else:
            dv_sum[...] += dv_part
            dk_sum[...] += dk_part
    dko[...] = dk_sum[:rows, :]
    dvo[...] = dv_sum[:rows, :]
    dks[...] = dk_sum[rows : 2 * rows, :].astype(BF16)
    dvs[...] = dv_sum[rows : 2 * rows, :].astype(BF16)
    dkp[...] = dk_sum[2 * rows :, :]
    dvp[...] = dv_sum[2 * rows :, :]


def attention_specs(rows, pairs):
    def column(height, offset):
        return pl.BlockSpec((height, PAIR), lambda p: (0, offset + p))

    labels = pl.BlockSpec((rows, LABELS), lambda p: (0, 0))
    ins = [
        column(rows, 0), column(rows, pairs), column(rows, 2 * pairs),
        column(rows, 0), column(rows, pairs),
        column(PREFIX, 0), column(PREFIX, 0),
        labels, labels, labels,
    ]
    return column, ins, pl.BlockSpec((1, 8, rows), lambda p: (p, 0, 0))


def attend(qkv, kv_sib, pre, labels):
    rows, width = qkv.shape[0], qkv.shape[1] // 3
    pairs = width // PAIR
    column, ins, lse_spec = attention_specs(rows, pairs)
    size = 2 * rows + PREFIX
    return pl.pallas_call(
        functools.partial(attend_kernel, min(rows, 256)),
        grid=(pairs,),
        in_specs=ins,
        out_specs=[column(rows, 0), lse_spec],
        out_shape=[
            jax.ShapeDtypeStruct((rows, width), BF16),
            jax.ShapeDtypeStruct((pairs, 8, rows), F32),
        ],
        scratch_shapes=[pltpu.VMEM((size, PAIR + LABELS), BF16), pltpu.VMEM((PAIR, size), BF16)],
        compiler_params=pltpu.CompilerParams(vmem_limit_bytes=40 << 20),
        cost_estimate=pl.CostEstimate(
            flops=2 * 2 * rows * size * width, transcendentals=rows * size * width // HEAD,
            bytes_accessed=16 * rows * width,
        ),
        name="attend",
    )(qkv, qkv, qkv, kv_sib, kv_sib, pre[0], pre[1], *labels)


def attend_back(qkv, kv_sib, pre, labels, merged, lse, grad):
    rows, width = qkv.shape[0], qkv.shape[1] // 3
    pairs = width // PAIR
    column, ins, lse_spec = attention_specs(rows, pairs)
    size = 2 * rows + PREFIX
    shape = jax.ShapeDtypeStruct
    return pl.pallas_call(
        functools.partial(attend_back_kernel, min(rows, 256)),
        grid=(pairs,),
        in_specs=ins + [column(rows, 0), lse_spec, column(rows, 0)],
        out_specs=[column(rows, 0)] * 5 + [column(PREFIX, 0)] * 2,
        out_shape=[
            shape((rows, width), BF16),
            shape((rows, width), F32), shape((rows, width), F32),
            shape((rows, width), BF16), shape((rows, width), BF16),
            shape((PREFIX, width), F32), shape((PREFIX, width), F32),
        ],
        scratch_shapes=[
            pltpu.VMEM((size, PAIR + LABELS), BF16), pltpu.VMEM((size, PAIR), BF16),
            pltpu.VMEM((PAIR, size), BF16), pltpu.VMEM((size, PAIR), F32), pltpu.VMEM((size, PAIR), F32),
        ],
        compiler_params=pltpu.CompilerParams(vmem_limit_bytes=40 << 20),
        cost_estimate=pl.CostEstimate(
            flops=5 * 2 * rows * size * width, transcendentals=rows * size * width // HEAD,
            bytes_accessed=32 * rows * width,
        ),
        name="attend_back",
    )(qkv, qkv, qkv, kv_sib, kv_sib, pre[0], pre[1], *labels, merged, lse, grad)


def norm_stats(values):
    center = values - jnp.mean(values, axis=-1, keepdims=True)
    scale = lax.rsqrt(jnp.mean(center * center, axis=-1, keepdims=True) + 1e-05)
    return center * scale, scale


def norm_back(grad, gain, normed, scale):
    dn = grad * gain
    return scale * (
        dn
        - jnp.mean(dn, axis=-1, keepdims=True)
        - normed * jnp.mean(dn * normed, axis=-1, keepdims=True)
    )


def gelu_pair(u):
    cdf = 0.5 * (1.0 + lax.erf(u * 0.7071067811865476))
    pdf = jnp.exp(-0.5 * u * u) * 0.3989422804014327
    return (u * cdf).astype(BF16), (cdf + u * pdf).astype(BF16)


class Links:
    def __init__(self):
        self.core = lax.axis_index("section")
        self.place = lax.axis_index("tensor")
        self.size = lax.axis_size("tensor")
        self.low = self.place % 2
        self.high = self.place // 2
        self.group = self.size // 2

    def sibling(self, a, only=None):
        pairs = [(0, 1), (1, 0)] if only is None else [(only, 1 - only)]
        return lax.ppermute(a, "section", pairs)

    def across(self, a, only=None):
        if only is None:
            return lax.ppermute(a, "tensor", [(t, t ^ 1) for t in range(self.size)])
        pairs = [(only * self.size + t, only * self.size + (t ^ 1)) for t in range(self.size)]
        return lax.ppermute(a, ("section", "tensor"), pairs)

    def diagonal(self, a, source):
        pairs = [(source * self.size + t, (1 - source) * self.size + (t ^ 1)) for t in range(self.size)]
        return lax.ppermute(a, ("section", "tensor"), pairs)

    def from_ahead(self, a, by):
        g = self.group
        pairs = [(2 * ((h + by) % g) + p, 2 * h + p) for h in range(g) for p in range(2)]
        return lax.ppermute(a, "tensor", pairs)

    def gather(self, a):
        return [a] + [self.from_ahead(a, k) for k in range(1, self.group)]

    def scatter_sum(self, part_fn):
        arrived = [self.from_ahead(part_fn(k).astype(BF16), self.group - k) for k in range(1, self.group)]
        total = part_fn(0)
        for a in arrived:
            total = total + a.astype(F32)
        return total


def forward(links, x, weights, pre, labels):
    qkv_w, out_w, up_w, up_b, down_w, gains, shifts = weights
    width = out_w.shape[0]
    blocks = [dot(b, qkv_w).astype(BF16) for b in links.gather(x)]
    qkv = jnp.concatenate(blocks, 0)
    kv_sib = links.sibling(qkv[:, width:])
    merged, lse = attend(qkv, kv_sib, pre, labels)
    rows = x.shape[0]
    attended = links.scatter_sum(lambda k: dot(merged[k * rows : (k + 1) * rows], out_w)) + shifts[0]
    normed_first, scale_first = norm_stats(x.astype(F32) + attended)
    middle = normed_first * gains[0] + shifts[1]
    blocks = links.gather(middle.astype(BF16))
    pairs = [gelu_pair(dot(b, up_w) + up_b) for b in blocks]
    branch = links.scatter_sum(lambda k: dot(pairs[k][0], down_w)) + shifts[2]
    normed_last, scale_last = norm_stats(middle + branch)
    result = (normed_last * gains[1] + shifts[3]).astype(BF16)
    slopes = [p[1] for p in pairs]
    return result, (qkv, kv_sib, merged, lse, normed_first, scale_first, slopes, normed_last, scale_last)


def backward(links, grad, weights, pre, labels, kept):
    qkv_w, out_w, up_w, up_b, down_w, gains, shifts = weights
    qkv, kv_sib, merged, lse, normed_first, scale_first, slopes, normed_last, scale_last = kept
    rows = grad.shape[0]
    grad_second = norm_back(grad.astype(F32), gains[1], normed_last, scale_last)
    blocks = links.gather(grad_second.astype(BF16))
    hiddens = [
        (dot_t(b, down_w) * s.astype(F32)).astype(BF16) for b, s in zip(blocks, slopes, strict=True)
    ]
    grad_middle = grad_second + links.scatter_sum(lambda k: dot_t(hiddens[k], up_w))
    grad_first = norm_back(grad_middle, gains[0], normed_first, scale_first)
    blocks = links.gather(grad_first.astype(BF16))
    grad_merged = jnp.concatenate([dot_t(b, out_w).astype(BF16) for b in blocks], 0)
    dq, dko, dvo, dks, dvs, dkp, dvp = attend_back(qkv, kv_sib, pre, labels, merged, lse, grad_merged)
    arrived = links.sibling(jnp.concatenate([dks, dvs], 1)).astype(F32)
    width = out_w.shape[0]
    dk = (dko + arrived[:, :width]).astype(BF16)
    dv = (dvo + arrived[:, width:]).astype(BF16)
    dqkv = jnp.concatenate([dq, dk, dv], 1)
    grad_inputs = grad_first + links.scatter_sum(
        lambda k: dot_t(dqkv[k * rows : (k + 1) * rows], qkv_w)
    )
    return grad_inputs, jnp.stack([dkp, dvp])


def spread_weights(links, arrays):
    first = links.core == 0
    layers = ([], [])
    for layer in range(2):
        for a in arrays:
            other = links.across(a, layer)
            sib_a, sib_other = links.sibling(a, layer), links.sibling(other, layer)
            here = links.core == layer
            layers[layer].append((jnp.where(here, a, sib_a), jnp.where(here, other, sib_other)))
    return layers


def sum_over_dp(a):
    size = lax.axis_size("dp")
    step = 1
    if size & (size - 1):
        return lax.psum(a, "dp")
    while step < size:
        a = a + lax.ppermute(a, "dp", [(i, i ^ step) for i in range(size)])
        step *= 2
    return a


def local(
    states, segment_ids, cotangent, qkv_weight, out_weight, up_weight, up_bias, down_weight,
    norm_gain, shift_vec, prefix,
):
    links = Links()
    first = links.core == 0
    low = links.low

    def arrange(both):
        mine = lax.dynamic_index_in_dim(both, low, 0, keepdims=False)
        other = lax.dynamic_index_in_dim(both, 1 - low, 0, keepdims=False)
        return jnp.where(first, mine, links.across(other, 1))

    x = arrange(states)
    grad = arrange(cotangent)

    segment = lax.dynamic_index_in_dim(segment_ids, low, 0, keepdims=False)
    classes = (segment[-1] - segment).reshape(links.group, 2, -1)
    classes = jnp.roll(classes, -links.high, 0)
    parity = jnp.where(first, low, 1 - low)
    own = lax.dynamic_index_in_dim(classes, parity, 1, keepdims=False).reshape(-1)
    sib = lax.dynamic_index_in_dim(classes, 1 - parity, 1, keepdims=False).reshape(-1)
    numbers = jnp.arange(LABELS)[None, :]
    label_q = (own[:, None] == numbers).astype(BF16)
    known = numbers <= 2 * SPAN
    label_o = jnp.where(known & (own[:, None] != numbers), HIDDEN, 0.0).astype(BF16)
    label_s = jnp.where(known & (sib[:, None] != numbers), HIDDEN, 0.0).astype(BF16)
    labels = (label_q, label_o, label_s)

    small = jnp.concatenate(
        [norm_gain[0], shift_vec[0]], 0
    )
    small_sib = links.sibling(small)
    layers = spread_weights(
        links,
        [jnp.transpose(qkv_weight[0], (1, 0, 2)), prefix[0], out_weight[0], up_weight[0], up_bias, down_weight[0]],
    )
    weights, prefixes = [], []
    for layer in range(2):
        qkv, pre, out, up, bias, down = layers[layer]
        vectors = jnp.where(links.core == layer, small, small_sib).astype(F32)
        weights.append((
            jnp.concatenate([p[i] for i in range(3) for p in qkv], 1),
            jnp.concatenate(out, 0),
            jnp.concatenate(up, 1),
            jnp.concatenate(bias, 1).astype(F32),
            jnp.concatenate(down, 0),
            vectors[:2],
            vectors[2:],
        ))
        prefixes.append(jnp.concatenate(pre, 2))

    y0, kept0 = forward(links, x, weights[0], prefixes[0], labels)
    y1, kept1 = forward(links, y0, weights[1], prefixes[1], labels)
    g1, p1 = backward(links, grad, weights[1], prefixes[1], labels, kept1)
    g0, p0 = backward(links, g1.astype(BF16), weights[0], prefixes[0], labels, kept0)

    def deliver(first_layer, second_layer, wire, dtype):
        near = jnp.where(first, first_layer.astype(dtype), links.sibling(second_layer.astype(wire), 0).astype(dtype))
        far0 = links.diagonal(first_layer.astype(wire), 1)
        far1 = links.across(second_layer.astype(wire), 1)
        far = jnp.where(first, far0, far1).astype(dtype)
        return jnp.stack([jnp.where(low == 0, near, far), jnp.where(low == 0, far, near)])

    hidden_out = deliver(y0, y1, BF16, BF16)
    input_grads = deliver(g0, g1, BF16, F32)

    total = jnp.where(first, p0, p1) + links.sibling(jnp.where(first, p1, p0))
    quarter = total.shape[-1] // 2
    total = total[..., :quarter] + links.across(total[..., quarter:])
    prefix_grads = sum_over_dp(total)
    return hidden_out[None], input_grads[None], prefix_grads[None]


def solution(mesh):
    placed = (
        P(None, ("dp", "tensor"), None),
        P(None, "dp"),
        P(None, ("dp", "tensor"), None),
        P("section", None, None, "tensor"),
        P("section", "tensor", None),
        P("section", None, "tensor"),
        P("section", "tensor"),
        P("section", "tensor", None),
        P("section", None, None),
        P("section", None, None),
        P("section", None, None, "tensor"),
    )
    return jax.shard_map(
        local,
        mesh=mesh,
        in_specs=placed,
        out_specs=(
            P("section", None, ("dp", "tensor"), None),
            P("section", None, ("dp", "tensor"), None),
            P("section", None, None, "tensor"),
        ),
        check_vma=False,
    )
```

```python
import functools

import jax
import jax.numpy as jnp
from jax import lax
from jax.experimental import pallas as pl
from jax.experimental.pallas import tpu as pltpu
from jax.sharding import PartitionSpec as P

D = 1024
HEAD = 64
PAIR = 2 * HEAD
PREFIX = 64
LEN = 1024
SPAN = LEN // 32
LABELS = 128
HIDDEN = -1e30
F32 = jnp.float32
BF16 = jnp.bfloat16


def dot(a, b):
    return jnp.dot(a, b, preferred_element_type=F32)


def dot_t(a, b):
    return lax.dot_general(a, b, (((1,), (1,)), ((), ())), preferred_element_type=F32)


def head_lanes(rows, head):
    lanes = lax.broadcasted_iota(jnp.int32, (rows, PAIR), 1)
    return (lanes >= head * HEAD) & (lanes < (head + 1) * HEAD)


def fill_keys(keys, own, sib, pre, own_lab, sib_lab):
    rows = own.shape[0]
    keys[:rows, :PAIR] = own[...]
    keys[rows : 2 * rows, :PAIR] = sib[...]
    keys[2 * rows :, :PAIR] = pre[...]
    keys[:rows, PAIR:] = own_lab[...]
    keys[rows : 2 * rows, PAIR:] = sib_lab[...]
    keys[2 * rows :, PAIR:] = jnp.zeros((PREFIX, LABELS), BF16)


def attend_kernel(block, q, ko, vo, ks, vs, kp, vp, lab_q, lab_o, lab_s, out, lse, keys, vals_t):
    rows = q.shape[0]
    fill_keys(keys, ko, ks, kp, lab_o, lab_s)
    vals_t[:, :rows] = vo[...].T
    vals_t[:, rows : 2 * rows] = vs[...].T
    vals_t[:, 2 * rows :] = vp[...].T
    for start in range(0, rows, block):
        part = pl.ds(start, block)
        query = q[part, :] * 0.125
        label = lab_q[part, :]
        results = []
        for head in range(2):
            mine = jnp.where(head_lanes(block, head), query, 0)
            scores = dot_t(keys[...], jnp.concatenate([mine, label], 1))
            peak = jnp.max(scores, axis=0, keepdims=True)
            weights = jnp.exp(scores - peak)
            total = jnp.sum(weights, axis=0, keepdims=True)
            merged = dot(vals_t[head * HEAD : (head + 1) * HEAD, :], weights.astype(BF16))
            results.append(merged / total)
            lse[0, head : head + 1, part] = peak + jnp.log(total)
        out[part, :] = jnp.concatenate(results, 0).T.astype(BF16)


def attend_back_kernel(
    block, q, ko, vo, ks, vs, kp, vp, lab_q, lab_o, lab_s, out, lse, grad,
    dq, dko, dvo, dks, dvs, dkp, dvp, keys, vals, keys_t, dk_sum, dv_sum,
):
    rows = q.shape[0]
    fill_keys(keys, ko, ks, kp, lab_o, lab_s)
    vals[:rows, :] = vo[...]
    vals[rows : 2 * rows, :] = vs[...]
    vals[2 * rows :, :] = vp[...]
    keys_t[:, :rows] = ko[...].T
    keys_t[:, rows : 2 * rows] = ks[...].T
    keys_t[:, 2 * rows :] = kp[...].T
    for start in range(0, rows, block):
        part = pl.ds(start, block)
        query = q[part, :] * 0.125
        label = lab_q[part, :]
        grad_part = grad[part, :]
        product = (grad_part.astype(F32) * out[part, :].astype(F32)).T
        queries, grads, weights_all, scores_all, results = [], [], [], [], []
        for head in range(2):
            span = slice(head * HEAD, (head + 1) * HEAD)
            mine = jnp.where(head_lanes(block, head), query, 0)
            mine_grad = jnp.where(head_lanes(block, head), grad_part, 0)
            scores = dot_t(keys[...], jnp.concatenate([mine, label], 1))
            weights = jnp.exp(scores - lse[0, head : head + 1, part])
            delta = jnp.sum(product[span], axis=0, keepdims=True)
            grad_scores = (weights * (dot_t(vals[...], mine_grad) - delta)).astype(BF16)
            results.append(dot(keys_t[span, :], grad_scores))
            queries.append(mine)
            grads.append(mine_grad)
            weights_all.append(weights.astype(BF16))
            scores_all.append(grad_scores)
        dq[part, :] = (jnp.concatenate(results, 0).T * 0.125).astype(BF16)
        dv_part = dot(jnp.concatenate(weights_all, 1), jnp.concatenate(grads, 0))
        dk_part = dot(jnp.concatenate(scores_all, 1), jnp.concatenate(queries, 0))
        if start == 0:
            dv_sum[...] = dv_part
            dk_sum[...] = dk_part
        else:
            dv_sum[...] += dv_part
            dk_sum[...] += dk_part
    dko[...] = dk_sum[:rows, :]
    dvo[...] = dv_sum[:rows, :]
    dks[...] = dk_sum[rows : 2 * rows, :].astype(BF16)
    dvs[...] = dv_sum[rows : 2 * rows, :].astype(BF16)
    dkp[...] = dk_sum[2 * rows :, :]
    dvp[...] = dv_sum[2 * rows :, :]


def attention_specs(rows, pairs):
    def column(height, offset):
        return pl.BlockSpec((height, PAIR), lambda p: (0, offset + p))

    labels = pl.BlockSpec((rows, LABELS), lambda p: (0, 0))
    ins = [
        column(rows, 0), column(rows, pairs), column(rows, 2 * pairs),
        column(rows, 0), column(rows, pairs),
        column(PREFIX, 0), column(PREFIX, 0),
        labels, labels, labels,
    ]
    return column, ins, pl.BlockSpec((1, 8, rows), lambda p: (p, 0, 0))


def attend(qkv, kv_sib, pre, labels):
    rows, width = qkv.shape[0], qkv.shape[1] // 3
    pairs = width // PAIR
    column, ins, lse_spec = attention_specs(rows, pairs)
    size = 2 * rows + PREFIX
    return pl.pallas_call(
        functools.partial(attend_kernel, min(rows, 256)),
        grid=(pairs,),
        in_specs=ins,
        out_specs=[column(rows, 0), lse_spec],
        out_shape=[
            jax.ShapeDtypeStruct((rows, width), BF16),
            jax.ShapeDtypeStruct((pairs, 8, rows), F32),
        ],
        scratch_shapes=[pltpu.VMEM((size, PAIR + LABELS), BF16), pltpu.VMEM((PAIR, size), BF16)],
        compiler_params=pltpu.CompilerParams(vmem_limit_bytes=40 << 20),
        cost_estimate=pl.CostEstimate(
            flops=2 * 2 * rows * size * width, transcendentals=rows * size * width // HEAD,
            bytes_accessed=16 * rows * width,
        ),
        name="attend",
    )(qkv, qkv, qkv, kv_sib, kv_sib, pre[0], pre[1], *labels)


def attend_back(qkv, kv_sib, pre, labels, merged, lse, grad):
    rows, width = qkv.shape[0], qkv.shape[1] // 3
    pairs = width // PAIR
    column, ins, lse_spec = attention_specs(rows, pairs)
    size = 2 * rows + PREFIX
    shape = jax.ShapeDtypeStruct
    return pl.pallas_call(
        functools.partial(attend_back_kernel, min(rows, 256)),
        grid=(pairs,),
        in_specs=ins + [column(rows, 0), lse_spec, column(rows, 0)],
        out_specs=[column(rows, 0)] * 5 + [column(PREFIX, 0)] * 2,
        out_shape=[
            shape((rows, width), BF16),
            shape((rows, width), F32), shape((rows, width), F32),
            shape((rows, width), BF16), shape((rows, width), BF16),
            shape((PREFIX, width), F32), shape((PREFIX, width), F32),
        ],
        scratch_shapes=[
            pltpu.VMEM((size, PAIR + LABELS), BF16), pltpu.VMEM((size, PAIR), BF16),
            pltpu.VMEM((PAIR, size), BF16), pltpu.VMEM((size, PAIR), F32), pltpu.VMEM((size, PAIR), F32),
        ],
        compiler_params=pltpu.CompilerParams(vmem_limit_bytes=40 << 20),
        cost_estimate=pl.CostEstimate(
            flops=5 * 2 * rows * size * width, transcendentals=rows * size * width // HEAD,
            bytes_accessed=32 * rows * width,
        ),
        name="attend_back",
    )(qkv, qkv, qkv, kv_sib, kv_sib, pre[0], pre[1], *labels, merged, lse, grad)


def norm_stats(values):
    center = values - jnp.mean(values, axis=-1, keepdims=True)
    scale = lax.rsqrt(jnp.mean(center * center, axis=-1, keepdims=True) + 1e-05)
    return center * scale, scale


def norm_back(grad, gain, normed, scale):
    dn = grad * gain
    return scale * (
        dn
        - jnp.mean(dn, axis=-1, keepdims=True)
        - normed * jnp.mean(dn * normed, axis=-1, keepdims=True)
    )


def gelu_pair(u):
    cdf = 0.5 * (1.0 + lax.erf(u * 0.7071067811865476))
    pdf = jnp.exp(-0.5 * u * u) * 0.3989422804014327
    return (u * cdf).astype(BF16), (cdf + u * pdf).astype(BF16)


MESH = pl.DeviceIdType.MESH
ROWS = 256
CORE = 2 * ROWS
CHUNK = 128
STEPS = ROWS // CHUNK
QUARTER = D // 4
UNITS = D
TILE = 256
PAIRS = 4
KEYS = 2 * CORE + PREFIX
SEMS = 128


def gelu_both(u):
    size = jnp.abs(u) * 0.7071067811865476
    t = 1.0 / (1.0 + 0.3275911 * size)
    poly = t * (0.254829592 + t * (-0.284496736 + t * (1.421413741 + t * (-1.453152027 + t * 1.061405429))))
    bell = jnp.exp(-(size * size))
    tail = 0.5 * poly * bell
    cdf = jnp.where(u >= 0, 1.0 - tail, tail)
    return (u * cdf).astype(BF16), (cdf + u * (bell * 0.3989422804014327)).astype(BF16)


def norm_chunk(values):
    center = values - jnp.mean(values, axis=-1, keepdims=True)
    scale = lax.rsqrt(jnp.mean(center * center, axis=-1, keepdims=True) + 1e-05)
    return center * scale, scale


class Copies:
    def __init__(self, send, arrive, here):
        self.send, self.arrive, self.here = send, arrive, here
        self.remotes = self.locals = 0

    def remote(self, src, dst, device, number=None):
        if number is None:
            number = self.remotes
            self.remotes += 1
        copy = pltpu.make_async_remote_copy(
            src_ref=src, dst_ref=dst, send_sem=self.send.at[number], recv_sem=self.arrive.at[number],
            device_id=device, device_id_type=MESH,
        )
        return copy, number

    def local(self, src, dst):
        number = self.locals
        self.locals += 1
        return pltpu.make_async_copy(src, dst, self.here.at[number])


def fused_kernel(
    dp,
    states, cotangent, segments, qkv, out_w, up_w, down_w, pre, pack,
    hidden, grads, pgrads, gup, gdown,
    xb, xg, cot, lab_q, lab_k, qw, ow, uw, dw, pw, pk,
    qs, kv, kvs, mg, lse, n1, r1, n2, r2, slopes,
    mid, acc, act, mrecv, fsnd, fin, fout, fret, gsec, gfirst, gm, gms, gout,
    keys, vals_t, vals, dk_acc, dv_acc, dq, dkv, dkv_send, dkv_recv, dxs, dxr, pacc, psib, pacross, psum, pdp,
    send_sem, arrive_sem, here_sem,
):
    core, z, place = lax.axis_index("section"), lax.axis_index("dp"), lax.axis_index("tensor")
    low, high = lax.rem(place, 2), place // 2
    across = place + 1 - 2 * low
    along = lax.rem(place + 2, 4)
    sib_dev = {"section": 1 - core}
    x_dev, y_dev = {"tensor": across}, {"tensor": along}
    diag_dev = {"section": 1 - core, "tensor": across}

    def dp_dev(step):
        return {"dp": z + step - 2 * step * lax.rem(z // step, 2)}

    dp_steps = []
    while (1 << len(dp_steps)) < dp:
        dp_steps.append(1 << len(dp_steps))
    z_dev = dp_dev(1)
    wires = Copies(send_sem, arrive_sem, here_sem)
    pending = []

    barrier = pltpu.get_barrier_semaphore()
    greeted = [sib_dev, x_dev, y_dev, diag_dev] + [dp_dev(s) for s in dp_steps]
    for device in greeted:
        pl.semaphore_signal(barrier, inc=1, device_id=device, device_id_type=MESH)
    pl.semaphore_wait(barrier, len(greeted))

    half = lax.rem(z, 2) * (UNITS // 2)
    other_half = UNITS // 2 - half

    class Heads:
        def __init__(self, layer):
            self.layer = layer
            items = [(qkv, qw, x_dev), (pre, pw, x_dev), (pack, pk, y_dev)]
            self.here = [wires.local(src, dst.at[layer, 0]) for src, dst, _ in items]
            self.over = [wires.remote(src, dst.at[layer, 1], dev)[0] for src, dst, dev in items]
            self.first = [wires.remote(src, dst.at[layer, 0], sib_dev)[0] for src, dst, _ in items]
            self.second = [wires.remote(dst.at[layer, 1], dst.at[layer, 1], sib_dev)[0] for _, dst, _ in items]

        def start(self):
            @pl.when(core == self.layer)
            def _():
                for c in self.over + self.here + self.first:
                    c.start()

        def forward(self):
            @pl.when(core == self.layer)
            def _():
                for arriving, onward in zip(self.over, self.second, strict=True):
                    arriving.wait_recv()
                    onward.start()

        def need(self):
            @pl.when(core == self.layer)
            def _():
                for c in self.here:
                    c.wait()

            @pl.when(core != self.layer)
            def _():
                for c in self.first + self.second:
                    c.wait_recv()

        def finish(self):
            @pl.when(core == self.layer)
            def _():
                for c in self.over + self.first + self.second:
                    c.wait_send()

    class Outs:
        def __init__(self, layer):
            self.layer = layer
            self.here = wires.local(out_w, ow.at[layer, 0])
            self.over = wires.remote(out_w, ow.at[layer, 1], x_dev)[0]
            self.beside = wires.remote(out_w, ow.at[layer, 2], y_dev)[0]
            self.third = wires.remote(ow.at[layer, 1], ow.at[layer, 3], y_dev)[0]
            self.first = wires.remote(out_w, ow.at[layer, 0], sib_dev)[0]
            self.rest = [wires.remote(ow.at[layer, i], ow.at[layer, i], sib_dev)[0] for i in (1, 2, 3)]

        def start(self):
            @pl.when(core == self.layer)
            def _():
                for c in (self.over, self.beside, self.here, self.first):
                    c.start()

        def forward(self):
            @pl.when(core == self.layer)
            def _():
                self.over.wait_recv()
                self.third.start()
                self.rest[0].start()

        def forward_last(self):
            @pl.when(core == self.layer)
            def _():
                self.beside.wait_recv()
                self.rest[1].start()
                self.third.wait_recv()
                self.rest[2].start()

        def need(self):
            @pl.when(core == self.layer)
            def _():
                self.here.wait()

            @pl.when(core != self.layer)
            def _():
                for c in [self.first] + self.rest:
                    c.wait_recv()

        def finish(self):
            @pl.when(core == self.layer)
            def _():
                for c in [self.over, self.beside, self.third, self.first] + self.rest:
                    c.wait_send()

    class Units:
        def __init__(self, layer):
            self.layer = layer
            mine, theirs = pl.ds(half, UNITS // 2), pl.ds(other_half, UNITS // 2)
            pairs = [(up_w, gup), (down_w, gdown)]
            self.here = [wires.local(src, dst.at[layer, 0]) for src, dst in pairs]
            self.first = [wires.remote(src, dst.at[layer, 0], sib_dev)[0] for src, dst in pairs]
            self.over = [wires.remote(src.at[mine], dst.at[layer, 1, mine], y_dev)[0] for src, dst in pairs]
            self.dp = [wires.remote(dst.at[layer, 1, mine], dst.at[layer, 1, mine], z_dev) for _, dst in pairs]
            self.dp_in = [
                wires.remote(dst.at[layer, 1, theirs], dst.at[layer, 1, theirs], z_dev, number)[0]
                for (_, dst), (_, number) in zip(pairs, self.dp, strict=True)
            ]
            self.dp = [c for c, _ in self.dp]
            self.rest = [wires.remote(dst.at[layer, 1, mine], dst.at[layer, 1, mine], sib_dev)[0] for _, dst in pairs]
            self.last = [wires.remote(dst.at[layer, 1, theirs], dst.at[layer, 1, theirs], sib_dev)[0] for _, dst in pairs]

        def start(self):
            @pl.when(core == self.layer)
            def _():
                for c in self.over + self.here + self.first:
                    c.start()

        def forward(self, index):
            @pl.when(core == self.layer)
            def _():
                self.over[index].wait_recv()
                self.dp[index].start()
                self.rest[index].start()

        def forward_last(self, index):
            @pl.when(core == self.layer)
            def _():
                self.dp_in[index].wait_recv()
                self.last[index].start()

        def need(self):
            @pl.when(core == self.layer)
            def _():
                for c in self.here:
                    c.wait()

            @pl.when(core != self.layer)
            def _():
                for c in self.first + self.rest + self.last:
                    c.wait_recv()

        def finish(self):
            @pl.when(core == self.layer)
            def _():
                for c in self.first + self.over + self.dp + self.rest + self.last:
                    c.wait_send()

    heads = [Heads(0), Heads(1)]
    outs = [Outs(0), Outs(1)]
    units = [Units(0), Units(1)]
    loads = {}

    def load_units(layer, when):
        copies = [wires.local(gup.at[layer], uw), wires.local(gdown.at[layer], dw)]
        for c in copies:
            c.start()
        loads[layer, when] = copies

    def wait_units(layer, when):
        for c in loads[layer, when]:
            c.wait()

    class Tokens:
        def __init__(self, source, dest):
            self.near = wires.local(source.at[low], dest)
            self.far = wires.remote(source.at[1 - low], dest, x_dev)[0]

        def start(self):
            @pl.when(core == 0)
            def _():
                self.near.start()

            @pl.when(core == 1)
            def _():
                self.far.start()

        def wait(self):
            @pl.when(core == 0)
            def _():
                self.near.wait()

            @pl.when(core == 1)
            def _():
                self.far.wait_recv()

        def finish(self):
            @pl.when(core == 1)
            def _():
                self.far.wait_send()

    tokens = Tokens(states, xb.at[0])
    ends = Tokens(cotangent, cot)

    tokens.start()
    heads[0].start()
    tokens.wait()

    def chunk_rows(step):
        return pl.ds(step * CHUNK, CHUNK)

    def send_chunk(src, dst, device):
        copy, _ = wires.remote(src, dst, device)
        copy.start()
        return copy

    gathers = {}

    def gather_x(layer, step):
        gathers[layer, step] = send_chunk(
            xb.at[layer, chunk_rows(step)], xg.at[chunk_rows(step)], y_dev
        )

    for step in range(STEPS):
        gather_x(0, step)
    units[0].start()
    outs[0].start()

    parity = low + core - 2 * low * core
    row = segments[pl.ds(low, 1), :]
    last = row[:, LEN - 1 :]

    def block_labels(block):
        ids = last - segments[pl.ds(low, 1), pl.ds(pl.multiple_of(block * ROWS, ROWS), ROWS)]
        numbers = lax.broadcasted_iota(jnp.int32, (LABELS, ROWS), 0)
        same = jnp.where(numbers == ids, 1.0, 0.0)
        return same.T, jnp.where(numbers <= 2 * SPAN, HIDDEN * (1.0 - same), 0.0).T

    for index, (h, p) in enumerate(((high, parity), (1 - high, parity), (high, 1 - parity), (1 - high, 1 - parity))):
        same, differ = block_labels(2 * h + p)
        if index < 2:
            lab_q[pl.ds(index * ROWS, ROWS), :] = same.astype(BF16)
        lab_k[pl.ds(index * ROWS, ROWS), :] = differ.astype(BF16)

    def project(layer, source, start, size):
        for slot in range(2):
            columns = slice(slot * QUARTER, (slot + 1) * QUARTER)
            rows = pl.ds(start, size)
            qs[layer, rows, columns] = dot(source, qw[layer, slot, 0]).astype(BF16)
            kv[layer, rows, columns] = dot(source, qw[layer, slot, 1]).astype(BF16)
            kv[layer, rows, slice(CORE + columns.start, CORE + columns.stop)] = dot(
                source, qw[layer, slot, 2]
            ).astype(BF16)

    def lanes(index, base=0):
        return pl.ds(pl.multiple_of(base + index * PAIR, PAIR), PAIR)

    def fill(layer, p):
        pre_lanes = pl.ds(pl.multiple_of(lax.rem(p, 2) * PAIR, PAIR), PAIR)
        keys[:CORE, :PAIR] = kv[layer, :, lanes(p)]
        keys[CORE : 2 * CORE, :PAIR] = kvs[layer, :, lanes(p)]
        keys[2 * CORE :, :PAIR] = pw[layer, p // 2, 0, :, pre_lanes]
        return kv[layer, :, lanes(p, CORE)], kvs[layer, :, lanes(p, CORE)], pw[layer, p // 2, 1, :, pre_lanes]

    keys[: 2 * CORE, PAIR:] = lab_k[...]
    keys[2 * CORE :, PAIR:] = jnp.zeros((PREFIX, LABELS), BF16)

    def attend_rows(layer, start):
        rows = pl.ds(start, ROWS)

        def body(p, _):
            vo, vs, vp = fill(layer, p)
            vals_t[:, :CORE] = vo.T
            vals_t[:, CORE : 2 * CORE] = vs.T
            vals_t[:, 2 * CORE :] = vp.T
            query = qs[layer, rows, lanes(p)] * 0.125
            label = lab_q[rows, :]
            results = []
            for head in range(2):
                mine = jnp.where(head_lanes(ROWS, head), query, 0)
                scores = dot_t(keys[...], jnp.concatenate([mine, label], 1))
                peak = jnp.max(scores, axis=0, keepdims=True)
                weights = jnp.exp(scores - peak)
                total = jnp.sum(weights, axis=0, keepdims=True)
                merged = dot(vals_t[head * HEAD : (head + 1) * HEAD, :], weights.astype(BF16))
                results.append(merged / total)
                lse[layer, p, head : head + 1, rows] = peak + jnp.log(total)
            mg[layer, rows, lanes(p)] = jnp.concatenate(results, 0).T.astype(BF16)
            return 0

        lax.fori_loop(0, PAIRS, body, 0)

    def attend_rows_back(layer, start, fresh):
        rows = pl.ds(start, ROWS)

        def body(p, _):
            vo, vs, vp = fill(layer, p)
            vals[:CORE, :] = vo
            vals[CORE : 2 * CORE, :] = vs
            vals[2 * CORE :, :] = vp
            vals_t[:, :CORE] = keys[:CORE, :PAIR].T
            vals_t[:, CORE : 2 * CORE] = keys[CORE : 2 * CORE, :PAIR].T
            vals_t[:, 2 * CORE :] = keys[2 * CORE :, :PAIR].T
            query = qs[layer, rows, lanes(p)] * 0.125
            label = lab_q[rows, :]
            grad_part = gm[rows, lanes(p)]
            product = (grad_part.astype(F32) * mg[layer, rows, lanes(p)].astype(F32)).T
            queries, grad_list, weights_all, scores_all, results = [], [], [], [], []
            for head in range(2):
                span = slice(head * HEAD, (head + 1) * HEAD)
                mine = jnp.where(head_lanes(ROWS, head), query, 0)
                mine_grad = jnp.where(head_lanes(ROWS, head), grad_part, 0)
                scores = dot_t(keys[...], jnp.concatenate([mine, label], 1))
                weights = jnp.exp(scores - lse[layer, p, head : head + 1, rows])
                delta = jnp.sum(product[span], axis=0, keepdims=True)
                grad_scores = (weights * (dot_t(vals[...], mine_grad) - delta)).astype(BF16)
                results.append(dot(vals_t[span, :], grad_scores))
                queries.append(mine)
                grad_list.append(mine_grad)
                weights_all.append(weights.astype(BF16))
                scores_all.append(grad_scores)
            dq[rows, lanes(p)] = (jnp.concatenate(results, 0).T * 0.125).astype(BF16)
            dv_part = dot(jnp.concatenate(weights_all, 1), jnp.concatenate(grad_list, 0))
            dk_part = dot(jnp.concatenate(scores_all, 1), jnp.concatenate(queries, 0))
            if fresh:
                dv_acc[:, lanes(p)] = dv_part
                dk_acc[:, lanes(p)] = dk_part
            else:
                dv_acc[:, lanes(p)] += dv_part
                dk_acc[:, lanes(p)] += dk_part
            return 0

        lax.fori_loop(0, PAIRS, body, 0)

    def vector(layer, index):
        return pk[layer, 0, index : index + 1, :]

    def keep_norm(store, scales, layer, rows, normed, scale):
        store[layer, rows, :] = normed.astype(BF16)
        scales[layer, rows, :] = jnp.broadcast_to(scale, (CHUNK, PAIR))

    def forward_attention(layer):
        if layer == 0:
            heads[0].forward()
        heads[layer].need()
        project(layer, xb[layer], 0, ROWS)
        sent = [send_chunk(kv.at[layer, :ROWS], kvs.at[layer, :ROWS], sib_dev)]
        for step in range(STEPS):
            gathers[layer, step].wait_recv()
            project(layer, xg[chunk_rows(step), :], ROWS + step * CHUNK, CHUNK)
        sent.append(send_chunk(kv.at[layer, ROWS:], kvs.at[layer, ROWS:], sib_dev))
        if layer == 0:
            heads[1].start()
            outs[0].forward()
            units[0].forward(0)
        for c in sent:
            c.wait_recv()
        attend_rows(layer, ROWS)
        swap = send_chunk(mg.at[layer, ROWS:], mrecv, y_dev)
        if layer == 0:
            outs[0].forward_last()
            units[0].forward(1)
            units[0].forward_last(0)
        else:
            units[1].forward(1)
            units[1].forward_last(0)
        attend_rows(layer, 0)
        if layer == 0:
            outs[1].start()
            ends.start()
            units[0].forward_last(1)
            units[0].need()
            load_units(0, 0)
        else:
            units[1].forward_last(1)
            units[1].need()
            load_units(1, 0)
        outs[layer].need()
        swap.wait_recv()
        copies = []
        for step in range(STEPS):
            rows = chunk_rows(step)
            parts = [mg[layer, rows, :QUARTER], mg[layer, rows, QUARTER:], mrecv[rows, :QUARTER], mrecv[rows, QUARTER:]]
            total = xb[layer, rows, :].astype(F32) + vector(layer, 3)
            for i, part in enumerate(parts):
                total = total + dot(part, ow[layer, i])
            normed, scale = norm_chunk(total)
            keep_norm(n1, r1, layer, rows, normed, scale)
            middle = normed * vector(layer, 1) + vector(layer, 4)
            mid[rows, :] = middle
            fsnd[rows, :] = middle.astype(BF16)
            copies.append(send_chunk(fsnd.at[rows], fin.at[rows], x_dev))
        for c in sent + [swap] + [gathers[layer, s] for s in range(STEPS)]:
            c.wait_send()
        return copies

    def feed_rows(layer, source, start, size):
        def up_tile(j, _):
            slot, columns = j // 4, pl.ds(pl.multiple_of(lax.rem(j, 4) * TILE, TILE), TILE)
            wide = pl.ds(pl.multiple_of(j * TILE, TILE), TILE)
            u = dot(source[...], uw[slot, :, columns]) + pk[layer, slot, 0:1, columns]
            act[:size, wide], slopes[layer, pl.ds(start, size), wide] = gelu_both(u)
            return 0

        lax.fori_loop(0, 2 * UNITS // TILE, up_tile, 0)

    def feed_rows_back(layer, source, start, size):
        def tile(j, _):
            slot, units_at = j // 4, pl.ds(pl.multiple_of(lax.rem(j, 4) * TILE, TILE), TILE)
            wide = pl.ds(pl.multiple_of(j * TILE, TILE), TILE)
            u = dot_t(source[...], dw[slot, units_at, :]) * slopes[layer, pl.ds(start, size), wide].astype(F32)
            act[:size, wide] = u.astype(BF16)
            return 0

        lax.fori_loop(0, 2 * UNITS // TILE, tile, 0)

    def feed_out(store, size, back):
        def tile(j, _):
            columns = pl.ds(pl.multiple_of(j * TILE, TILE), TILE)
            if back:
                u = dot_t(act[:size, :UNITS], uw[0, columns, :]) + dot_t(act[:size, UNITS:], uw[1, columns, :])
            else:
                u = dot(act[:size, :UNITS], dw[0, :, columns]) + dot(act[:size, UNITS:], dw[1, :, columns])
            store[:, columns] = u.astype(store.dtype)
            return 0

        lax.fori_loop(0, D // TILE, tile, 0)

    def feed(layer, copies, back, finish):
        rows_fn = feed_rows_back if back else feed_rows
        rows_fn(layer, fsnd, 0, ROWS)
        feed_out(acc, ROWS, back)
        returned = []
        for step in range(STEPS):
            rows = chunk_rows(step)
            copies[step].wait_recv()
            rows_fn(layer, fin.at[rows], ROWS + step * CHUNK, CHUNK)
            feed_out(fout.at[rows], CHUNK, back)
            returned.append(send_chunk(fout.at[rows], fret.at[rows], x_dev))
        for step in range(STEPS):
            returned[step].wait_recv()
            finish(step, chunk_rows(step), acc[chunk_rows(step), :] + fret[chunk_rows(step), :].astype(F32))
        for c in copies + returned:
            c.wait_send()

    deliveries = []

    def deliver(layer, source, dest, step):
        rows = chunk_rows(step)
        far, number = wires.remote(source.at[rows], dest.at[low, rows], {"section": layer, "tensor": across})
        far_in, _ = wires.remote(source.at[rows], dest.at[1 - low, rows], {"section": layer, "tensor": across}, number)
        if layer == 0:
            near = wires.local(source.at[rows], dest.at[low, rows])
        else:
            near, _ = wires.remote(source.at[rows], dest.at[low, rows], sib_dev)

        @pl.when(core == 0)
        def _():
            near.start()

        @pl.when(core == 1)
        def _():
            far.start()

        def sent():
            @pl.when(core == 0)
            def _():
                near.wait() if layer == 0 else near.wait_send()

            @pl.when(core == 1)
            def _():
                far.wait_send()

        def arrived():
            @pl.when(core == layer)
            def _():
                far_in.wait_recv()
                if layer == 1:
                    near.wait_recv()

        deliveries.append(arrived)
        return sent

    def start_back(layer, step, rows, grad):
        normed, scale = n2[layer, rows, :].astype(F32), r2[layer, rows, :1]
        value = norm_back(grad, vector(layer, 2), normed, scale)
        gsec[rows, :] = value
        fsnd[rows, :] = value.astype(BF16)
        return send_chunk(fsnd.at[rows], fin.at[rows], x_dev)

    unsent = []
    back_copies = []

    def forward_finish(layer):
        def finish(step, rows, branch):
            normed, scale = norm_chunk(mid[rows, :] + branch + vector(layer, 5))
            keep_norm(n2, r2, layer, rows, normed, scale)
            xb[layer + 1, rows, :] = (normed * vector(layer, 2) + vector(layer, 6)).astype(BF16)
            if layer == 0:
                gather_x(1, step)
            unsent.append(deliver(layer, xb.at[layer + 1], hidden, step))

        return finish

    copies = forward_attention(0)
    wait_units(0, 0)
    heads[1].forward()
    units[1].start()
    outs[1].forward()
    feed(0, copies, False, forward_finish(0))
    outs[1].forward_last()
    units[1].forward(0)
    copies = forward_attention(1)
    wait_units(1, 0)
    feed(1, copies, False, forward_finish(1))

    ends.wait()
    for step in range(STEPS):
        back_copies.append(start_back(1, step, chunk_rows(step), cot[chunk_rows(step), :].astype(F32)))

    grad_sent = []

    def backward(layer, copies):
        swaps = []

        def finish(step, rows, term):
            middle = gsec[rows, :] + term
            first = norm_back(middle, vector(layer, 1), n1[layer, rows, :].astype(F32), r1[layer, rows, :1])
            gfirst[rows, :] = first
            low_first = first.astype(BF16)
            for i in range(4):
                part = dot_t(low_first, ow[layer, i]).astype(BF16)
                columns = slice((i % 2) * QUARTER, (i % 2 + 1) * QUARTER)
                if i < 2:
                    gm[rows, columns] = part
                else:
                    gms[rows, columns] = part
            swaps.append(send_chunk(gms.at[rows], gm.at[pl.ds(ROWS + step * CHUNK, CHUNK)], y_dev))

        feed(layer, copies, True, finish)
        if layer == 1:
            load_units(0, 1)
        attend_rows_back(layer, 0, True)
        for c in swaps:
            c.wait_recv()
        attend_rows_back(layer, ROWS, False)
        dkv_send[:, :CORE] = dk_acc[CORE : 2 * CORE, :].astype(BF16)
        dkv_send[:, CORE:] = dv_acc[CORE : 2 * CORE, :].astype(BF16)
        given = send_chunk(dkv_send, dkv_recv.at[layer], sib_dev)
        pacc[layer, 0] = dk_acc[2 * CORE :, :]
        pacc[layer, 1] = dv_acc[2 * CORE :, :]
        if layer == 0:
            total = prefix_start()
        given.wait_recv()
        dkv[:, :CORE] = (dk_acc[:CORE, :] + dkv_recv[layer, :, :CORE].astype(F32)).astype(BF16)
        dkv[:, CORE:] = (dv_acc[:CORE, :] + dkv_recv[layer, :, CORE:].astype(F32)).astype(BF16)

        def input_term(store, start, size):
            rows = pl.ds(start, size)

            def tile(j, _):
                features = pl.ds(pl.multiple_of(j * TILE, TILE), TILE)
                total = None
                for slot in range(2):
                    columns = slice(slot * QUARTER, (slot + 1) * QUARTER)
                    shifted = slice(CORE + slot * QUARTER, CORE + (slot + 1) * QUARTER)
                    for part, source in enumerate((dq[rows, columns], dkv[rows, columns], dkv[rows, shifted])):
                        term = dot_t(source, qw[layer, slot, part, features, :])
                        total = term if total is None else total + term
                store[:, features] = total.astype(store.dtype)
                return 0

            lax.fori_loop(0, D // TILE, tile, 0)

        returned = []
        for step in range(STEPS):
            input_term(dxs.at[chunk_rows(step)], ROWS + step * CHUNK, CHUNK)
            returned.append(send_chunk(dxs.at[chunk_rows(step)], dxr.at[chunk_rows(step)], y_dev))
        if layer == 0:
            total.stage()
        input_term(acc, 0, ROWS)
        if layer == 1:
            wait_units(0, 1)
        else:
            total.stage()
        for sent in grad_sent:
            sent()
        grad_sent.clear()
        onward = []
        for step in range(STEPS):
            rows = chunk_rows(step)
            returned[step].wait_recv()
            value = gfirst[rows, :] + (acc[rows, :] + dxr[rows, :].astype(F32))
            gout[rows, :] = value
            grad_sent.append(deliver(layer, gout, grads, step))
            if layer == 1:
                onward.append(start_back(0, step, rows, value.astype(BF16).astype(F32)))
            else:
                total.stage()
        for c in swaps + [given] + returned:
            c.wait_send()
        return onward

    class prefix_start:
        def __init__(self):
            self.sib = send_chunk(pacc.at[1 - core], psib, sib_dev)
            self.sent = [self.sib]
            self.at = 0

        def stage(self):
            if self.at == 0:
                self.sib.wait_recv()
                total = pacc[core] + psib[...]
                psum[0] = total[:, :, :QUARTER]
                pacross[0] = total[:, :, QUARTER:]
                self.next = send_chunk(pacross.at[0], pacross.at[1], x_dev)
                self.sent.append(self.next)
            elif self.at <= len(dp_steps) + 1:
                self.next.wait_recv()
                arrived = pacross[1] if self.at == 1 else pdp[self.at - 2]
                psum[self.at] = psum[self.at - 1] + arrived
                if self.at <= len(dp_steps):
                    step = self.at - 1
                    self.next = send_chunk(psum.at[self.at], pdp.at[step], dp_dev(dp_steps[step]))
                    self.sent.append(self.next)
                else:
                    self.done = wires.local(psum.at[self.at], pgrads)
                    self.done.start()
            self.at += 1

        def finish(self):
            while self.at <= len(dp_steps) + 1:
                self.stage()
            for c in self.sent:
                c.wait_send()
            self.done.wait()

    holder = []
    start_class = prefix_start

    def prefix_start():
        holder.append(start_class())
        return holder[0]

    back_copies = backward(1, back_copies)
    backward(0, back_copies)
    holder[0].finish()
    for sent in unsent + grad_sent:
        sent()
    for arrived in deliveries:
        arrived()
    tokens.finish()
    ends.finish()
    for layer in range(2):
        heads[layer].finish()
        outs[layer].finish()
        units[layer].finish()


def fused(dp, states, cotangent, segments, qkv, out_w, up_w, down_w, pre, pack):
    shape = jax.ShapeDtypeStruct
    steps = dp.bit_length() - 1
    vmem = pltpu.VMEM
    scratch = [
        vmem((3, ROWS, D), BF16),
        vmem((ROWS, D), BF16),
        vmem((ROWS, D), BF16),
        vmem((CORE, LABELS), BF16), vmem((2 * CORE, LABELS), BF16),
        vmem((2, 2, 3, D, QUARTER), BF16),
        vmem((2, 4, QUARTER, D), BF16),
        vmem((2, D, UNITS), BF16), vmem((2, UNITS, D), BF16),
        vmem((2, 2, 2, PREFIX, QUARTER), BF16),
        vmem((2, 2, 8, D), F32),
        vmem((2, CORE, CORE), BF16), vmem((2, CORE, 2 * CORE), BF16), vmem((2, CORE, 2 * CORE), BF16),
        vmem((2, CORE, CORE), BF16), vmem((2, PAIRS, 8, CORE), F32),
        vmem((2, ROWS, D), BF16), vmem((2, ROWS, PAIR), F32),
        vmem((2, ROWS, D), BF16), vmem((2, ROWS, PAIR), F32),
        vmem((2, CORE, 2 * UNITS), BF16),
        vmem((ROWS, D), F32), vmem((ROWS, D), F32), vmem((ROWS, 2 * UNITS), BF16),
        vmem((ROWS, CORE), BF16),
        vmem((ROWS, D), BF16), vmem((ROWS, D), BF16), vmem((ROWS, D), BF16), vmem((ROWS, D), BF16),
        vmem((ROWS, D), F32), vmem((ROWS, D), F32),
        vmem((CORE, CORE), BF16), vmem((ROWS, CORE), BF16), vmem((ROWS, D), F32),
        vmem((KEYS, PAIR + LABELS), BF16), vmem((PAIR, KEYS), BF16), vmem((KEYS, PAIR), BF16),
        vmem((KEYS, CORE), F32), vmem((KEYS, CORE), F32),
        vmem((CORE, CORE), BF16), vmem((CORE, 2 * CORE), BF16), vmem((CORE, 2 * CORE), BF16),
        vmem((2, CORE, 2 * CORE), BF16),
        vmem((ROWS, D), BF16), vmem((ROWS, D), BF16),
        vmem((2, 2, PREFIX, CORE), F32), vmem((2, PREFIX, CORE), F32),
        vmem((2, 2, PREFIX, QUARTER), F32), vmem((steps + 2, 2, PREFIX, QUARTER), F32),
        vmem((max(steps, 1), 2, PREFIX, QUARTER), F32),
        pltpu.SemaphoreType.DMA((SEMS,)), pltpu.SemaphoreType.DMA((SEMS,)), pltpu.SemaphoreType.DMA((SEMS,)),
    ]
    anywhere = pl.BlockSpec(memory_space=pl.ANY)
    result = pl.pallas_call(
        functools.partial(fused_kernel, dp),
        out_shape=[
            shape((2, ROWS, D), BF16), shape((2, ROWS, D), F32), shape((2, PREFIX, QUARTER), F32),
            shape((2, 2, D, UNITS), BF16), shape((2, 2, UNITS, D), BF16),
        ],
        in_specs=[anywhere, anywhere, pl.BlockSpec(memory_space=pltpu.VMEM)] + [anywhere] * 6,
        out_specs=[anywhere] * 5,
        scratch_shapes=scratch,
        compiler_params=pltpu.CompilerParams(
            collective_id=0, has_side_effects=True, vmem_limit_bytes=63 << 20
        ),
        name="layers",
    )(states, cotangent, segments, qkv, out_w, up_w, down_w, pre, pack)
    return result[:3]


class Links:
    def __init__(self):
        self.core = lax.axis_index("section")
        self.place = lax.axis_index("tensor")
        self.size = lax.axis_size("tensor")
        self.low = self.place % 2
        self.high = self.place // 2
        self.group = self.size // 2

    def sibling(self, a, only=None):
        pairs = [(0, 1), (1, 0)] if only is None else [(only, 1 - only)]
        return lax.ppermute(a, "section", pairs)

    def across(self, a, only=None):
        if only is None:
            return lax.ppermute(a, "tensor", [(t, t ^ 1) for t in range(self.size)])
        pairs = [(only * self.size + t, only * self.size + (t ^ 1)) for t in range(self.size)]
        return lax.ppermute(a, ("section", "tensor"), pairs)

    def diagonal(self, a, source):
        pairs = [(source * self.size + t, (1 - source) * self.size + (t ^ 1)) for t in range(self.size)]
        return lax.ppermute(a, ("section", "tensor"), pairs)

    def from_ahead(self, a, by):
        g = self.group
        pairs = [(2 * ((h + by) % g) + p, 2 * h + p) for h in range(g) for p in range(2)]
        return lax.ppermute(a, "tensor", pairs)

    def gather(self, a):
        return [a] + [self.from_ahead(a, k) for k in range(1, self.group)]

    def scatter_sum(self, part_fn):
        arrived = [self.from_ahead(part_fn(k).astype(BF16), self.group - k) for k in range(1, self.group)]
        total = part_fn(0)
        for a in arrived:
            total = total + a.astype(F32)
        return total


def forward(links, x, weights, pre, labels):
    qkv_w, out_w, up_w, up_b, down_w, gains, shifts = weights
    width = out_w.shape[0]
    blocks = [dot(b, qkv_w).astype(BF16) for b in links.gather(x)]
    qkv = jnp.concatenate(blocks, 0)
    kv_sib = links.sibling(qkv[:, width:])
    merged, lse = attend(qkv, kv_sib, pre, labels)
    rows = x.shape[0]
    attended = links.scatter_sum(lambda k: dot(merged[k * rows : (k + 1) * rows], out_w)) + shifts[0]
    normed_first, scale_first = norm_stats(x.astype(F32) + attended)
    middle = normed_first * gains[0] + shifts[1]
    blocks = links.gather(middle.astype(BF16))
    pairs = [gelu_pair(dot(b, up_w) + up_b) for b in blocks]
    branch = links.scatter_sum(lambda k: dot(pairs[k][0], down_w)) + shifts[2]
    normed_last, scale_last = norm_stats(middle + branch)
    result = (normed_last * gains[1] + shifts[3]).astype(BF16)
    slopes = [p[1] for p in pairs]
    return result, (qkv, kv_sib, merged, lse, normed_first, scale_first, slopes, normed_last, scale_last)


def backward(links, grad, weights, pre, labels, kept):
    qkv_w, out_w, up_w, up_b, down_w, gains, shifts = weights
    qkv, kv_sib, merged, lse, normed_first, scale_first, slopes, normed_last, scale_last = kept
    rows = grad.shape[0]
    grad_second = norm_back(grad.astype(F32), gains[1], normed_last, scale_last)
    blocks = links.gather(grad_second.astype(BF16))
    hiddens = [
        (dot_t(b, down_w) * s.astype(F32)).astype(BF16) for b, s in zip(blocks, slopes, strict=True)
    ]
    grad_middle = grad_second + links.scatter_sum(lambda k: dot_t(hiddens[k], up_w))
    grad_first = norm_back(grad_middle, gains[0], normed_first, scale_first)
    blocks = links.gather(grad_first.astype(BF16))
    grad_merged = jnp.concatenate([dot_t(b, out_w).astype(BF16) for b in blocks], 0)
    dq, dko, dvo, dks, dvs, dkp, dvp = attend_back(qkv, kv_sib, pre, labels, merged, lse, grad_merged)
    arrived = links.sibling(jnp.concatenate([dks, dvs], 1)).astype(F32)
    width = out_w.shape[0]
    dk = (dko + arrived[:, :width]).astype(BF16)
    dv = (dvo + arrived[:, width:]).astype(BF16)
    dqkv = jnp.concatenate([dq, dk, dv], 1)
    grad_inputs = grad_first + links.scatter_sum(
        lambda k: dot_t(dqkv[k * rows : (k + 1) * rows], qkv_w)
    )
    return grad_inputs, jnp.stack([dkp, dvp])


def spread_weights(links, arrays):
    first = links.core == 0
    layers = ([], [])
    for layer in range(2):
        for a in arrays:
            other = links.across(a, layer)
            sib_a, sib_other = links.sibling(a, layer), links.sibling(other, layer)
            here = links.core == layer
            layers[layer].append((jnp.where(here, a, sib_a), jnp.where(here, other, sib_other)))
    return layers


def sum_over_dp(a):
    size = lax.axis_size("dp")
    step = 1
    if size & (size - 1):
        return lax.psum(a, "dp")
    while step < size:
        a = a + lax.ppermute(a, "dp", [(i, i ^ step) for i in range(size)])
        step *= 2
    return a


def plain(
    states, segment_ids, cotangent, qkv_weight, out_weight, up_weight, up_bias, down_weight,
    norm_gain, shift_vec, prefix,
):
    links = Links()
    first = links.core == 0
    low = links.low

    def arrange(both):
        mine = lax.dynamic_index_in_dim(both, low, 0, keepdims=False)
        other = lax.dynamic_index_in_dim(both, 1 - low, 0, keepdims=False)
        return jnp.where(first, mine, links.across(other, 1))

    x = arrange(states)
    grad = arrange(cotangent)

    segment = lax.dynamic_index_in_dim(segment_ids, low, 0, keepdims=False)
    classes = (segment[-1] - segment).reshape(links.group, 2, -1)
    classes = jnp.roll(classes, -links.high, 0)
    parity = jnp.where(first, low, 1 - low)
    own = lax.dynamic_index_in_dim(classes, parity, 1, keepdims=False).reshape(-1)
    sib = lax.dynamic_index_in_dim(classes, 1 - parity, 1, keepdims=False).reshape(-1)
    numbers = jnp.arange(LABELS)[None, :]
    label_q = (own[:, None] == numbers).astype(BF16)
    known = numbers <= 2 * SPAN
    label_o = jnp.where(known & (own[:, None] != numbers), HIDDEN, 0.0).astype(BF16)
    label_s = jnp.where(known & (sib[:, None] != numbers), HIDDEN, 0.0).astype(BF16)
    labels = (label_q, label_o, label_s)

    small = jnp.concatenate(
        [norm_gain[0], shift_vec[0]], 0
    )
    small_sib = links.sibling(small)
    layers = spread_weights(
        links,
        [jnp.transpose(qkv_weight[0], (1, 0, 2)), prefix[0], out_weight[0], up_weight[0], up_bias, down_weight[0]],
    )
    weights, prefixes = [], []
    for layer in range(2):
        qkv, pre, out, up, bias, down = layers[layer]
        vectors = jnp.where(links.core == layer, small, small_sib).astype(F32)
        weights.append((
            jnp.concatenate([p[i] for i in range(3) for p in qkv], 1),
            jnp.concatenate(out, 0),
            jnp.concatenate(up, 1),
            jnp.concatenate(bias, 1).astype(F32),
            jnp.concatenate(down, 0),
            vectors[:2],
            vectors[2:],
        ))
        prefixes.append(jnp.concatenate(pre, 2))

    y0, kept0 = forward(links, x, weights[0], prefixes[0], labels)
    y1, kept1 = forward(links, y0, weights[1], prefixes[1], labels)
    g1, p1 = backward(links, grad, weights[1], prefixes[1], labels, kept1)
    g0, p0 = backward(links, g1.astype(BF16), weights[0], prefixes[0], labels, kept0)

    def deliver(first_layer, second_layer, wire, dtype):
        near = jnp.where(first, first_layer.astype(dtype), links.sibling(second_layer.astype(wire), 0).astype(dtype))
        far0 = links.diagonal(first_layer.astype(wire), 1)
        far1 = links.across(second_layer.astype(wire), 1)
        far = jnp.where(first, far0, far1).astype(dtype)
        return jnp.stack([jnp.where(low == 0, near, far), jnp.where(low == 0, far, near)])

    hidden_out = deliver(y0, y1, BF16, BF16)
    input_grads = deliver(g0, g1, BF16, F32)

    total = jnp.where(first, p0, p1) + links.sibling(jnp.where(first, p1, p0))
    quarter = total.shape[-1] // 2
    total = total[..., :quarter] + links.across(total[..., quarter:])
    prefix_grads = sum_over_dp(total)
    return hidden_out[None], input_grads[None], prefix_grads[None]


def whole_kernel(
    states, segment_ids, cotangent, qkv_weight, out_weight, up_weight, up_bias, down_weight,
    norm_gain, shift_vec, prefix,
):
    pack = jnp.concatenate([up_bias, norm_gain[0], shift_vec[0], jnp.zeros_like(up_bias)], 0).astype(F32)
    results = fused(
        lax.axis_size("dp"), states, cotangent, segment_ids, jnp.transpose(qkv_weight[0], (1, 0, 2)),
        out_weight[0], up_weight[0], down_weight[0], prefix[0], pack,
    )
    return tuple(r[None] for r in results)


def fits(mesh):
    dp = mesh.shape["dp"]
    return mesh.shape["tensor"] == 4 and dp > 1 and dp & (dp - 1) == 0


def solution(mesh):
    placed = (
        P(None, ("dp", "tensor"), None),
        P(None, "dp"),
        P(None, ("dp", "tensor"), None),
        P("section", None, None, "tensor"),
        P("section", "tensor", None),
        P("section", None, "tensor"),
        P("section", "tensor"),
        P("section", "tensor", None),
        P("section", None, None),
        P("section", None, None),
        P("section", None, None, "tensor"),
    )
    return jax.shard_map(
        whole_kernel if fits(mesh) else plain,
        mesh=mesh,
        in_specs=placed,
        out_specs=(
            P("section", None, ("dp", "tensor"), None),
            P("section", None, ("dp", "tensor"), None),
            P("section", None, None, "tensor"),
        ),
        check_vma=False,
    )
```

```python
import functools

import jax
import jax.numpy as jnp
from jax import lax
from jax.experimental import pallas as pl
from jax.experimental.pallas import tpu as pltpu
from jax.sharding import PartitionSpec as P

D = 1024
HEAD = 64
PAIR = 2 * HEAD
PREFIX = 64
LEN = 1024
SPAN = LEN // 32
LABELS = 128
HIDDEN = -1e30
F32 = jnp.float32
BF16 = jnp.bfloat16


def dot(a, b):
    return jnp.dot(a, b, preferred_element_type=F32)


def dot_t(a, b):
    return lax.dot_general(a, b, (((1,), (1,)), ((), ())), preferred_element_type=F32)


def head_lanes(rows, head):
    lanes = lax.broadcasted_iota(jnp.int32, (rows, PAIR), 1)
    return (lanes >= head * HEAD) & (lanes < (head + 1) * HEAD)


def fill_keys(keys, own, sib, pre, own_lab, sib_lab):
    rows = own.shape[0]
    keys[:rows, :PAIR] = own[...]
    keys[rows : 2 * rows, :PAIR] = sib[...]
    keys[2 * rows :, :PAIR] = pre[...]
    keys[:rows, PAIR:] = own_lab[...]
    keys[rows : 2 * rows, PAIR:] = sib_lab[...]
    keys[2 * rows :, PAIR:] = jnp.zeros((PREFIX, LABELS), BF16)


def attend_kernel(block, q, ko, vo, ks, vs, kp, vp, lab_q, lab_o, lab_s, out, lse, keys, vals_t):
    rows = q.shape[0]
    fill_keys(keys, ko, ks, kp, lab_o, lab_s)
    vals_t[:, :rows] = vo[...].T
    vals_t[:, rows : 2 * rows] = vs[...].T
    vals_t[:, 2 * rows :] = vp[...].T
    for start in range(0, rows, block):
        part = pl.ds(start, block)
        query = q[part, :] * 0.125
        label = lab_q[part, :]
        results = []
        for head in range(2):
            mine = jnp.where(head_lanes(block, head), query, 0)
            scores = dot_t(keys[...], jnp.concatenate([mine, label], 1))
            peak = jnp.max(scores, axis=0, keepdims=True)
            weights = jnp.exp(scores - peak)
            total = jnp.sum(weights, axis=0, keepdims=True)
            merged = dot(vals_t[head * HEAD : (head + 1) * HEAD, :], weights.astype(BF16))
            results.append(merged / total)
            lse[0, head : head + 1, part] = peak + jnp.log(total)
        out[part, :] = jnp.concatenate(results, 0).T.astype(BF16)


def attend_back_kernel(
    block, q, ko, vo, ks, vs, kp, vp, lab_q, lab_o, lab_s, out, lse, grad,
    dq, dko, dvo, dks, dvs, dkp, dvp, keys, vals, keys_t, dk_sum, dv_sum,
):
    rows = q.shape[0]
    fill_keys(keys, ko, ks, kp, lab_o, lab_s)
    vals[:rows, :] = vo[...]
    vals[rows : 2 * rows, :] = vs[...]
    vals[2 * rows :, :] = vp[...]
    keys_t[:, :rows] = ko[...].T
    keys_t[:, rows : 2 * rows] = ks[...].T
    keys_t[:, 2 * rows :] = kp[...].T
    for start in range(0, rows, block):
        part = pl.ds(start, block)
        query = q[part, :] * 0.125
        label = lab_q[part, :]
        grad_part = grad[part, :]
        product = (grad_part.astype(F32) * out[part, :].astype(F32)).T
        queries, grads, weights_all, scores_all, results = [], [], [], [], []
        for head in range(2):
            span = slice(head * HEAD, (head + 1) * HEAD)
            mine = jnp.where(head_lanes(block, head), query, 0)
            mine_grad = jnp.where(head_lanes(block, head), grad_part, 0)
            scores = dot_t(keys[...], jnp.concatenate([mine, label], 1))
            weights = jnp.exp(scores - lse[0, head : head + 1, part])
            delta = jnp.sum(product[span], axis=0, keepdims=True)
            grad_scores = (weights * (dot_t(vals[...], mine_grad) - delta)).astype(BF16)
            results.append(dot(keys_t[span, :], grad_scores))
            queries.append(mine)
            grads.append(mine_grad)
            weights_all.append(weights.astype(BF16))
            scores_all.append(grad_scores)
        dq[part, :] = (jnp.concatenate(results, 0).T * 0.125).astype(BF16)
        dv_part = dot(jnp.concatenate(weights_all, 1), jnp.concatenate(grads, 0))
        dk_part = dot(jnp.concatenate(scores_all, 1), jnp.concatenate(queries, 0))
        if start == 0:
            dv_sum[...] = dv_part
            dk_sum[...] = dk_part
        else:
            dv_sum[...] += dv_part
            dk_sum[...] += dk_part
    dko[...] = dk_sum[:rows, :]
    dvo[...] = dv_sum[:rows, :]
    dks[...] = dk_sum[rows : 2 * rows, :].astype(BF16)
    dvs[...] = dv_sum[rows : 2 * rows, :].astype(BF16)
    dkp[...] = dk_sum[2 * rows :, :]
    dvp[...] = dv_sum[2 * rows :, :]


def attention_specs(rows, pairs):
    def column(height, offset):
        return pl.BlockSpec((height, PAIR), lambda p: (0, offset + p))

    labels = pl.BlockSpec((rows, LABELS), lambda p: (0, 0))
    ins = [
        column(rows, 0), column(rows, pairs), column(rows, 2 * pairs),
        column(rows, 0), column(rows, pairs),
        column(PREFIX, 0), column(PREFIX, 0),
        labels, labels, labels,
    ]
    return column, ins, pl.BlockSpec((1, 8, rows), lambda p: (p, 0, 0))


def attend(qkv, kv_sib, pre, labels):
    rows, width = qkv.shape[0], qkv.shape[1] // 3
    pairs = width // PAIR
    column, ins, lse_spec = attention_specs(rows, pairs)
    size = 2 * rows + PREFIX
    return pl.pallas_call(
        functools.partial(attend_kernel, min(rows, 256)),
        grid=(pairs,),
        in_specs=ins,
        out_specs=[column(rows, 0), lse_spec],
        out_shape=[
            jax.ShapeDtypeStruct((rows, width), BF16),
            jax.ShapeDtypeStruct((pairs, 8, rows), F32),
        ],
        scratch_shapes=[pltpu.VMEM((size, PAIR + LABELS), BF16), pltpu.VMEM((PAIR, size), BF16)],
        compiler_params=pltpu.CompilerParams(vmem_limit_bytes=40 << 20),
        cost_estimate=pl.CostEstimate(
            flops=2 * 2 * rows * size * width, transcendentals=rows * size * width // HEAD,
            bytes_accessed=16 * rows * width,
        ),
        name="attend",
    )(qkv, qkv, qkv, kv_sib, kv_sib, pre[0], pre[1], *labels)


def attend_back(qkv, kv_sib, pre, labels, merged, lse, grad):
    rows, width = qkv.shape[0], qkv.shape[1] // 3
    pairs = width // PAIR
    column, ins, lse_spec = attention_specs(rows, pairs)
    size = 2 * rows + PREFIX
    shape = jax.ShapeDtypeStruct
    return pl.pallas_call(
        functools.partial(attend_back_kernel, min(rows, 256)),
        grid=(pairs,),
        in_specs=ins + [column(rows, 0), lse_spec, column(rows, 0)],
        out_specs=[column(rows, 0)] * 5 + [column(PREFIX, 0)] * 2,
        out_shape=[
            shape((rows, width), BF16),
            shape((rows, width), F32), shape((rows, width), F32),
            shape((rows, width), BF16), shape((rows, width), BF16),
            shape((PREFIX, width), F32), shape((PREFIX, width), F32),
        ],
        scratch_shapes=[
            pltpu.VMEM((size, PAIR + LABELS), BF16), pltpu.VMEM((size, PAIR), BF16),
            pltpu.VMEM((PAIR, size), BF16), pltpu.VMEM((size, PAIR), F32), pltpu.VMEM((size, PAIR), F32),
        ],
        compiler_params=pltpu.CompilerParams(vmem_limit_bytes=40 << 20),
        cost_estimate=pl.CostEstimate(
            flops=5 * 2 * rows * size * width, transcendentals=rows * size * width // HEAD,
            bytes_accessed=32 * rows * width,
        ),
        name="attend_back",
    )(qkv, qkv, qkv, kv_sib, kv_sib, pre[0], pre[1], *labels, merged, lse, grad)


def norm_stats(values):
    center = values - jnp.mean(values, axis=-1, keepdims=True)
    scale = lax.rsqrt(jnp.mean(center * center, axis=-1, keepdims=True) + 1e-05)
    return center * scale, scale


def norm_back(grad, gain, normed, scale):
    dn = grad * gain
    return scale * (
        dn
        - jnp.mean(dn, axis=-1, keepdims=True)
        - normed * jnp.mean(dn * normed, axis=-1, keepdims=True)
    )


def gelu_pair(u):
    cdf = 0.5 * (1.0 + lax.erf(u * 0.7071067811865476))
    pdf = jnp.exp(-0.5 * u * u) * 0.3989422804014327
    return (u * cdf).astype(BF16), (cdf + u * pdf).astype(BF16)


MESH = pl.DeviceIdType.MESH
ROWS = 256
CORE = 2 * ROWS
CHUNK = 128
STEPS = ROWS // CHUNK
QUARTER = D // 4
UNITS = D
TILE = 256
PAIRS = 4
KEYS = 2 * CORE + PREFIX
SEMS = 192


def gelu_both(u):
    size = jnp.abs(u) * 0.7071067811865476
    t = 1.0 / (1.0 + 0.3275911 * size)
    poly = t * (0.254829592 + t * (-0.284496736 + t * (1.421413741 + t * (-1.453152027 + t * 1.061405429))))
    bell = jnp.exp(-(size * size))
    tail = 0.5 * poly * bell
    cdf = jnp.where(u >= 0, 1.0 - tail, tail)
    return (u * cdf).astype(BF16), (cdf + u * (bell * 0.3989422804014327)).astype(BF16)


def norm_chunk(values):
    center = values - jnp.mean(values, axis=-1, keepdims=True)
    scale = lax.rsqrt(jnp.mean(center * center, axis=-1, keepdims=True) + 1e-05)
    return center * scale, scale


class Copies:
    def __init__(self, send, arrive, here):
        self.send, self.arrive, self.here = send, arrive, here
        self.remotes = self.locals = 0

    def remote(self, src, dst, device, number=None):
        if number is None:
            number = self.remotes
            self.remotes += 1
        copy = pltpu.make_async_remote_copy(
            src_ref=src, dst_ref=dst, send_sem=self.send.at[number], recv_sem=self.arrive.at[number],
            device_id=device, device_id_type=MESH,
        )
        return copy, number

    def local(self, src, dst, number=None):
        if number is None:
            number = self.locals
            self.locals += 1
        return pltpu.make_async_copy(src, dst, self.here.at[number])


def fused_kernel(
    dp,
    states, cotangent, segments, qkv, out_w, up_w, down_w, pre, pack,
    hidden, grads, pgrads, gup, gdown,
    xb, xg, cot, lab_q, lab_k, qw, ow, uw, dw, pw, pk,
    qs, kv, kvs, mg, lse, n1, r1, n2, r2, slopes,
    mid, acc, act, mrecv, fsnd, fin, fout, fret, gsec, gfirst, gm, gms, gout,
    keys, vals_t, vals, dk_acc, dv_acc, dq, dkv, dkv_send, dkv_recv, dxs, dxr, pacc, psib, pacross, psum, pdp,
    send_sem, arrive_sem, here_sem,
):
    core, z, place = lax.axis_index("section"), lax.axis_index("dp"), lax.axis_index("tensor")
    low, high = lax.rem(place, 2), place // 2
    across = place + 1 - 2 * low
    along = lax.rem(place + 2, 4)
    sib_dev = {"section": 1 - core}
    x_dev, y_dev = {"tensor": across}, {"tensor": along}
    diag_dev = {"section": 1 - core, "tensor": across}

    def dp_dev(step):
        return {"dp": z + step - 2 * step * lax.rem(z // step, 2)}

    dp_steps = []
    while (1 << len(dp_steps)) < dp:
        dp_steps.append(1 << len(dp_steps))
    z_dev = dp_dev(1)
    wires = Copies(send_sem, arrive_sem, here_sem)
    pending = []

    barrier = pltpu.get_barrier_semaphore()
    greeted = [sib_dev, x_dev, y_dev, diag_dev] + [dp_dev(s) for s in dp_steps]
    for device in greeted:
        pl.semaphore_signal(barrier, inc=1, device_id=device, device_id_type=MESH)
    pl.semaphore_wait(barrier, len(greeted))

    class Own:
        def __init__(self, layer, src, dst):
            self.layer = layer
            self.here = wires.local(src, dst)
            self.first = wires.remote(src, dst, sib_dev)[0]

        def start(self):
            @pl.when(core == self.layer)
            def _():
                self.here.start()
                self.first.start()

        def need(self):
            @pl.when(core == self.layer)
            def _():
                self.here.wait()

            @pl.when(core != self.layer)
            def _():
                self.first.wait_recv()

        def finish(self):
            @pl.when(core == self.layer)
            def _():
                self.first.wait_send()

    class Away:
        def __init__(self, layer, src, dst):
            self.layer = layer
            self.first = wires.remote(src, dst, sib_dev)[0]

        def start(self):
            @pl.when(core == self.layer)
            def _():
                self.first.start()

        def need(self):
            @pl.when(core != self.layer)
            def _():
                self.first.wait_recv()

        def finish(self):
            @pl.when(core == self.layer)
            def _():
                self.first.wait_send()

    class Direct:
        def __init__(self, layer, src, dst, dev):
            self.layer = layer
            self.over = wires.remote(src, dst, dev)[0]
            self.rest = wires.remote(dst, dst, sib_dev)[0]

        def start(self):
            @pl.when(core == self.layer)
            def _():
                self.over.start()

        def forward(self):
            @pl.when(core == self.layer)
            def _():
                self.over.wait_recv()
                self.rest.start()

        def need(self):
            @pl.when(core != self.layer)
            def _():
                self.rest.wait_recv()

        def finish(self):
            @pl.when(core == self.layer)
            def _():
                self.over.wait_send()
                self.rest.wait_send()

    class Shared:
        def __init__(self, layer, src, dst, mine, theirs, dev):
            self.layer = layer
            self.over = wires.remote(src.at[mine], dst.at[mine], dev)[0]
            self.dp, number = wires.remote(dst.at[mine], dst.at[mine], z_dev)
            self.dp_in = wires.remote(dst.at[theirs], dst.at[theirs], z_dev, number)[0]
            self.rest = wires.remote(dst.at[mine], dst.at[mine], sib_dev)[0]
            self.last = wires.remote(dst.at[theirs], dst.at[theirs], sib_dev)[0]

        def start(self):
            @pl.when(core == self.layer)
            def _():
                self.over.start()

        def forward(self):
            @pl.when(core == self.layer)
            def _():
                self.over.wait_recv()
                self.dp.start()
                self.rest.start()

        def forward_last(self):
            @pl.when(core == self.layer)
            def _():
                self.dp_in.wait_recv()
                self.last.start()

        def need(self):
            @pl.when(core != self.layer)
            def _():
                self.rest.wait_recv()
                self.last.wait_recv()

        def finish(self):
            @pl.when(core == self.layer)
            def _():
                for c in (self.over, self.dp, self.rest, self.last):
                    c.wait_send()

    odd = lax.rem(z, 2)

    def halves(size, pieces):
        step = size // 2 // pieces
        return [
            tuple(pl.ds(pl.multiple_of(parity_z * (size // 2) + i * step, step), step) for parity_z in (odd, 1 - odd))
            for i in range(pieces)
        ]

    class Layer:
        def __init__(self, layer):
            self.heads_own = Own(layer, qkv, qw.at[layer, 0])
            self.small_own = [Own(layer, pre, pw.at[layer, 0]), Own(layer, pack, pk.at[layer, 0])]
            self.out_own = Own(layer, out_w, ow.at[layer, 0])
            self.units_own = [Away(layer, up_w, gup.at[layer, 0]), Away(layer, down_w, gdown.at[layer, 0])]
            if layer == 0:
                (mine, theirs), = halves(D, 1)
                self.heads = [
                    Shared(layer, qkv.at[i], qw.at[layer, 1, i], mine, theirs, x_dev) for i in range(3)
                ]
            else:
                self.heads = [Direct(layer, qkv, qw.at[layer, 1], x_dev)]
            self.small = [Direct(layer, pre, pw.at[layer, 1], x_dev), Direct(layer, pack, pk.at[layer, 1], y_dev)]
            self.out_x = Direct(layer, out_w, ow.at[layer, 1], x_dev)
            (mine, theirs), = halves(QUARTER, 1)
            self.out_y = [
                Shared(layer, out_w, ow.at[layer, 2], mine, theirs, y_dev),
                Shared(layer, ow.at[layer, 1], ow.at[layer, 3], mine, theirs, y_dev),
            ]
            self.units = [
                Shared(layer, src, dst.at[layer, 1], mine, theirs, y_dev)
                for src, dst in ((up_w, gup), (down_w, gdown))
                for mine, theirs in halves(UNITS, 2)
            ]

        def everything(self):
            return (
                [self.heads_own, self.out_own, self.out_x] + self.small_own + self.units_own + self.heads + self.small
                + self.out_y + self.units
            )

    layers = [Layer(0), Layer(1)]

    def each(items, action):
        for item in items:
            getattr(item, action)()

    loads = {}

    def load_units(layer, when):
        mine = [wires.local(up_w, uw.at[0]), wires.local(down_w, dw.at[0])]
        sibs = [
            wires.local(gup.at[layer, 0], uw.at[0], wires.locals - 2),
            wires.local(gdown.at[layer, 0], dw.at[0], wires.locals - 1),
        ]
        rest = [wires.local(gup.at[layer, 1], uw.at[1]), wires.local(gdown.at[layer, 1], dw.at[1])]

        @pl.when(core == layer)
        def _():
            for c in mine:
                c.start()

        @pl.when(core != layer)
        def _():
            for c in sibs:
                c.start()

        for c in rest:
            c.start()
        loads[layer, when] = mine + rest

    def wait_units(layer, when):
        for c in loads[layer, when]:
            c.wait()

    class Tokens:
        def __init__(self, source, dest):
            self.near = wires.local(source.at[low], dest)
            self.far = wires.remote(source.at[1 - low], dest, x_dev)[0]

        def start(self):
            @pl.when(core == 0)
            def _():
                self.near.start()

            @pl.when(core == 1)
            def _():
                self.far.start()

        def wait(self):
            @pl.when(core == 0)
            def _():
                self.near.wait()

            @pl.when(core == 1)
            def _():
                self.far.wait_recv()

        def finish(self):
            @pl.when(core == 1)
            def _():
                self.far.wait_send()

    tokens = Tokens(states, xb.at[0])
    ends = Tokens(cotangent, cot)

    first = layers[0]
    tokens.start()
    each([first.heads_own] + first.small_own, "start")
    tokens.wait()

    def chunk_rows(step):
        return pl.ds(step * CHUNK, CHUNK)

    def send_chunk(src, dst, device):
        copy, _ = wires.remote(src, dst, device)
        copy.start()
        return copy

    gathers = {}

    def gather_x(layer, step):
        gathers[layer, step] = send_chunk(
            xb.at[layer, chunk_rows(step)], xg.at[chunk_rows(step)], y_dev
        )

    for step in range(STEPS):
        gather_x(0, step)

    @pl.when(core == 0)
    def _():
        for step in range(STEPS):
            gathers[0, step].wait_send()

    each(first.heads + first.small, "start")

    parity = low + core - 2 * low * core
    row = segments[pl.ds(low, 1), :]
    last = row[:, LEN - 1 :]

    def block_labels(block):
        ids = last - segments[pl.ds(low, 1), pl.ds(pl.multiple_of(block * ROWS, ROWS), ROWS)]
        numbers = lax.broadcasted_iota(jnp.int32, (LABELS, ROWS), 0)
        same = jnp.where(numbers == ids, 1.0, 0.0)
        return same.T, jnp.where(numbers <= 2 * SPAN, HIDDEN * (1.0 - same), 0.0).T

    for index, (h, p) in enumerate(((high, parity), (1 - high, parity), (high, 1 - parity), (1 - high, 1 - parity))):
        same, differ = block_labels(2 * h + p)
        if index < 2:
            lab_q[pl.ds(index * ROWS, ROWS), :] = same.astype(BF16)
        lab_k[pl.ds(index * ROWS, ROWS), :] = differ.astype(BF16)

    def project(layer, source, start, size, slots=(0, 1)):
        for slot in slots:
            columns = slice(slot * QUARTER, (slot + 1) * QUARTER)
            rows = pl.ds(start, size)
            qs[layer, rows, columns] = dot(source, qw[layer, slot, 0]).astype(BF16)
            kv[layer, rows, columns] = dot(source, qw[layer, slot, 1]).astype(BF16)
            kv[layer, rows, slice(CORE + columns.start, CORE + columns.stop)] = dot(
                source, qw[layer, slot, 2]
            ).astype(BF16)

    def lanes(index, base=0):
        return pl.ds(pl.multiple_of(base + index * PAIR, PAIR), PAIR)

    def fill(layer, p):
        pre_lanes = pl.ds(pl.multiple_of(lax.rem(p, 2) * PAIR, PAIR), PAIR)
        keys[:CORE, :PAIR] = kv[layer, :, lanes(p)]
        keys[CORE : 2 * CORE, :PAIR] = kvs[layer, :, lanes(p)]
        keys[2 * CORE :, :PAIR] = pw[layer, p // 2, 0, :, pre_lanes]
        return kv[layer, :, lanes(p, CORE)], kvs[layer, :, lanes(p, CORE)], pw[layer, p // 2, 1, :, pre_lanes]

    keys[: 2 * CORE, PAIR:] = lab_k[...]
    keys[2 * CORE :, PAIR:] = jnp.zeros((PREFIX, LABELS), BF16)

    def attend_rows(layer, start):
        rows = pl.ds(start, ROWS)

        def body(p, _):
            vo, vs, vp = fill(layer, p)
            vals_t[:, :CORE] = vo.T
            vals_t[:, CORE : 2 * CORE] = vs.T
            vals_t[:, 2 * CORE :] = vp.T
            query = qs[layer, rows, lanes(p)] * 0.125
            label = lab_q[rows, :]
            results = []
            for head in range(2):
                mine = jnp.where(head_lanes(ROWS, head), query, 0)
                scores = dot_t(keys[...], jnp.concatenate([mine, label], 1))
                peak = jnp.max(scores, axis=0, keepdims=True)
                weights = jnp.exp(scores - peak)
                total = jnp.sum(weights, axis=0, keepdims=True)
                merged = dot(vals_t[head * HEAD : (head + 1) * HEAD, :], weights.astype(BF16))
                results.append(merged / total)
                lse[layer, p, head : head + 1, rows] = peak + jnp.log(total)
            mg[layer, rows, lanes(p)] = jnp.concatenate(results, 0).T.astype(BF16)
            return 0

        lax.fori_loop(0, PAIRS, body, 0)

    def attend_rows_back(layer, start, fresh):
        rows = pl.ds(start, ROWS)

        def body(p, _):
            vo, vs, vp = fill(layer, p)
            vals[:CORE, :] = vo
            vals[CORE : 2 * CORE, :] = vs
            vals[2 * CORE :, :] = vp
            vals_t[:, :CORE] = keys[:CORE, :PAIR].T
            vals_t[:, CORE : 2 * CORE] = keys[CORE : 2 * CORE, :PAIR].T
            vals_t[:, 2 * CORE :] = keys[2 * CORE :, :PAIR].T
            query = qs[layer, rows, lanes(p)] * 0.125
            label = lab_q[rows, :]
            grad_part = gm[rows, lanes(p)]
            product = (grad_part.astype(F32) * mg[layer, rows, lanes(p)].astype(F32)).T
            queries, grad_list, weights_all, scores_all, results = [], [], [], [], []
            for head in range(2):
                span = slice(head * HEAD, (head + 1) * HEAD)
                mine = jnp.where(head_lanes(ROWS, head), query, 0)
                mine_grad = jnp.where(head_lanes(ROWS, head), grad_part, 0)
                scores = dot_t(keys[...], jnp.concatenate([mine, label], 1))
                weights = jnp.exp(scores - lse[layer, p, head : head + 1, rows])
                delta = jnp.sum(product[span], axis=0, keepdims=True)
                grad_scores = (weights * (dot_t(vals[...], mine_grad) - delta)).astype(BF16)
                results.append(dot(vals_t[span, :], grad_scores))
                queries.append(mine)
                grad_list.append(mine_grad)
                weights_all.append(weights.astype(BF16))
                scores_all.append(grad_scores)
            dq[rows, lanes(p)] = (jnp.concatenate(results, 0).T * 0.125).astype(BF16)
            dv_part = dot(jnp.concatenate(weights_all, 1), jnp.concatenate(grad_list, 0))
            dk_part = dot(jnp.concatenate(scores_all, 1), jnp.concatenate(queries, 0))
            if fresh:
                dv_acc[:, lanes(p)] = dv_part
                dk_acc[:, lanes(p)] = dk_part
            else:
                dv_acc[:, lanes(p)] += dv_part
                dk_acc[:, lanes(p)] += dk_part
            return 0

        lax.fori_loop(0, PAIRS, body, 0)

    def vector(layer, index):
        return pk[layer, 0, index : index + 1, :]

    def keep_norm(store, scales, layer, rows, normed, scale):
        store[layer, rows, :] = normed.astype(BF16)
        scales[layer, rows, :] = jnp.broadcast_to(scale, (CHUNK, PAIR))

    def forward_attention(layer):
        this, later = layers[layer], layers[1]
        if layer == 0:
            this.heads_own.need()
            project(0, xb[0], 0, ROWS, (0,))
            for step in range(STEPS):
                gathers[0, step].wait_recv()
                project(0, xg[chunk_rows(step), :], ROWS + step * CHUNK, CHUNK, (0,))
            each(this.units, "start")
            this.out_x.start()
            each(this.heads, "forward")
            each(this.small, "forward")
            each(this.heads, "forward_last")
            each([this.out_own] + this.units_own, "start")
            each(this.heads + this.small_own + this.small, "need")
            project(0, xb[0], 0, ROWS, (1,))
            sent = [send_chunk(kv.at[0, :ROWS], kvs.at[0, :ROWS], sib_dev)]
            project(0, xg[...], ROWS, ROWS, (1,))
            sent.append(send_chunk(kv.at[0, ROWS:], kvs.at[0, ROWS:], sib_dev))
            this.out_x.forward()
            each(this.out_y, "start")
            each(later.heads + later.small, "start")
            each(this.units[:2], "forward")
        else:
            each([this.heads_own] + this.heads + this.small_own + this.small, "need")
            project(1, xb[1], 0, ROWS)
            sent = [send_chunk(kv.at[1, :ROWS], kvs.at[1, :ROWS], sib_dev)]
            for step in range(STEPS):
                gathers[1, step].wait_recv()
                project(1, xg[chunk_rows(step), :], ROWS + step * CHUNK, CHUNK)
            sent.append(send_chunk(kv.at[1, ROWS:], kvs.at[1, ROWS:], sib_dev))
            each(this.out_y, "start")
        for c in sent:
            c.wait_recv()
        attend_rows(layer, ROWS)
        swap = send_chunk(mg.at[layer, ROWS:], mrecv, y_dev)
        if layer == 0:
            each(this.units[2:], "forward")
            each(this.units[:2], "forward_last")
        else:
            each(this.out_y, "forward")
            each(this.units, "forward_last")
        attend_rows(layer, 0)
        if layer == 0:
            each(this.out_y, "forward")
            each(this.units[2:], "forward_last")
            each(this.out_y, "forward_last")
            ends.start()
        else:
            each(this.out_y, "forward_last")
        each(this.units_own + this.units, "need")
        load_units(layer, 0)
        each([this.out_own, this.out_x] + this.out_y, "need")
        swap.wait_recv()
        copies = []
        for step in range(STEPS):
            rows = chunk_rows(step)
            parts = [mg[layer, rows, :QUARTER], mg[layer, rows, QUARTER:], mrecv[rows, :QUARTER], mrecv[rows, QUARTER:]]
            total = xb[layer, rows, :].astype(F32) + vector(layer, 3)
            for i, part in enumerate(parts):
                total = total + dot(part, ow[layer, i])
            normed, scale = norm_chunk(total)
            keep_norm(n1, r1, layer, rows, normed, scale)
            middle = normed * vector(layer, 1) + vector(layer, 4)
            mid[rows, :] = middle
            fsnd[rows, :] = middle.astype(BF16)
            copies.append(send_chunk(fsnd.at[rows], fin.at[rows], x_dev))
        for c in sent + [swap]:
            c.wait_send()

        def gathered():
            for step in range(STEPS):
                gathers[layer, step].wait_send()

        gathered() if layer == 1 else pl.when(core == 1)(gathered)
        return copies

    def feed_rows(layer, source, start, size):
        def up_tile(j, _):
            slot, columns = j // 4, pl.ds(pl.multiple_of(lax.rem(j, 4) * TILE, TILE), TILE)
            wide = pl.ds(pl.multiple_of(j * TILE, TILE), TILE)
            u = dot(source[...], uw[slot, :, columns]) + pk[layer, slot, 0:1, columns]
            act[:size, wide], slopes[layer, pl.ds(start, size), wide] = gelu_both(u)
            return 0

        lax.fori_loop(0, 2 * UNITS // TILE, up_tile, 0)

    def feed_rows_back(layer, source, start, size):
        def tile(j, _):
            slot, units_at = j // 4, pl.ds(pl.multiple_of(lax.rem(j, 4) * TILE, TILE), TILE)
            wide = pl.ds(pl.multiple_of(j * TILE, TILE), TILE)
            u = dot_t(source[...], dw[slot, units_at, :]) * slopes[layer, pl.ds(start, size), wide].astype(F32)
            act[:size, wide] = u.astype(BF16)
            return 0

        lax.fori_loop(0, 2 * UNITS // TILE, tile, 0)

    def feed_out(store, size, back):
        def tile(j, _):
            columns = pl.ds(pl.multiple_of(j * TILE, TILE), TILE)
            if back:
                u = dot_t(act[:size, :UNITS], uw[0, columns, :]) + dot_t(act[:size, UNITS:], uw[1, columns, :])
            else:
                u = dot(act[:size, :UNITS], dw[0, :, columns]) + dot(act[:size, UNITS:], dw[1, :, columns])
            store[:, columns] = u.astype(store.dtype)
            return 0

        lax.fori_loop(0, D // TILE, tile, 0)

    def feed(layer, copies, back, finish):
        rows_fn = feed_rows_back if back else feed_rows
        rows_fn(layer, fsnd, 0, ROWS)
        feed_out(acc, ROWS, back)
        returned = []
        for step in range(STEPS):
            rows = chunk_rows(step)
            copies[step].wait_recv()
            rows_fn(layer, fin.at[rows], ROWS + step * CHUNK, CHUNK)
            feed_out(fout.at[rows], CHUNK, back)
            returned.append(send_chunk(fout.at[rows], fret.at[rows], x_dev))
        for step in range(STEPS):
            returned[step].wait_recv()
            finish(step, chunk_rows(step), acc[chunk_rows(step), :] + fret[chunk_rows(step), :].astype(F32))
        for c in copies + returned:
            c.wait_send()

    deliveries = []

    def deliver(layer, source, dest, step):
        rows = chunk_rows(step)
        far, number = wires.remote(source.at[rows], dest.at[low, rows], {"section": layer, "tensor": across})
        far_in, _ = wires.remote(source.at[rows], dest.at[1 - low, rows], {"section": layer, "tensor": across}, number)
        if layer == 0:
            near = wires.local(source.at[rows], dest.at[low, rows])
        else:
            near, _ = wires.remote(source.at[rows], dest.at[low, rows], sib_dev)

        @pl.when(core == 0)
        def _():
            near.start()

        @pl.when(core == 1)
        def _():
            far.start()

        def sent():
            @pl.when(core == 0)
            def _():
                near.wait() if layer == 0 else near.wait_send()

            @pl.when(core == 1)
            def _():
                far.wait_send()

        def arrived():
            @pl.when(core == layer)
            def _():
                far_in.wait_recv()
                if layer == 1:
                    near.wait_recv()

        deliveries.append(arrived)
        return sent

    def start_back(layer, step, rows, grad):
        normed, scale = n2[layer, rows, :].astype(F32), r2[layer, rows, :1]
        value = norm_back(grad, vector(layer, 2), normed, scale)
        gsec[rows, :] = value
        fsnd[rows, :] = value.astype(BF16)
        return send_chunk(fsnd.at[rows], fin.at[rows], x_dev)

    unsent = []
    back_copies = []

    def forward_finish(layer):
        def finish(step, rows, branch):
            normed, scale = norm_chunk(mid[rows, :] + branch + vector(layer, 5))
            keep_norm(n2, r2, layer, rows, normed, scale)
            xb[layer + 1, rows, :] = (normed * vector(layer, 2) + vector(layer, 6)).astype(BF16)
            if layer == 0:
                gather_x(1, step)
            unsent.append(deliver(layer, xb.at[layer + 1], hidden, step))

        return finish

    copies = forward_attention(0)
    wait_units(0, 0)
    second = layers[1]
    each([second.heads_own] + second.small_own + [second.out_own] + second.units_own, "start")
    each(second.units, "start")
    second.out_x.start()
    each(second.heads + second.small, "forward")
    feed(0, copies, False, forward_finish(0))
    second.out_x.forward()
    each(second.units, "forward")
    copies = forward_attention(1)
    wait_units(1, 0)
    feed(1, copies, False, forward_finish(1))

    ends.wait()
    for step in range(STEPS):
        back_copies.append(start_back(1, step, chunk_rows(step), cot[chunk_rows(step), :].astype(F32)))

    grad_sent = []

    def backward(layer, copies):
        swaps = []

        def finish(step, rows, term):
            middle = gsec[rows, :] + term
            first = norm_back(middle, vector(layer, 1), n1[layer, rows, :].astype(F32), r1[layer, rows, :1])
            gfirst[rows, :] = first
            low_first = first.astype(BF16)
            for i in range(4):
                part = dot_t(low_first, ow[layer, i]).astype(BF16)
                columns = slice((i % 2) * QUARTER, (i % 2 + 1) * QUARTER)
                if i < 2:
                    gm[rows, columns] = part
                else:
                    gms[rows, columns] = part
            swaps.append(send_chunk(gms.at[rows], gm.at[pl.ds(ROWS + step * CHUNK, CHUNK)], y_dev))

        feed(layer, copies, True, finish)
        if layer == 1:
            load_units(0, 1)
        attend_rows_back(layer, 0, True)
        for c in swaps:
            c.wait_recv()
        attend_rows_back(layer, ROWS, False)
        dkv_send[:, :CORE] = dk_acc[CORE : 2 * CORE, :].astype(BF16)
        dkv_send[:, CORE:] = dv_acc[CORE : 2 * CORE, :].astype(BF16)
        given = send_chunk(dkv_send, dkv_recv.at[layer], sib_dev)
        pacc[layer, 0] = dk_acc[2 * CORE :, :]
        pacc[layer, 1] = dv_acc[2 * CORE :, :]
        if layer == 0:
            total = prefix_start()
        given.wait_recv()
        dkv[:, :CORE] = (dk_acc[:CORE, :] + dkv_recv[layer, :, :CORE].astype(F32)).astype(BF16)
        dkv[:, CORE:] = (dv_acc[:CORE, :] + dkv_recv[layer, :, CORE:].astype(F32)).astype(BF16)

        def input_term(store, start, size):
            rows = pl.ds(start, size)

            def tile(j, _):
                features = pl.ds(pl.multiple_of(j * TILE, TILE), TILE)
                total = None
                for slot in range(2):
                    columns = slice(slot * QUARTER, (slot + 1) * QUARTER)
                    shifted = slice(CORE + slot * QUARTER, CORE + (slot + 1) * QUARTER)
                    for part, source in enumerate((dq[rows, columns], dkv[rows, columns], dkv[rows, shifted])):
                        term = dot_t(source, qw[layer, slot, part, features, :])
                        total = term if total is None else total + term
                store[:, features] = total.astype(store.dtype)
                return 0

            lax.fori_loop(0, D // TILE, tile, 0)

        returned = []
        for step in range(STEPS):
            input_term(dxs.at[chunk_rows(step)], ROWS + step * CHUNK, CHUNK)
            returned.append(send_chunk(dxs.at[chunk_rows(step)], dxr.at[chunk_rows(step)], y_dev))
        if layer == 0:
            total.stage()
        input_term(acc, 0, ROWS)
        if layer == 1:
            wait_units(0, 1)
        else:
            total.stage()
        for sent in grad_sent:
            sent()
        grad_sent.clear()
        onward = []
        for step in range(STEPS):
            rows = chunk_rows(step)
            returned[step].wait_recv()
            value = gfirst[rows, :] + (acc[rows, :] + dxr[rows, :].astype(F32))
            gout[rows, :] = value
            grad_sent.append(deliver(layer, gout, grads, step))
            if layer == 1:
                onward.append(start_back(0, step, rows, value.astype(BF16).astype(F32)))
            else:
                total.stage()
        for c in swaps + [given] + returned:
            c.wait_send()
        return onward

    class prefix_start:
        def __init__(self):
            self.sib = send_chunk(pacc.at[1 - core], psib, sib_dev)
            self.sent = [self.sib]
            self.at = 0

        def stage(self):
            if self.at == 0:
                self.sib.wait_recv()
                total = pacc[core] + psib[...]
                psum[0] = total[:, :, :QUARTER]
                pacross[0] = total[:, :, QUARTER:]
                self.next = send_chunk(pacross.at[0], pacross.at[1], x_dev)
                self.sent.append(self.next)
            elif self.at <= len(dp_steps) + 1:
                self.next.wait_recv()
                arrived = pacross[1] if self.at == 1 else pdp[self.at - 2]
                psum[self.at] = psum[self.at - 1] + arrived
                if self.at <= len(dp_steps):
                    step = self.at - 1
                    self.next = send_chunk(psum.at[self.at], pdp.at[step], dp_dev(dp_steps[step]))
                    self.sent.append(self.next)
                else:
                    self.done = wires.local(psum.at[self.at], pgrads)
                    self.done.start()
            self.at += 1

        def finish(self):
            while self.at <= len(dp_steps) + 1:
                self.stage()
            for c in self.sent:
                c.wait_send()
            self.done.wait()

    holder = []
    start_class = prefix_start

    def prefix_start():
        holder.append(start_class())
        return holder[0]

    back_copies = backward(1, back_copies)
    backward(0, back_copies)
    holder[0].finish()
    for sent in unsent + grad_sent:
        sent()
    for arrived in deliveries:
        arrived()
    tokens.finish()
    ends.finish()
    for layer in layers:
        each(layer.everything(), "finish")


def fused(dp, states, cotangent, segments, qkv, out_w, up_w, down_w, pre, pack):
    shape = jax.ShapeDtypeStruct
    steps = dp.bit_length() - 1
    vmem = pltpu.VMEM
    scratch = [
        vmem((3, ROWS, D), BF16),
        vmem((ROWS, D), BF16),
        vmem((ROWS, D), BF16),
        vmem((CORE, LABELS), BF16), vmem((2 * CORE, LABELS), BF16),
        vmem((2, 2, 3, D, QUARTER), BF16),
        vmem((2, 4, QUARTER, D), BF16),
        vmem((2, D, UNITS), BF16), vmem((2, UNITS, D), BF16),
        vmem((2, 2, 2, PREFIX, QUARTER), BF16),
        vmem((2, 2, 8, D), F32),
        vmem((2, CORE, CORE), BF16), vmem((2, CORE, 2 * CORE), BF16), vmem((2, CORE, 2 * CORE), BF16),
        vmem((2, CORE, CORE), BF16), vmem((2, PAIRS, 8, CORE), F32),
        vmem((2, ROWS, D), BF16), vmem((2, ROWS, PAIR), F32),
        vmem((2, ROWS, D), BF16), vmem((2, ROWS, PAIR), F32),
        vmem((2, CORE, 2 * UNITS), BF16),
        vmem((ROWS, D), F32), vmem((ROWS, D), F32), vmem((ROWS, 2 * UNITS), BF16),
        vmem((ROWS, CORE), BF16),
        vmem((ROWS, D), BF16), vmem((ROWS, D), BF16), vmem((ROWS, D), BF16), vmem((ROWS, D), BF16),
        vmem((ROWS, D), F32), vmem((ROWS, D), F32),
        vmem((CORE, CORE), BF16), vmem((ROWS, CORE), BF16), vmem((ROWS, D), F32),
        vmem((KEYS, PAIR + LABELS), BF16), vmem((PAIR, KEYS), BF16), vmem((KEYS, PAIR), BF16),
        vmem((KEYS, CORE), F32), vmem((KEYS, CORE), F32),
        vmem((CORE, CORE), BF16), vmem((CORE, 2 * CORE), BF16), vmem((CORE, 2 * CORE), BF16),
        vmem((2, CORE, 2 * CORE), BF16),
        vmem((ROWS, D), BF16), vmem((ROWS, D), BF16),
        vmem((2, 2, PREFIX, CORE), F32), vmem((2, PREFIX, CORE), F32),
        vmem((2, 2, PREFIX, QUARTER), F32), vmem((steps + 2, 2, PREFIX, QUARTER), F32),
        vmem((max(steps, 1), 2, PREFIX, QUARTER), F32),
        pltpu.SemaphoreType.DMA((SEMS,)), pltpu.SemaphoreType.DMA((SEMS,)), pltpu.SemaphoreType.DMA((SEMS,)),
    ]
    anywhere = pl.BlockSpec(memory_space=pl.ANY)
    result = pl.pallas_call(
        functools.partial(fused_kernel, dp),
        out_shape=[
            shape((2, ROWS, D), BF16), shape((2, ROWS, D), F32), shape((2, PREFIX, QUARTER), F32),
            shape((2, 2, D, UNITS), BF16), shape((2, 2, UNITS, D), BF16),
        ],
        in_specs=[anywhere, anywhere, pl.BlockSpec(memory_space=pltpu.VMEM)] + [anywhere] * 6,
        out_specs=[anywhere] * 5,
        scratch_shapes=scratch,
        compiler_params=pltpu.CompilerParams(
            collective_id=0, has_side_effects=True, vmem_limit_bytes=63 << 20
        ),
        name="layers",
    )(states, cotangent, segments, qkv, out_w, up_w, down_w, pre, pack)
    return result[:3]


class Links:
    def __init__(self):
        self.core = lax.axis_index("section")
        self.place = lax.axis_index("tensor")
        self.size = lax.axis_size("tensor")
        self.low = self.place % 2
        self.high = self.place // 2
        self.group = self.size // 2

    def sibling(self, a, only=None):
        pairs = [(0, 1), (1, 0)] if only is None else [(only, 1 - only)]
        return lax.ppermute(a, "section", pairs)

    def across(self, a, only=None):
        if only is None:
            return lax.ppermute(a, "tensor", [(t, t ^ 1) for t in range(self.size)])
        pairs = [(only * self.size + t, only * self.size + (t ^ 1)) for t in range(self.size)]
        return lax.ppermute(a, ("section", "tensor"), pairs)

    def diagonal(self, a, source):
        pairs = [(source * self.size + t, (1 - source) * self.size + (t ^ 1)) for t in range(self.size)]
        return lax.ppermute(a, ("section", "tensor"), pairs)

    def from_ahead(self, a, by):
        g = self.group
        pairs = [(2 * ((h + by) % g) + p, 2 * h + p) for h in range(g) for p in range(2)]
        return lax.ppermute(a, "tensor", pairs)

    def gather(self, a):
        return [a] + [self.from_ahead(a, k) for k in range(1, self.group)]

    def scatter_sum(self, part_fn):
        arrived = [self.from_ahead(part_fn(k).astype(BF16), self.group - k) for k in range(1, self.group)]
        total = part_fn(0)
        for a in arrived:
            total = total + a.astype(F32)
        return total


def forward(links, x, weights, pre, labels):
    qkv_w, out_w, up_w, up_b, down_w, gains, shifts = weights
    width = out_w.shape[0]
    blocks = [dot(b, qkv_w).astype(BF16) for b in links.gather(x)]
    qkv = jnp.concatenate(blocks, 0)
    kv_sib = links.sibling(qkv[:, width:])
    merged, lse = attend(qkv, kv_sib, pre, labels)
    rows = x.shape[0]
    attended = links.scatter_sum(lambda k: dot(merged[k * rows : (k + 1) * rows], out_w)) + shifts[0]
    normed_first, scale_first = norm_stats(x.astype(F32) + attended)
    middle = normed_first * gains[0] + shifts[1]
    blocks = links.gather(middle.astype(BF16))
    pairs = [gelu_pair(dot(b, up_w) + up_b) for b in blocks]
    branch = links.scatter_sum(lambda k: dot(pairs[k][0], down_w)) + shifts[2]
    normed_last, scale_last = norm_stats(middle + branch)
    result = (normed_last * gains[1] + shifts[3]).astype(BF16)
    slopes = [p[1] for p in pairs]
    return result, (qkv, kv_sib, merged, lse, normed_first, scale_first, slopes, normed_last, scale_last)


def backward(links, grad, weights, pre, labels, kept):
    qkv_w, out_w, up_w, up_b, down_w, gains, shifts = weights
    qkv, kv_sib, merged, lse, normed_first, scale_first, slopes, normed_last, scale_last = kept
    rows = grad.shape[0]
    grad_second = norm_back(grad.astype(F32), gains[1], normed_last, scale_last)
    blocks = links.gather(grad_second.astype(BF16))
    hiddens = [
        (dot_t(b, down_w) * s.astype(F32)).astype(BF16) for b, s in zip(blocks, slopes, strict=True)
    ]
    grad_middle = grad_second + links.scatter_sum(lambda k: dot_t(hiddens[k], up_w))
    grad_first = norm_back(grad_middle, gains[0], normed_first, scale_first)
    blocks = links.gather(grad_first.astype(BF16))
    grad_merged = jnp.concatenate([dot_t(b, out_w).astype(BF16) for b in blocks], 0)
    dq, dko, dvo, dks, dvs, dkp, dvp = attend_back(qkv, kv_sib, pre, labels, merged, lse, grad_merged)
    arrived = links.sibling(jnp.concatenate([dks, dvs], 1)).astype(F32)
    width = out_w.shape[0]
    dk = (dko + arrived[:, :width]).astype(BF16)
    dv = (dvo + arrived[:, width:]).astype(BF16)
    dqkv = jnp.concatenate([dq, dk, dv], 1)
    grad_inputs = grad_first + links.scatter_sum(
        lambda k: dot_t(dqkv[k * rows : (k + 1) * rows], qkv_w)
    )
    return grad_inputs, jnp.stack([dkp, dvp])


def spread_weights(links, arrays):
    first = links.core == 0
    layers = ([], [])
    for layer in range(2):
        for a in arrays:
            other = links.across(a, layer)
            sib_a, sib_other = links.sibling(a, layer), links.sibling(other, layer)
            here = links.core == layer
            layers[layer].append((jnp.where(here, a, sib_a), jnp.where(here, other, sib_other)))
    return layers


def sum_over_dp(a):
    size = lax.axis_size("dp")
    step = 1
    if size & (size - 1):
        return lax.psum(a, "dp")
    while step < size:
        a = a + lax.ppermute(a, "dp", [(i, i ^ step) for i in range(size)])
        step *= 2
    return a


def plain(
    states, segment_ids, cotangent, qkv_weight, out_weight, up_weight, up_bias, down_weight,
    norm_gain, shift_vec, prefix,
):
    links = Links()
    first = links.core == 0
    low = links.low

    def arrange(both):
        mine = lax.dynamic_index_in_dim(both, low, 0, keepdims=False)
        other = lax.dynamic_index_in_dim(both, 1 - low, 0, keepdims=False)
        return jnp.where(first, mine, links.across(other, 1))

    x = arrange(states)
    grad = arrange(cotangent)

    segment = lax.dynamic_index_in_dim(segment_ids, low, 0, keepdims=False)
    classes = (segment[-1] - segment).reshape(links.group, 2, -1)
    classes = jnp.roll(classes, -links.high, 0)
    parity = jnp.where(first, low, 1 - low)
    own = lax.dynamic_index_in_dim(classes, parity, 1, keepdims=False).reshape(-1)
    sib = lax.dynamic_index_in_dim(classes, 1 - parity, 1, keepdims=False).reshape(-1)
    numbers = jnp.arange(LABELS)[None, :]
    label_q = (own[:, None] == numbers).astype(BF16)
    known = numbers <= 2 * SPAN
    label_o = jnp.where(known & (own[:, None] != numbers), HIDDEN, 0.0).astype(BF16)
    label_s = jnp.where(known & (sib[:, None] != numbers), HIDDEN, 0.0).astype(BF16)
    labels = (label_q, label_o, label_s)

    small = jnp.concatenate(
        [norm_gain[0], shift_vec[0]], 0
    )
    small_sib = links.sibling(small)
    layers = spread_weights(
        links,
        [jnp.transpose(qkv_weight[0], (1, 0, 2)), prefix[0], out_weight[0], up_weight[0], up_bias, down_weight[0]],
    )
    weights, prefixes = [], []
    for layer in range(2):
        qkv, pre, out, up, bias, down = layers[layer]
        vectors = jnp.where(links.core == layer, small, small_sib).astype(F32)
        weights.append((
            jnp.concatenate([p[i] for i in range(3) for p in qkv], 1),
            jnp.concatenate(out, 0),
            jnp.concatenate(up, 1),
            jnp.concatenate(bias, 1).astype(F32),
            jnp.concatenate(down, 0),
            vectors[:2],
            vectors[2:],
        ))
        prefixes.append(jnp.concatenate(pre, 2))

    y0, kept0 = forward(links, x, weights[0], prefixes[0], labels)
    y1, kept1 = forward(links, y0, weights[1], prefixes[1], labels)
    g1, p1 = backward(links, grad, weights[1], prefixes[1], labels, kept1)
    g0, p0 = backward(links, g1.astype(BF16), weights[0], prefixes[0], labels, kept0)

    def deliver(first_layer, second_layer, wire, dtype):
        near = jnp.where(first, first_layer.astype(dtype), links.sibling(second_layer.astype(wire), 0).astype(dtype))
        far0 = links.diagonal(first_layer.astype(wire), 1)
        far1 = links.across(second_layer.astype(wire), 1)
        far = jnp.where(first, far0, far1).astype(dtype)
        return jnp.stack([jnp.where(low == 0, near, far), jnp.where(low == 0, far, near)])

    hidden_out = deliver(y0, y1, BF16, BF16)
    input_grads = deliver(g0, g1, BF16, F32)

    total = jnp.where(first, p0, p1) + links.sibling(jnp.where(first, p1, p0))
    quarter = total.shape[-1] // 2
    total = total[..., :quarter] + links.across(total[..., quarter:])
    prefix_grads = sum_over_dp(total)
    return hidden_out[None], input_grads[None], prefix_grads[None]


def whole_kernel(
    states, segment_ids, cotangent, qkv_weight, out_weight, up_weight, up_bias, down_weight,
    norm_gain, shift_vec, prefix,
):
    pack = jnp.concatenate([up_bias, norm_gain[0], shift_vec[0], jnp.zeros_like(up_bias)], 0).astype(F32)
    results = fused(
        lax.axis_size("dp"), states, cotangent, segment_ids, jnp.transpose(qkv_weight[0], (1, 0, 2)),
        out_weight[0], up_weight[0], down_weight[0], prefix[0], pack,
    )
    return tuple(r[None] for r in results)


def fits(mesh):
    dp = mesh.shape["dp"]
    return mesh.shape["tensor"] == 4 and dp > 1 and dp & (dp - 1) == 0


def solution(mesh):
    placed = (
        P(None, ("dp", "tensor"), None),
        P(None, "dp"),
        P(None, ("dp", "tensor"), None),
        P("section", None, None, "tensor"),
        P("section", "tensor", None),
        P("section", None, "tensor"),
        P("section", "tensor"),
        P("section", "tensor", None),
        P("section", None, None),
        P("section", None, None),
        P("section", None, None, "tensor"),
    )
    return jax.shard_map(
        whole_kernel if fits(mesh) else plain,
        mesh=mesh,
        in_specs=placed,
        out_specs=(
            P("section", None, ("dp", "tensor"), None),
            P("section", None, ("dp", "tensor"), None),
            P("section", None, None, "tensor"),
        ),
        check_vma=False,
    )
```

```python
import functools

import jax
import jax.numpy as jnp
from jax import lax
from jax.experimental import pallas as pl
from jax.experimental.pallas import tpu as pltpu
from jax.sharding import PartitionSpec as P

D = 1024
HEAD = 64
PAIR = 2 * HEAD
PREFIX = 64
LEN = 1024
SPAN = LEN // 32
LABELS = 128
HIDDEN = -1e30
F32 = jnp.float32
BF16 = jnp.bfloat16


def dot(a, b):
    return jnp.dot(a, b, preferred_element_type=F32)


def dot_t(a, b):
    return lax.dot_general(a, b, (((1,), (1,)), ((), ())), preferred_element_type=F32)


def head_lanes(rows, head):
    lanes = lax.broadcasted_iota(jnp.int32, (rows, PAIR), 1)
    return (lanes >= head * HEAD) & (lanes < (head + 1) * HEAD)


def fill_keys(keys, own, sib, pre, own_lab, sib_lab):
    rows = own.shape[0]
    keys[:rows, :PAIR] = own[...]
    keys[rows : 2 * rows, :PAIR] = sib[...]
    keys[2 * rows :, :PAIR] = pre[...]
    keys[:rows, PAIR:] = own_lab[...]
    keys[rows : 2 * rows, PAIR:] = sib_lab[...]
    keys[2 * rows :, PAIR:] = jnp.zeros((PREFIX, LABELS), BF16)


def attend_kernel(block, q, ko, vo, ks, vs, kp, vp, lab_q, lab_o, lab_s, out, lse, keys, vals_t):
    rows = q.shape[0]
    fill_keys(keys, ko, ks, kp, lab_o, lab_s)
    vals_t[:, :rows] = vo[...].T
    vals_t[:, rows : 2 * rows] = vs[...].T
    vals_t[:, 2 * rows :] = vp[...].T
    for start in range(0, rows, block):
        part = pl.ds(start, block)
        query = q[part, :] * 0.125
        label = lab_q[part, :]
        results = []
        for head in range(2):
            mine = jnp.where(head_lanes(block, head), query, 0)
            scores = dot_t(keys[...], jnp.concatenate([mine, label], 1))
            peak = jnp.max(scores, axis=0, keepdims=True)
            weights = jnp.exp(scores - peak)
            total = jnp.sum(weights, axis=0, keepdims=True)
            merged = dot(vals_t[head * HEAD : (head + 1) * HEAD, :], weights.astype(BF16))
            results.append(merged / total)
            lse[0, head : head + 1, part] = peak + jnp.log(total)
        out[part, :] = jnp.concatenate(results, 0).T.astype(BF16)


def attend_back_kernel(
    block, q, ko, vo, ks, vs, kp, vp, lab_q, lab_o, lab_s, out, lse, grad,
    dq, dko, dvo, dks, dvs, dkp, dvp, keys, vals, keys_t, dk_sum, dv_sum,
):
    rows = q.shape[0]
    fill_keys(keys, ko, ks, kp, lab_o, lab_s)
    vals[:rows, :] = vo[...]
    vals[rows : 2 * rows, :] = vs[...]
    vals[2 * rows :, :] = vp[...]
    keys_t[:, :rows] = ko[...].T
    keys_t[:, rows : 2 * rows] = ks[...].T
    keys_t[:, 2 * rows :] = kp[...].T
    for start in range(0, rows, block):
        part = pl.ds(start, block)
        query = q[part, :] * 0.125
        label = lab_q[part, :]
        grad_part = grad[part, :]
        product = (grad_part.astype(F32) * out[part, :].astype(F32)).T
        queries, grads, weights_all, scores_all, results = [], [], [], [], []
        for head in range(2):
            span = slice(head * HEAD, (head + 1) * HEAD)
            mine = jnp.where(head_lanes(block, head), query, 0)
            mine_grad = jnp.where(head_lanes(block, head), grad_part, 0)
            scores = dot_t(keys[...], jnp.concatenate([mine, label], 1))
            weights = jnp.exp(scores - lse[0, head : head + 1, part])
            delta = jnp.sum(product[span], axis=0, keepdims=True)
            grad_scores = (weights * (dot_t(vals[...], mine_grad) - delta)).astype(BF16)
            results.append(dot(keys_t[span, :], grad_scores))
            queries.append(mine)
            grads.append(mine_grad)
            weights_all.append(weights.astype(BF16))
            scores_all.append(grad_scores)
        dq[part, :] = (jnp.concatenate(results, 0).T * 0.125).astype(BF16)
        dv_part = dot(jnp.concatenate(weights_all, 1), jnp.concatenate(grads, 0))
        dk_part = dot(jnp.concatenate(scores_all, 1), jnp.concatenate(queries, 0))
        if start == 0:
            dv_sum[...] = dv_part
            dk_sum[...] = dk_part
        else:
            dv_sum[...] += dv_part
            dk_sum[...] += dk_part
    dko[...] = dk_sum[:rows, :]
    dvo[...] = dv_sum[:rows, :]
    dks[...] = dk_sum[rows : 2 * rows, :].astype(BF16)
    dvs[...] = dv_sum[rows : 2 * rows, :].astype(BF16)
    dkp[...] = dk_sum[2 * rows :, :]
    dvp[...] = dv_sum[2 * rows :, :]


def attention_specs(rows, pairs):
    def column(height, offset):
        return pl.BlockSpec((height, PAIR), lambda p: (0, offset + p))

    labels = pl.BlockSpec((rows, LABELS), lambda p: (0, 0))
    ins = [
        column(rows, 0), column(rows, pairs), column(rows, 2 * pairs),
        column(rows, 0), column(rows, pairs),
        column(PREFIX, 0), column(PREFIX, 0),
        labels, labels, labels,
    ]
    return column, ins, pl.BlockSpec((1, 8, rows), lambda p: (p, 0, 0))


def attend(qkv, kv_sib, pre, labels):
    rows, width = qkv.shape[0], qkv.shape[1] // 3
    pairs = width // PAIR
    column, ins, lse_spec = attention_specs(rows, pairs)
    size = 2 * rows + PREFIX
    return pl.pallas_call(
        functools.partial(attend_kernel, min(rows, 256)),
        grid=(pairs,),
        in_specs=ins,
        out_specs=[column(rows, 0), lse_spec],
        out_shape=[
            jax.ShapeDtypeStruct((rows, width), BF16),
            jax.ShapeDtypeStruct((pairs, 8, rows), F32),
        ],
        scratch_shapes=[pltpu.VMEM((size, PAIR + LABELS), BF16), pltpu.VMEM((PAIR, size), BF16)],
        compiler_params=pltpu.CompilerParams(vmem_limit_bytes=40 << 20),
        cost_estimate=pl.CostEstimate(
            flops=2 * 2 * rows * size * width, transcendentals=rows * size * width // HEAD,
            bytes_accessed=16 * rows * width,
        ),
        name="attend",
    )(qkv, qkv, qkv, kv_sib, kv_sib, pre[0], pre[1], *labels)


def attend_back(qkv, kv_sib, pre, labels, merged, lse, grad):
    rows, width = qkv.shape[0], qkv.shape[1] // 3
    pairs = width // PAIR
    column, ins, lse_spec = attention_specs(rows, pairs)
    size = 2 * rows + PREFIX
    shape = jax.ShapeDtypeStruct
    return pl.pallas_call(
        functools.partial(attend_back_kernel, min(rows, 256)),
        grid=(pairs,),
        in_specs=ins + [column(rows, 0), lse_spec, column(rows, 0)],
        out_specs=[column(rows, 0)] * 5 + [column(PREFIX, 0)] * 2,
        out_shape=[
            shape((rows, width), BF16),
            shape((rows, width), F32), shape((rows, width), F32),
            shape((rows, width), BF16), shape((rows, width), BF16),
            shape((PREFIX, width), F32), shape((PREFIX, width), F32),
        ],
        scratch_shapes=[
            pltpu.VMEM((size, PAIR + LABELS), BF16), pltpu.VMEM((size, PAIR), BF16),
            pltpu.VMEM((PAIR, size), BF16), pltpu.VMEM((size, PAIR), F32), pltpu.VMEM((size, PAIR), F32),
        ],
        compiler_params=pltpu.CompilerParams(vmem_limit_bytes=40 << 20),
        cost_estimate=pl.CostEstimate(
            flops=5 * 2 * rows * size * width, transcendentals=rows * size * width // HEAD,
            bytes_accessed=32 * rows * width,
        ),
        name="attend_back",
    )(qkv, qkv, qkv, kv_sib, kv_sib, pre[0], pre[1], *labels, merged, lse, grad)


def norm_stats(values):
    center = values - jnp.mean(values, axis=-1, keepdims=True)
    scale = lax.rsqrt(jnp.mean(center * center, axis=-1, keepdims=True) + 1e-05)
    return center * scale, scale


def norm_back(grad, gain, normed, scale):
    dn = grad * gain
    return scale * (
        dn
        - jnp.mean(dn, axis=-1, keepdims=True)
        - normed * jnp.mean(dn * normed, axis=-1, keepdims=True)
    )


def gelu_pair(u):
    cdf = 0.5 * (1.0 + lax.erf(u * 0.7071067811865476))
    pdf = jnp.exp(-0.5 * u * u) * 0.3989422804014327
    return (u * cdf).astype(BF16), (cdf + u * pdf).astype(BF16)


MESH = pl.DeviceIdType.MESH
ROWS = 256
CORE = 2 * ROWS
CHUNK = 128
PART = 64
STEPS = ROWS // CHUNK
QUARTER = D // 4
UNITS = D
TILE = 256
PAIRS = 4
KEYS = 2 * CORE + PREFIX
SEMS = 224


def gelu_both(u):
    size = jnp.abs(u) * 0.7071067811865476
    t = 1.0 / (1.0 + 0.3275911 * size)
    poly = t * (0.254829592 + t * (-0.284496736 + t * (1.421413741 + t * (-1.453152027 + t * 1.061405429))))
    bell = jnp.exp(-(size * size))
    tail = 0.5 * poly * bell
    cdf = jnp.where(u >= 0, 1.0 - tail, tail)
    return (u * cdf).astype(BF16), (cdf + u * (bell * 0.3989422804014327)).astype(BF16)


def norm_chunk(values):
    center = values - jnp.mean(values, axis=-1, keepdims=True)
    scale = lax.rsqrt(jnp.mean(center * center, axis=-1, keepdims=True) + 1e-05)
    return center * scale, scale


class Copies:
    def __init__(self, send, arrive, here):
        self.send, self.arrive, self.here = send, arrive, here
        self.remotes = self.locals = 0

    def remote(self, src, dst, device, number=None):
        if number is None:
            number = self.remotes
            self.remotes += 1
        copy = pltpu.make_async_remote_copy(
            src_ref=src, dst_ref=dst, send_sem=self.send.at[number], recv_sem=self.arrive.at[number],
            device_id=device, device_id_type=MESH,
        )
        return copy, number

    def local(self, src, dst, number=None):
        if number is None:
            number = self.locals
            self.locals += 1
        return pltpu.make_async_copy(src, dst, self.here.at[number])


def fused_kernel(
    dp,
    states, cotangent, segments, qkv, out_w, up_w, down_w, pre, pack,
    hidden, grads, pgrads, gup, gdown,
    xb, xg, cot, lab_q, lab_k, qw, ow, uw, dw, pw, pk,
    qs, kv, kvs, mg, lse, n1, r1, n2, r2, slopes,
    mid, acc, act, mrecv, fsnd, fin, fout, fret, gfirst, gm, gms, gout,
    keys, turned, vals, dk_acc, dv_acc, dq, dkv, dkv_send, dkv_recv, dxs, dxr, pacc, psib, pacross, psum, pdp,
    send_sem, arrive_sem, here_sem,
):
    core, z, place = lax.axis_index("section"), lax.axis_index("dp"), lax.axis_index("tensor")
    low, high = lax.rem(place, 2), place // 2
    across = place + 1 - 2 * low
    along = lax.rem(place + 2, 4)
    sib_dev = {"section": 1 - core}
    x_dev, y_dev = {"tensor": across}, {"tensor": along}
    diag_dev = {"section": 1 - core, "tensor": across}

    def dp_dev(step):
        return {"dp": z + step - 2 * step * lax.rem(z // step, 2)}

    dp_steps = []
    while (1 << len(dp_steps)) < dp:
        dp_steps.append(1 << len(dp_steps))
    z_dev = dp_dev(1)
    wires = Copies(send_sem, arrive_sem, here_sem)
    pending = []

    barrier = pltpu.get_barrier_semaphore()
    greeted = [sib_dev, x_dev, y_dev, diag_dev] + [dp_dev(s) for s in dp_steps]
    for device in greeted:
        pl.semaphore_signal(barrier, inc=1, device_id=device, device_id_type=MESH)
    pl.semaphore_wait(barrier, len(greeted))

    class Own:
        def __init__(self, layer, src, dst):
            self.layer = layer
            self.here = wires.local(src, dst)
            self.first = wires.remote(src, dst, sib_dev)[0]

        def start(self):
            @pl.when(core == self.layer)
            def _():
                self.here.start()
                self.first.start()

        def need(self):
            @pl.when(core == self.layer)
            def _():
                self.here.wait()

            @pl.when(core != self.layer)
            def _():
                self.first.wait_recv()

        def finish(self):
            @pl.when(core == self.layer)
            def _():
                self.first.wait_send()

    class Away:
        def __init__(self, layer, src, dst):
            self.layer = layer
            self.first = wires.remote(src, dst, sib_dev)[0]

        def start(self):
            @pl.when(core == self.layer)
            def _():
                self.first.start()

        def need(self):
            @pl.when(core != self.layer)
            def _():
                self.first.wait_recv()

        def finish(self):
            @pl.when(core == self.layer)
            def _():
                self.first.wait_send()

    class Direct:
        def __init__(self, layer, src, dst, dev):
            self.layer = layer
            self.over = wires.remote(src, dst, dev)[0]
            self.rest = wires.remote(dst, dst, sib_dev)[0]

        def start(self):
            @pl.when(core == self.layer)
            def _():
                self.over.start()

        def forward(self):
            @pl.when(core == self.layer)
            def _():
                self.over.wait_recv()
                self.rest.start()

        def need(self):
            @pl.when(core != self.layer)
            def _():
                self.rest.wait_recv()

        def finish(self):
            @pl.when(core == self.layer)
            def _():
                self.over.wait_send()
                self.rest.wait_send()

    class Shared:
        def __init__(self, layer, src, dst, mine, theirs, dev):
            self.layer = layer
            self.over = wires.remote(src.at[mine], dst.at[mine], dev)[0]
            self.dp, number = wires.remote(dst.at[mine], dst.at[mine], z_dev)
            self.dp_in = wires.remote(dst.at[theirs], dst.at[theirs], z_dev, number)[0]
            self.rest = wires.remote(dst.at[mine], dst.at[mine], sib_dev)[0]
            self.last = wires.remote(dst.at[theirs], dst.at[theirs], sib_dev)[0]

        def start(self):
            @pl.when(core == self.layer)
            def _():
                self.over.start()

        def forward(self):
            @pl.when(core == self.layer)
            def _():
                self.over.wait_recv()
                self.dp.start()
                self.rest.start()

        def forward_last(self):
            @pl.when(core == self.layer)
            def _():
                self.dp_in.wait_recv()
                self.last.start()

        def need(self):
            @pl.when(core != self.layer)
            def _():
                self.rest.wait_recv()
                self.last.wait_recv()

        def finish(self):
            @pl.when(core == self.layer)
            def _():
                for c in (self.over, self.dp, self.rest, self.last):
                    c.wait_send()

    odd = lax.rem(z, 2)

    def halves(size, pieces):
        places, at = [], 0
        for piece in pieces:
            places.append(
                tuple(pl.ds(pl.multiple_of(parity_z * (size // 2) + at, 16), piece) for parity_z in (odd, 1 - odd))
            )
            at += piece
        return places

    class Layer:
        def __init__(self, layer):
            self.heads_own = Own(layer, qkv, qw.at[layer, 0])
            self.small_own = [Own(layer, pre, pw.at[layer, 0]), Own(layer, pack, pk.at[layer, 0])]
            self.out_own = Own(layer, out_w, ow.at[layer, 0])
            self.units_own = [Away(layer, up_w, gup.at[layer, 0]), Away(layer, down_w, gdown.at[layer, 0])]
            if layer == 0:
                (mine, theirs), = halves(D, [D // 2])
                self.heads = [
                    Shared(layer, qkv.at[i], qw.at[layer, 1, i], mine, theirs, x_dev) for i in range(3)
                ]
            else:
                self.heads = [Direct(layer, qkv, qw.at[layer, 1], x_dev)]
            self.small = [Direct(layer, pre, pw.at[layer, 1], x_dev), Direct(layer, pack, pk.at[layer, 1], y_dev)]
            self.out_x = Direct(layer, out_w, ow.at[layer, 1], x_dev)
            (mine, theirs), = halves(QUARTER, [QUARTER // 2])
            self.out_y = [
                Shared(layer, out_w, ow.at[layer, 2], mine, theirs, y_dev),
                Shared(layer, ow.at[layer, 1], ow.at[layer, 3], mine, theirs, y_dev),
            ]
            self.units = [
                Shared(layer, src, dst.at[layer, 1], mine, theirs, y_dev)
                for src, dst, pieces in ((up_w, gup, [256, 256]), (down_w, gdown, [256, 128, 128]))
                for mine, theirs in halves(UNITS, pieces)
            ]

        def everything(self):
            return (
                [self.heads_own, self.out_own, self.out_x] + self.small_own + self.units_own + self.heads + self.small
                + self.out_y + self.units
            )

    layers = [Layer(0), Layer(1)]

    def each(items, action):
        for item in items:
            getattr(item, action)()

    loads = {}

    def load(layer, slot, array, when):
        spread, native, dst = ((gup, up_w, uw), (gdown, down_w, dw))[array]
        copy = wires.local(spread.at[layer, slot], dst.at[slot])
        loads[layer, slot, array, when] = copy
        if slot == 0:
            mine = wires.local(native, dst.at[0], wires.locals - 1)

            @pl.when(core == layer)
            def _():
                mine.start()

            @pl.when(core != layer)
            def _():
                copy.start()
        else:
            copy.start()

    def loaded(layer, slot, array, when):
        loads[layer, slot, array, when].wait()

    def chunk_rows(step):
        return pl.ds(step * CHUNK, CHUNK)

    class Tokens:
        def __init__(self, source, dest):
            self.near = [wires.local(source.at[low, chunk_rows(i)], dest.at[chunk_rows(i)]) for i in range(STEPS)]
            self.far = [
                wires.remote(source.at[1 - low, chunk_rows(i)], dest.at[chunk_rows(i)], x_dev)[0] for i in range(STEPS)
            ]

        def start(self):
            @pl.when(core == 0)
            def _():
                for c in self.near:
                    c.start()

            @pl.when(core == 1)
            def _():
                for c in self.far:
                    c.start()

        def wait(self, step):
            @pl.when(core == 0)
            def _():
                self.near[step].wait()

            @pl.when(core == 1)
            def _():
                self.far[step].wait_recv()

        def finish(self):
            @pl.when(core == 1)
            def _():
                for c in self.far:
                    c.wait_send()

    tokens = Tokens(states, xb.at[0])
    ends = Tokens(cotangent, cot)

    first = layers[0]
    tokens.start()
    each([first.heads_own] + first.small_own, "start")
    each(first.heads + first.small, "start")
    each([first.out_own] + first.units_own, "start")

    def send_chunk(src, dst, device):
        copy, _ = wires.remote(src, dst, device)
        copy.start()
        return copy

    gathers = {}

    def gather_x(layer, step):
        gathers[layer, step] = send_chunk(
            xb.at[layer, chunk_rows(step)], xg.at[chunk_rows(step)], y_dev
        )

    for step in range(STEPS):
        tokens.wait(step)
        gather_x(0, step)

    each(first.units[:2], "start")

    parity = low + core - 2 * low * core
    row = segments[pl.ds(low, 1), :]
    last = row[:, LEN - 1 :]

    def block_labels(block):
        ids = last - segments[pl.ds(low, 1), pl.ds(pl.multiple_of(block * ROWS, ROWS), ROWS)]
        numbers = lax.broadcasted_iota(jnp.int32, (LABELS, ROWS), 0)
        same = jnp.where(numbers == ids, 1.0, 0.0)
        return same.T, jnp.where(numbers <= 2 * SPAN, HIDDEN * (1.0 - same), 0.0).T

    for index, (h, p) in enumerate(((high, parity), (1 - high, parity), (high, 1 - parity), (1 - high, 1 - parity))):
        same, differ = block_labels(2 * h + p)
        if index < 2:
            lab_q[pl.ds(index * ROWS, ROWS), :] = same.astype(BF16)
        lab_k[pl.ds(index * ROWS, ROWS), :] = differ.astype(BF16)

    def project(layer, source, start, size, slots=(0, 1)):
        for slot in slots:
            columns = slice(slot * QUARTER, (slot + 1) * QUARTER)
            rows = pl.ds(start, size)
            qs[layer, rows, columns] = dot(source, qw[layer, slot, 0]).astype(BF16)
            kv[layer, rows, columns] = dot(source, qw[layer, slot, 1]).astype(BF16)
            kv[layer, rows, slice(CORE + columns.start, CORE + columns.stop)] = dot(
                source, qw[layer, slot, 2]
            ).astype(BF16)

    def lanes(index, base=0):
        return slice(base + index * PAIR, base + (index + 1) * PAIR)

    def fill_keys(layer):
        for p in range(PAIRS):
            keys[p, :CORE, :PAIR] = kv[layer, :, lanes(p)]
            keys[p, CORE : 2 * CORE, :PAIR] = kvs[layer, :, lanes(p)]
            keys[p, 2 * CORE :, :PAIR] = pw[layer, p // 2, 0, :, lanes(p % 2)]

    def pair_values(layer, p):
        return kv[layer, :, lanes(p, CORE)], kvs[layer, :, lanes(p, CORE)], pw[layer, p // 2, 1, :, lanes(p % 2)]

    def fill_turned(p, own, sib, prefix):
        turned[p, :, :CORE] = own.T
        turned[p, :, CORE : 2 * CORE] = sib.T
        turned[p, :, 2 * CORE :] = prefix.T

    def fill_forward(layer):
        fill_keys(layer)
        for p in range(PAIRS):
            fill_turned(p, *pair_values(layer, p))

    def fill_backward(layer):
        if layer == 0:
            fill_keys(layer)
        for p in range(PAIRS):
            own, sib, prefix = pair_values(layer, p)
            vals[p, :CORE, :] = own
            vals[p, CORE : 2 * CORE, :] = sib
            vals[p, 2 * CORE :, :] = prefix
            fill_turned(p, keys[p, :CORE, :PAIR], keys[p, CORE : 2 * CORE, :PAIR], keys[p, 2 * CORE :, :PAIR])

    for p in range(PAIRS):
        keys[p, : 2 * CORE, PAIR:] = lab_k[...]
        keys[p, 2 * CORE :, PAIR:] = jnp.zeros((PREFIX, LABELS), BF16)

    def both_heads(values):
        return jnp.concatenate([jnp.where(head_lanes(CHUNK, h), values, 0) for h in range(2)], 0)

    def score_chunk(layer, start, p):
        rows = pl.ds(start, CHUNK)
        queries = both_heads(qs[layer, rows, lanes(p)] * 0.125)
        label = lab_q[rows, :]
        return queries, dot_t(keys[p], jnp.concatenate([queries, jnp.concatenate([label, label], 0)], 1))

    def untangle(both):
        return jnp.concatenate([both[:HEAD, :CHUNK], both[HEAD:, CHUNK:]], 0).T

    def attend_chunks(layer, steps):
        blocks = [(p, start, action if p + 1 == PAIRS else None) for start, action in steps for p in range(PAIRS)]
        ahead = score_chunk(layer, blocks[0][1], 0)
        for index, (p, start, action) in enumerate(blocks):
            rows, at = pl.ds(start, CHUNK), start // CHUNK
            _, scores = ahead
            if index + 1 < len(blocks):
                ahead = score_chunk(layer, blocks[index + 1][1], blocks[index + 1][0])
            peak = jnp.max(scores, axis=0, keepdims=True)
            weights = jnp.exp(scores - peak)
            total = jnp.sum(weights, axis=0, keepdims=True)
            merged = dot(turned[p], weights.astype(BF16)) * (1.0 / total)
            lse[layer, p, at : at + 1, :] = peak + jnp.log(total)
            mg[layer, rows, lanes(p)] = untangle(merged).astype(BF16)
            if action is not None:
                action()

    def attend_chunks_back(layer, starts, fresh, done=None):
        def begin(p, start):
            rows = pl.ds(start, CHUNK)
            queries, scores = score_chunk(layer, start, p)
            grad_both = both_heads(gm[rows, lanes(p)])
            return queries, scores, grad_both, dot_t(vals[p], grad_both)

        blocks = [(p, start) for p in range(PAIRS) for start in starts]
        ahead = begin(*blocks[0])
        kept = []
        for index, (p, start) in enumerate(blocks):
            rows, at = pl.ds(start, CHUNK), start // CHUNK
            queries, scores, grad_both, grad_weights = ahead
            if index + 1 < len(blocks):
                ahead = begin(*blocks[index + 1])
            product = (gm[rows, lanes(p)].astype(F32) * mg[layer, rows, lanes(p)].astype(F32)).T
            delta = jnp.concatenate(
                [jnp.sum(product[h * HEAD : (h + 1) * HEAD], axis=0, keepdims=True) for h in range(2)], 1
            )
            weights = jnp.exp(scores - lse[layer, p, at : at + 1, :])
            grad_scores = (weights * (grad_weights - delta)).astype(BF16)
            dq[rows, lanes(p)] = (untangle(dot(turned[p], grad_scores)) * 0.125).astype(BF16)
            kept.append((weights.astype(BF16), grad_both, grad_scores, queries))
            if len(kept) == len(starts):
                joined = [jnp.concatenate([k[i] for k in kept], 1 - i % 2) for i in range(4)]
                dv_part, dk_part = dot(joined[0], joined[1]), dot(joined[2], joined[3])
                if fresh:
                    dv_acc[:, lanes(p)] = dv_part
                    dk_acc[:, lanes(p)] = dk_part
                else:
                    dv_acc[:, lanes(p)] += dv_part
                    dk_acc[:, lanes(p)] += dk_part
                kept = []
                if done is not None:
                    done(p)

    def vector(layer, index):
        return pk[layer, 0, index : index + 1, :]

    def keep_norm(store, scales, layer, rows, normed, scale):
        store[layer, rows, :] = normed.astype(BF16)
        scales[layer, rows, :] = jnp.broadcast_to(scale, (CHUNK, PAIR))

    def forward_attention(layer):
        this, later = layers[layer], layers[1]
        if layer == 0:
            this.heads_own.need()
            project(0, xb[0], 0, ROWS, (0,))
            each(this.heads + this.small, "forward")
            this.out_x.start()
            this.out_y[0].start()
            for step in range(STEPS):
                gathers[0, step].wait_recv()
                project(0, xg[chunk_rows(step), :], ROWS + step * CHUNK, CHUNK, (0,))
            each(this.units[:2], "forward")
            this.out_x.forward()
            this.out_y[1].start()
            each(later.heads + later.small + [later.out_x], "start")
            each(this.units[2:], "start")
            each(this.heads, "forward_last")
            each(this.heads + this.small_own + this.small, "need")
            project(0, xb[0], 0, ROWS, (1,))
            sent = [send_chunk(kv.at[0, :ROWS], kvs.at[0, :ROWS], sib_dev)]
            project(0, xg[...], ROWS, ROWS, (1,))
            sent.append(send_chunk(kv.at[0, ROWS:], kvs.at[0, ROWS:], sib_dev))
        else:
            each([this.heads_own] + this.heads + this.small_own + this.small, "need")
            project(1, xb[1], 0, ROWS)
            sent = [send_chunk(kv.at[1, :ROWS], kvs.at[1, :ROWS], sib_dev)]
            for step in range(STEPS):
                gathers[1, step].wait_recv()
                project(1, xg[chunk_rows(step), :], ROWS + step * CHUNK, CHUNK)
            sent.append(send_chunk(kv.at[1, ROWS:], kvs.at[1, ROWS:], sib_dev))
        for c in sent:
            c.wait_recv()
        fill_forward(layer)
        swaps, copies = [], []

        def swap(step):
            rows = pl.ds(ROWS + step * CHUNK, CHUNK)
            swaps.append(send_chunk(mg.at[layer, rows], mrecv.at[chunk_rows(step)], y_dev))

        def finish(step):
            swaps[step].wait_recv()
            rows = chunk_rows(step)
            parts = [mg[layer, rows, :QUARTER], mg[layer, rows, QUARTER:], mrecv[rows, :QUARTER], mrecv[rows, QUARTER:]]
            total = xb[layer, rows, :].astype(F32) + vector(layer, 3)
            for i, part in enumerate(parts):
                total = total + dot(part, ow[layer, i])
            normed, scale = norm_chunk(total)
            keep_norm(n1, r1, layer, rows, normed, scale)
            middle = normed * vector(layer, 1) + vector(layer, 4)
            mid[rows, :] = middle
            fsnd[rows, :] = middle.astype(BF16)
            copies.append(send_chunk(fsnd.at[rows], fin.at[rows], x_dev))

        def first_peer():
            swap(0)
            if layer == 0:
                each(this.out_y, "forward")
            else:
                ends.start()

        def first_own():
            if layer == 0:
                each(this.units[2:], "forward")

        def second_peer():
            swap(1)
            each(this.out_y, "forward_last")
            each([this.out_own, this.out_x] + this.out_y, "need")
            finish(0)

        def second_own():
            finish(1)
            if layer == 0:
                each(later.units[:2], "start")

        attend_chunks(
            layer, [(ROWS, first_peer), (0, first_own), (ROWS + CHUNK, second_peer), (CHUNK, second_own)]
        )
        each(this.units_own, "need")
        load(layer, 0, 0, 0)
        load(layer, 0, 1, 0)
        for c in sent + swaps:
            c.wait_send()

        def gathered():
            for step in range(STEPS):
                gathers[layer, step].wait_send()

        gathered()
        return copies

    def feed_rows(layer, slot, source, start, store):
        size = source.shape[0]

        def up_tile(j, _):
            columns = pl.ds(pl.multiple_of(j * TILE, TILE), TILE)
            wide = pl.ds(pl.multiple_of(slot * UNITS + j * TILE, TILE), TILE)
            u = dot(source[...], uw[slot, :, columns]) + pk[layer, slot, 0:1, columns]
            store[:, columns], slopes[layer, pl.ds(start, size), wide] = gelu_both(u)
            return 0

        lax.fori_loop(0, UNITS // TILE, up_tile, 0)

    def feed_rows_back(layer, source, start, size):
        def tile(j, _):
            slot, units_at = j // 4, pl.ds(pl.multiple_of(lax.rem(j, 4) * TILE, TILE), TILE)
            wide = pl.ds(pl.multiple_of(j * TILE, TILE), TILE)
            u = dot_t(source[...], dw[slot, units_at, :]) * slopes[layer, pl.ds(start, size), wide].astype(F32)
            act[:size, wide] = u.astype(BF16)
            return 0

        lax.fori_loop(0, 2 * UNITS // TILE, tile, 0)

    def feed_out(store, acts, back):
        def tile(j, _):
            columns = pl.ds(pl.multiple_of(j * TILE, TILE), TILE)
            if back:
                u = dot_t(acts[0][...], uw[0, columns, :]) + dot_t(acts[1][...], uw[1, columns, :])
            else:
                u = dot(acts[0][...], dw[0, :, columns]) + dot(acts[1][...], dw[1, :, columns])
            store[:, columns] = u.astype(store.dtype)
            return 0

        lax.fori_loop(0, D // TILE, tile, 0)

    def act_slots(size):
        return [act.at[pl.ds(0, size), pl.ds(slot * UNITS, UNITS)] for slot in range(2)]

    def feed_forward(layer, copies, finish, arrivals):
        this = layers[layer]
        mine = act_slots(ROWS)
        theirs = [[dkv.at[pl.ds(slot * ROWS + step * CHUNK, CHUNK)] for slot in range(2)] for step in range(STEPS)]

        def feed_peer(slot, step):
            feed_rows(layer, slot, fin.at[chunk_rows(step)], ROWS + step * CHUNK, theirs[step][slot])

        loaded(layer, 0, 0, 0)
        feed_rows(layer, 0, fsnd, 0, mine[0])
        for step in range(STEPS):
            copies[step].wait_recv()
            feed_peer(0, step)
            arrivals[step]()
        each(this.units[:2], "forward_last")
        each(this.units[:2], "need")
        load(layer, 1, 0, 0)
        loaded(layer, 1, 0, 0)
        for step in range(STEPS):
            feed_peer(1, step)
        each(this.units[2:], "forward_last")
        each(this.units[2:], "need")
        load(layer, 1, 1, 0)
        loaded(layer, 0, 1, 0)
        loaded(layer, 1, 1, 0)
        returned = []
        for step in range(STEPS):
            rows = chunk_rows(step)
            feed_out(fout.at[rows], theirs[step], False)
            returned.append(send_chunk(fout.at[rows], fret.at[rows], x_dev))
        feed_rows(layer, 1, fsnd, 0, mine[1])
        feed_out(acc, mine, False)
        arrivals[STEPS]()
        for c in copies:
            c.wait_send()
        for step in range(STEPS):
            returned[step].wait_recv()
            finish(step, chunk_rows(step), acc[chunk_rows(step), :] + fret[chunk_rows(step), :].astype(F32))
        for c in returned:
            c.wait_send()

    def feed_back(layer, copies, finish, between):
        feed_rows_back(layer, fsnd, 0, ROWS)
        feed_out(acc, act_slots(ROWS), True)
        returned = []
        per = len(copies) // STEPS
        for step in range(STEPS):
            rows = chunk_rows(step)
            for c in copies[step * per : (step + 1) * per]:
                c.wait_recv()
            feed_rows_back(layer, fin.at[rows], ROWS + step * CHUNK, CHUNK)
            feed_out(fout.at[rows], act_slots(CHUNK), True)
            returned.append(send_chunk(fout.at[rows], fret.at[rows], x_dev))
        between()
        for step in range(STEPS):
            returned[step].wait_recv()
            finish(step, chunk_rows(step), acc[chunk_rows(step), :] + fret[chunk_rows(step), :].astype(F32))
        for c in copies + returned:
            c.wait_send()

    deliveries = []
    later_deliveries = []

    def deliver(layer, source, dest, rows, now=False):
        far, number = wires.remote(source.at[rows], dest.at[low, rows], {"section": layer, "tensor": across})
        far_in, _ = wires.remote(source.at[rows], dest.at[1 - low, rows], {"section": layer, "tensor": across}, number)
        if layer == 0:
            near = wires.local(source.at[rows], dest.at[low, rows])
        else:
            near, _ = wires.remote(source.at[rows], dest.at[low, rows], sib_dev)

        def start():
            @pl.when(core == 0)
            def _():
                near.start()

            @pl.when(core == 1)
            def _():
                far.start()

        if now:
            start()
        else:
            later_deliveries.append(start)

        def sent():
            @pl.when(core == 0)
            def _():
                near.wait() if layer == 0 else near.wait_send()

            @pl.when(core == 1)
            def _():
                far.wait_send()

        def arrived():
            @pl.when(core == layer)
            def _():
                far_in.wait_recv()
                if layer == 1:
                    near.wait_recv()

        deliveries.append(arrived)
        return sent

    def start_back(layer, rows, grad):
        normed, scale = n2[layer, rows, :].astype(F32), r2[layer, rows, :1]
        value = norm_back(grad, vector(layer, 2), normed, scale)
        mid[rows, :] = value
        fsnd[rows, :] = value.astype(BF16)
        return send_chunk(fsnd.at[rows], fin.at[rows], x_dev)

    unsent = []
    back_copies = []

    def forward_finish(layer):
        def finish(step, rows, branch):
            normed, scale = norm_chunk(mid[rows, :] + branch + vector(layer, 5))
            keep_norm(n2, r2, layer, rows, normed, scale)
            xb[layer + 1, rows, :] = (normed * vector(layer, 2) + vector(layer, 6)).astype(BF16)
            if layer == 0:
                gather_x(1, step)
            unsent.append(deliver(layer, xb.at[layer + 1], hidden, rows))
            if layer == 1:
                ends.wait(step)
                back_copies.append(start_back(1, rows, cot[rows, :].astype(F32)))

        return finish

    second = layers[1]

    def first_arrivals():
        each(second.heads + second.small, "forward")
        second.out_x.forward()
        each(second.units[2:], "start")
        each(second.out_y, "start")

    def later_arrivals():
        each([second.heads_own] + second.small_own + [second.out_own] + second.units_own, "start")
        each(second.units[:2], "forward")

    def after_units():
        each(second.out_y, "forward")
        each(second.units[2:], "forward")

    copies = forward_attention(0)
    feed_forward(0, copies, forward_finish(0), [first_arrivals, later_arrivals, after_units])
    copies = forward_attention(1)
    feed_forward(1, copies, forward_finish(1), [lambda: None] * 3)

    grad_sent = []

    def backward(layer, copies):
        swaps = []

        def finish(step, rows, term):
            middle = mid[rows, :] + term
            first = norm_back(middle, vector(layer, 1), n1[layer, rows, :].astype(F32), r1[layer, rows, :1])
            gfirst[rows, :] = first
            low_first = first.astype(BF16)
            for i in range(4):
                part = dot_t(low_first, ow[layer, i]).astype(BF16)
                columns = slice((i % 2) * QUARTER, (i % 2 + 1) * QUARTER)
                if i < 2:
                    gm[rows, columns] = part
                else:
                    gms[rows, columns] = part
            swaps.append(send_chunk(gms.at[rows], gm.at[pl.ds(ROWS + step * CHUNK, CHUNK)], y_dev))

            attend_chunks_back(layer, [step * CHUNK], step == 0)

        def between():
            if layer == 1:
                for slot in range(2):
                    for array in range(2):
                        load(0, slot, array, 1)
            fill_backward(layer)

        feed_back(layer, copies, finish, between)
        for d in later_deliveries:
            d()
        later_deliveries.clear()
        for c in swaps:
            c.wait_recv()
        given = []

        def give(p):
            dkv_send[p, 0] = dk_acc[CORE : 2 * CORE, lanes(p)].astype(BF16)
            dkv_send[p, 1] = dv_acc[CORE : 2 * CORE, lanes(p)].astype(BF16)
            given.append(send_chunk(dkv_send.at[p], dkv_recv.at[layer, p], sib_dev))

        attend_chunks_back(layer, [ROWS, ROWS + CHUNK], False, give)
        pacc[layer, 0] = dk_acc[2 * CORE :, :]
        pacc[layer, 1] = dv_acc[2 * CORE :, :]
        if layer == 0:
            total = prefix_start()
        for p in range(PAIRS):
            given[p].wait_recv()
            dkv[:, lanes(p)] = (dk_acc[:CORE, lanes(p)] + dkv_recv[layer, p, 0].astype(F32)).astype(BF16)
            dkv[:, lanes(p, CORE)] = (dv_acc[:CORE, lanes(p)] + dkv_recv[layer, p, 1].astype(F32)).astype(BF16)

        def input_term(store, start, size):
            rows = pl.ds(start, size)

            def tile(j, _):
                features = pl.ds(pl.multiple_of(j * TILE, TILE), TILE)
                total = None
                for slot in range(2):
                    columns = slice(slot * QUARTER, (slot + 1) * QUARTER)
                    shifted = slice(CORE + slot * QUARTER, CORE + (slot + 1) * QUARTER)
                    for part, source in enumerate((dq[rows, columns], dkv[rows, columns], dkv[rows, shifted])):
                        term = dot_t(source, qw[layer, slot, part, features, :])
                        total = term if total is None else total + term
                store[:, features] = total.astype(store.dtype)
                return 0

            lax.fori_loop(0, D // TILE, tile, 0)

        returned = []
        for step in range(STEPS):
            input_term(dxs.at[chunk_rows(step)], ROWS + step * CHUNK, CHUNK)
            for part in range(CHUNK // PART):
                rows = pl.ds(step * CHUNK + part * PART, PART)
                returned.append(send_chunk(dxs.at[rows], dxr.at[rows], y_dev))
        if layer == 0:
            total.stage()
        input_term(acc, 0, ROWS)
        if layer == 1:
            for slot in range(2):
                for array in range(2):
                    loaded(0, slot, array, 1)
        else:
            total.stage()
        for sent in grad_sent:
            sent()
        grad_sent.clear()
        onward = []
        for step in range(ROWS // PART):
            rows = pl.ds(step * PART, PART)
            returned[step].wait_recv()
            value = gfirst[rows, :] + (acc[rows, :] + dxr[rows, :].astype(F32))
            gout[rows, :] = value
            grad_sent.append(deliver(layer, gout, grads, rows, layer == 0))
            if layer == 1:
                onward.append(start_back(0, rows, value.astype(BF16).astype(F32)))
            else:
                total.stage()
        for c in swaps + given + returned:
            c.wait_send()
        return onward

    class prefix_start:
        def __init__(self):
            self.sib = send_chunk(pacc.at[1 - core], psib, sib_dev)
            self.sent = [self.sib]
            self.at = 0

        def stage(self):
            if self.at > len(dp_steps) + 1:
                return
            if self.at == 0:
                self.sib.wait_recv()
                total = pacc[core] + psib[...]
                psum[0] = total[:, :, :QUARTER]
                pacross[0] = total[:, :, QUARTER:]
                self.next = send_chunk(pacross.at[0], pacross.at[1], x_dev)
                self.sent.append(self.next)
            else:
                self.next.wait_recv()
                arrived = pacross[1] if self.at == 1 else pdp[self.at - 2]
                psum[self.at] = psum[self.at - 1] + arrived
                if self.at <= len(dp_steps):
                    step = self.at - 1
                    self.next = send_chunk(psum.at[self.at], pdp.at[step], dp_dev(dp_steps[step]))
                    self.sent.append(self.next)
                else:
                    self.done = wires.local(psum.at[self.at], pgrads)
                    self.done.start()
            self.at += 1

        def finish(self):
            while self.at <= len(dp_steps) + 1:
                self.stage()
            for c in self.sent:
                c.wait_send()
            self.done.wait()

    holder = []
    start_class = prefix_start

    def prefix_start():
        holder.append(start_class())
        return holder[0]

    back_copies = backward(1, back_copies)
    backward(0, back_copies)
    holder[0].finish()
    for sent in unsent + grad_sent:
        sent()
    for arrived in deliveries:
        arrived()
    tokens.finish()
    ends.finish()
    for layer in layers:
        each(layer.everything(), "finish")


def fused(dp, states, cotangent, segments, qkv, out_w, up_w, down_w, pre, pack):
    shape = jax.ShapeDtypeStruct
    steps = dp.bit_length() - 1
    vmem = pltpu.VMEM
    scratch = [
        vmem((3, ROWS, D), BF16),
        vmem((ROWS, D), BF16),
        vmem((ROWS, D), BF16),
        vmem((CORE, LABELS), BF16), vmem((2 * CORE, LABELS), BF16),
        vmem((2, 2, 3, D, QUARTER), BF16),
        vmem((2, 4, QUARTER, D), BF16),
        vmem((2, D, UNITS), BF16), vmem((2, UNITS, D), BF16),
        vmem((2, 2, 2, PREFIX, QUARTER), BF16),
        vmem((2, 2, 8, D), F32),
        vmem((2, CORE, CORE), BF16), vmem((2, CORE, 2 * CORE), BF16), vmem((2, CORE, 2 * CORE), BF16),
        vmem((2, CORE, CORE), BF16), vmem((2, PAIRS, 8, 2 * CHUNK), F32),
        vmem((2, ROWS, D), BF16), vmem((2, ROWS, PAIR), F32),
        vmem((2, ROWS, D), BF16), vmem((2, ROWS, PAIR), F32),
        vmem((2, CORE, 2 * UNITS), BF16),
        vmem((ROWS, D), F32), vmem((ROWS, D), F32), vmem((ROWS, 2 * UNITS), BF16),
        vmem((ROWS, CORE), BF16),
        vmem((ROWS, D), BF16), vmem((ROWS, D), BF16), vmem((ROWS, D), BF16), vmem((ROWS, D), BF16),
        vmem((ROWS, D), F32),
        vmem((CORE, CORE), BF16), vmem((ROWS, CORE), BF16), vmem((ROWS, D), F32),
        vmem((PAIRS, KEYS, PAIR + LABELS), BF16), vmem((PAIRS, PAIR, KEYS), BF16), vmem((PAIRS, KEYS, PAIR), BF16),
        vmem((KEYS, CORE), F32), vmem((KEYS, CORE), F32),
        vmem((CORE, CORE), BF16), vmem((CORE, 2 * CORE), BF16), vmem((PAIRS, 2, CORE, PAIR), BF16),
        vmem((2, PAIRS, 2, CORE, PAIR), BF16),
        vmem((ROWS, D), BF16), vmem((ROWS, D), BF16),
        vmem((2, 2, PREFIX, CORE), F32), vmem((2, PREFIX, CORE), F32),
        vmem((2, 2, PREFIX, QUARTER), F32), vmem((steps + 2, 2, PREFIX, QUARTER), F32),
        vmem((max(steps, 1), 2, PREFIX, QUARTER), F32),
        pltpu.SemaphoreType.DMA((SEMS,)), pltpu.SemaphoreType.DMA((SEMS,)), pltpu.SemaphoreType.DMA((SEMS,)),
    ]
    anywhere = pl.BlockSpec(memory_space=pl.ANY)
    result = pl.pallas_call(
        functools.partial(fused_kernel, dp),
        out_shape=[
            shape((2, ROWS, D), BF16), shape((2, ROWS, D), F32), shape((2, PREFIX, QUARTER), F32),
            shape((2, 2, D, UNITS), BF16), shape((2, 2, UNITS, D), BF16),
        ],
        in_specs=[anywhere, anywhere, pl.BlockSpec(memory_space=pltpu.VMEM)] + [anywhere] * 6,
        out_specs=[anywhere] * 5,
        scratch_shapes=scratch,
        compiler_params=pltpu.CompilerParams(
            collective_id=0, has_side_effects=True, vmem_limit_bytes=63 << 20
        ),
        name="layers",
    )(states, cotangent, segments, qkv, out_w, up_w, down_w, pre, pack)
    return result[:3]


class Links:
    def __init__(self):
        self.core = lax.axis_index("section")
        self.place = lax.axis_index("tensor")
        self.size = lax.axis_size("tensor")
        self.low = self.place % 2
        self.high = self.place // 2
        self.group = self.size // 2

    def sibling(self, a, only=None):
        pairs = [(0, 1), (1, 0)] if only is None else [(only, 1 - only)]
        return lax.ppermute(a, "section", pairs)

    def across(self, a, only=None):
        if only is None:
            return lax.ppermute(a, "tensor", [(t, t ^ 1) for t in range(self.size)])
        pairs = [(only * self.size + t, only * self.size + (t ^ 1)) for t in range(self.size)]
        return lax.ppermute(a, ("section", "tensor"), pairs)

    def diagonal(self, a, source):
        pairs = [(source * self.size + t, (1 - source) * self.size + (t ^ 1)) for t in range(self.size)]
        return lax.ppermute(a, ("section", "tensor"), pairs)

    def from_ahead(self, a, by):
        g = self.group
        pairs = [(2 * ((h + by) % g) + p, 2 * h + p) for h in range(g) for p in range(2)]
        return lax.ppermute(a, "tensor", pairs)

    def gather(self, a):
        return [a] + [self.from_ahead(a, k) for k in range(1, self.group)]

    def scatter_sum(self, part_fn):
        arrived = [self.from_ahead(part_fn(k).astype(BF16), self.group - k) for k in range(1, self.group)]
        total = part_fn(0)
        for a in arrived:
            total = total + a.astype(F32)
        return total


def forward(links, x, weights, pre, labels):
    qkv_w, out_w, up_w, up_b, down_w, gains, shifts = weights
    width = out_w.shape[0]
    blocks = [dot(b, qkv_w).astype(BF16) for b in links.gather(x)]
    qkv = jnp.concatenate(blocks, 0)
    kv_sib = links.sibling(qkv[:, width:])
    merged, lse = attend(qkv, kv_sib, pre, labels)
    rows = x.shape[0]
    attended = links.scatter_sum(lambda k: dot(merged[k * rows : (k + 1) * rows], out_w)) + shifts[0]
    normed_first, scale_first = norm_stats(x.astype(F32) + attended)
    middle = normed_first * gains[0] + shifts[1]
    blocks = links.gather(middle.astype(BF16))
    pairs = [gelu_pair(dot(b, up_w) + up_b) for b in blocks]
    branch = links.scatter_sum(lambda k: dot(pairs[k][0], down_w)) + shifts[2]
    normed_last, scale_last = norm_stats(middle + branch)
    result = (normed_last * gains[1] + shifts[3]).astype(BF16)
    slopes = [p[1] for p in pairs]
    return result, (qkv, kv_sib, merged, lse, normed_first, scale_first, slopes, normed_last, scale_last)


def backward(links, grad, weights, pre, labels, kept):
    qkv_w, out_w, up_w, up_b, down_w, gains, shifts = weights
    qkv, kv_sib, merged, lse, normed_first, scale_first, slopes, normed_last, scale_last = kept
    rows = grad.shape[0]
    grad_second = norm_back(grad.astype(F32), gains[1], normed_last, scale_last)
    blocks = links.gather(grad_second.astype(BF16))
    hiddens = [
        (dot_t(b, down_w) * s.astype(F32)).astype(BF16) for b, s in zip(blocks, slopes, strict=True)
    ]
    grad_middle = grad_second + links.scatter_sum(lambda k: dot_t(hiddens[k], up_w))
    grad_first = norm_back(grad_middle, gains[0], normed_first, scale_first)
    blocks = links.gather(grad_first.astype(BF16))
    grad_merged = jnp.concatenate([dot_t(b, out_w).astype(BF16) for b in blocks], 0)
    dq, dko, dvo, dks, dvs, dkp, dvp = attend_back(qkv, kv_sib, pre, labels, merged, lse, grad_merged)
    arrived = links.sibling(jnp.concatenate([dks, dvs], 1)).astype(F32)
    width = out_w.shape[0]
    dk = (dko + arrived[:, :width]).astype(BF16)
    dv = (dvo + arrived[:, width:]).astype(BF16)
    dqkv = jnp.concatenate([dq, dk, dv], 1)
    grad_inputs = grad_first + links.scatter_sum(
        lambda k: dot_t(dqkv[k * rows : (k + 1) * rows], qkv_w)
    )
    return grad_inputs, jnp.stack([dkp, dvp])


def spread_weights(links, arrays):
    first = links.core == 0
    layers = ([], [])
    for layer in range(2):
        for a in arrays:
            other = links.across(a, layer)
            sib_a, sib_other = links.sibling(a, layer), links.sibling(other, layer)
            here = links.core == layer
            layers[layer].append((jnp.where(here, a, sib_a), jnp.where(here, other, sib_other)))
    return layers


def sum_over_dp(a):
    size = lax.axis_size("dp")
    step = 1
    if size & (size - 1):
        return lax.psum(a, "dp")
    while step < size:
        a = a + lax.ppermute(a, "dp", [(i, i ^ step) for i in range(size)])
        step *= 2
    return a


def plain(
    states, segment_ids, cotangent, qkv_weight, out_weight, up_weight, up_bias, down_weight,
    norm_gain, shift_vec, prefix,
):
    links = Links()
    first = links.core == 0
    low = links.low

    def arrange(both):
        mine = lax.dynamic_index_in_dim(both, low, 0, keepdims=False)
        other = lax.dynamic_index_in_dim(both, 1 - low, 0, keepdims=False)
        return jnp.where(first, mine, links.across(other, 1))

    x = arrange(states)
    grad = arrange(cotangent)

    segment = lax.dynamic_index_in_dim(segment_ids, low, 0, keepdims=False)
    classes = (segment[-1] - segment).reshape(links.group, 2, -1)
    classes = jnp.roll(classes, -links.high, 0)
    parity = jnp.where(first, low, 1 - low)
    own = lax.dynamic_index_in_dim(classes, parity, 1, keepdims=False).reshape(-1)
    sib = lax.dynamic_index_in_dim(classes, 1 - parity, 1, keepdims=False).reshape(-1)
    numbers = jnp.arange(LABELS)[None, :]
    label_q = (own[:, None] == numbers).astype(BF16)
    known = numbers <= 2 * SPAN
    label_o = jnp.where(known & (own[:, None] != numbers), HIDDEN, 0.0).astype(BF16)
    label_s = jnp.where(known & (sib[:, None] != numbers), HIDDEN, 0.0).astype(BF16)
    labels = (label_q, label_o, label_s)

    small = jnp.concatenate(
        [norm_gain[0], shift_vec[0]], 0
    )
    small_sib = links.sibling(small)
    layers = spread_weights(
        links,
        [jnp.transpose(qkv_weight[0], (1, 0, 2)), prefix[0], out_weight[0], up_weight[0], up_bias, down_weight[0]],
    )
    weights, prefixes = [], []
    for layer in range(2):
        qkv, pre, out, up, bias, down = layers[layer]
        vectors = jnp.where(links.core == layer, small, small_sib).astype(F32)
        weights.append((
            jnp.concatenate([p[i] for i in range(3) for p in qkv], 1),
            jnp.concatenate(out, 0),
            jnp.concatenate(up, 1),
            jnp.concatenate(bias, 1).astype(F32),
            jnp.concatenate(down, 0),
            vectors[:2],
            vectors[2:],
        ))
        prefixes.append(jnp.concatenate(pre, 2))

    y0, kept0 = forward(links, x, weights[0], prefixes[0], labels)
    y1, kept1 = forward(links, y0, weights[1], prefixes[1], labels)
    g1, p1 = backward(links, grad, weights[1], prefixes[1], labels, kept1)
    g0, p0 = backward(links, g1.astype(BF16), weights[0], prefixes[0], labels, kept0)

    def deliver(first_layer, second_layer, wire, dtype):
        near = jnp.where(first, first_layer.astype(dtype), links.sibling(second_layer.astype(wire), 0).astype(dtype))
        far0 = links.diagonal(first_layer.astype(wire), 1)
        far1 = links.across(second_layer.astype(wire), 1)
        far = jnp.where(first, far0, far1).astype(dtype)
        return jnp.stack([jnp.where(low == 0, near, far), jnp.where(low == 0, far, near)])

    hidden_out = deliver(y0, y1, BF16, BF16)
    input_grads = deliver(g0, g1, BF16, F32)

    total = jnp.where(first, p0, p1) + links.sibling(jnp.where(first, p1, p0))
    quarter = total.shape[-1] // 2
    total = total[..., :quarter] + links.across(total[..., quarter:])
    prefix_grads = sum_over_dp(total)
    return hidden_out[None], input_grads[None], prefix_grads[None]


def whole_kernel(
    states, segment_ids, cotangent, qkv_weight, out_weight, up_weight, up_bias, down_weight,
    norm_gain, shift_vec, prefix,
):
    pack = jnp.concatenate([up_bias, norm_gain[0], shift_vec[0], jnp.zeros_like(up_bias)], 0).astype(F32)
    results = fused(
        lax.axis_size("dp"), states, cotangent, segment_ids, jnp.transpose(qkv_weight[0], (1, 0, 2)),
        out_weight[0], up_weight[0], down_weight[0], prefix[0], pack,
    )
    return tuple(r[None] for r in results)


def fits(mesh):
    dp = mesh.shape["dp"]
    return mesh.shape["tensor"] == 4 and dp > 1 and dp & (dp - 1) == 0


def solution(mesh):
    placed = (
        P(None, ("dp", "tensor"), None),
        P(None, "dp"),
        P(None, ("dp", "tensor"), None),
        P("section", None, None, "tensor"),
        P("section", "tensor", None),
        P("section", None, "tensor"),
        P("section", "tensor"),
        P("section", "tensor", None),
        P("section", None, None),
        P("section", None, None),
        P("section", None, None, "tensor"),
    )
    return jax.shard_map(
        whole_kernel if fits(mesh) else plain,
        mesh=mesh,
        in_specs=placed,
        out_specs=(
            P("section", None, ("dp", "tensor"), None),
            P("section", None, ("dp", "tensor"), None),
            P("section", None, None, "tensor"),
        ),
        check_vma=False,
    )
```

```python
import functools

import jax
import jax.numpy as jnp
from jax import lax
from jax.experimental import pallas as pl
from jax.experimental.pallas import tpu as pltpu
from jax.sharding import PartitionSpec as P

D = 1024
HEAD = 64
PAIR = 2 * HEAD
PREFIX = 64
LEN = 1024
SPAN = LEN // 32
LABELS = 128
HIDDEN = -1e30
F32 = jnp.float32
BF16 = jnp.bfloat16


def dot(a, b):
    return jnp.dot(a, b, preferred_element_type=F32)


def dot_t(a, b):
    return lax.dot_general(a, b, (((1,), (1,)), ((), ())), preferred_element_type=F32)


def head_lanes(rows, head):
    lanes = lax.broadcasted_iota(jnp.int32, (rows, PAIR), 1)
    return (lanes >= head * HEAD) & (lanes < (head + 1) * HEAD)


def fill_keys(keys, own, sib, pre, own_lab, sib_lab):
    rows = own.shape[0]
    keys[:rows, :PAIR] = own[...]
    keys[rows : 2 * rows, :PAIR] = sib[...]
    keys[2 * rows :, :PAIR] = pre[...]
    keys[:rows, PAIR:] = own_lab[...]
    keys[rows : 2 * rows, PAIR:] = sib_lab[...]
    keys[2 * rows :, PAIR:] = jnp.zeros((PREFIX, LABELS), BF16)


def attend_kernel(block, q, ko, vo, ks, vs, kp, vp, lab_q, lab_o, lab_s, out, lse, keys, vals_t):
    rows = q.shape[0]
    fill_keys(keys, ko, ks, kp, lab_o, lab_s)
    vals_t[:, :rows] = vo[...].T
    vals_t[:, rows : 2 * rows] = vs[...].T
    vals_t[:, 2 * rows :] = vp[...].T
    for start in range(0, rows, block):
        part = pl.ds(start, block)
        query = q[part, :] * 0.125
        label = lab_q[part, :]
        results = []
        for head in range(2):
            mine = jnp.where(head_lanes(block, head), query, 0)
            scores = dot_t(keys[...], jnp.concatenate([mine, label], 1))
            peak = jnp.max(scores, axis=0, keepdims=True)
            weights = jnp.exp(scores - peak)
            total = jnp.sum(weights, axis=0, keepdims=True)
            merged = dot(vals_t[head * HEAD : (head + 1) * HEAD, :], weights.astype(BF16))
            results.append(merged / total)
            lse[0, head : head + 1, part] = peak + jnp.log(total)
        out[part, :] = jnp.concatenate(results, 0).T.astype(BF16)


def attend_back_kernel(
    block, q, ko, vo, ks, vs, kp, vp, lab_q, lab_o, lab_s, out, lse, grad,
    dq, dko, dvo, dks, dvs, dkp, dvp, keys, vals, keys_t, dk_sum, dv_sum,
):
    rows = q.shape[0]
    fill_keys(keys, ko, ks, kp, lab_o, lab_s)
    vals[:rows, :] = vo[...]
    vals[rows : 2 * rows, :] = vs[...]
    vals[2 * rows :, :] = vp[...]
    keys_t[:, :rows] = ko[...].T
    keys_t[:, rows : 2 * rows] = ks[...].T
    keys_t[:, 2 * rows :] = kp[...].T
    for start in range(0, rows, block):
        part = pl.ds(start, block)
        query = q[part, :] * 0.125
        label = lab_q[part, :]
        grad_part = grad[part, :]
        product = (grad_part.astype(F32) * out[part, :].astype(F32)).T
        queries, grads, weights_all, scores_all, results = [], [], [], [], []
        for head in range(2):
            span = slice(head * HEAD, (head + 1) * HEAD)
            mine = jnp.where(head_lanes(block, head), query, 0)
            mine_grad = jnp.where(head_lanes(block, head), grad_part, 0)
            scores = dot_t(keys[...], jnp.concatenate([mine, label], 1))
            weights = jnp.exp(scores - lse[0, head : head + 1, part])
            delta = jnp.sum(product[span], axis=0, keepdims=True)
            grad_scores = (weights * (dot_t(vals[...], mine_grad) - delta)).astype(BF16)
            results.append(dot(keys_t[span, :], grad_scores))
            queries.append(mine)
            grads.append(mine_grad)
            weights_all.append(weights.astype(BF16))
            scores_all.append(grad_scores)
        dq[part, :] = (jnp.concatenate(results, 0).T * 0.125).astype(BF16)
        dv_part = dot(jnp.concatenate(weights_all, 1), jnp.concatenate(grads, 0))
        dk_part = dot(jnp.concatenate(scores_all, 1), jnp.concatenate(queries, 0))
        if start == 0:
            dv_sum[...] = dv_part
            dk_sum[...] = dk_part
        else:
            dv_sum[...] += dv_part
            dk_sum[...] += dk_part
    dko[...] = dk_sum[:rows, :]
    dvo[...] = dv_sum[:rows, :]
    dks[...] = dk_sum[rows : 2 * rows, :].astype(BF16)
    dvs[...] = dv_sum[rows : 2 * rows, :].astype(BF16)
    dkp[...] = dk_sum[2 * rows :, :]
    dvp[...] = dv_sum[2 * rows :, :]


def attention_specs(rows, pairs):
    def column(height, offset):
        return pl.BlockSpec((height, PAIR), lambda p: (0, offset + p))

    labels = pl.BlockSpec((rows, LABELS), lambda p: (0, 0))
    ins = [
        column(rows, 0), column(rows, pairs), column(rows, 2 * pairs),
        column(rows, 0), column(rows, pairs),
        column(PREFIX, 0), column(PREFIX, 0),
        labels, labels, labels,
    ]
    return column, ins, pl.BlockSpec((1, 8, rows), lambda p: (p, 0, 0))


def attend(qkv, kv_sib, pre, labels):
    rows, width = qkv.shape[0], qkv.shape[1] // 3
    pairs = width // PAIR
    column, ins, lse_spec = attention_specs(rows, pairs)
    size = 2 * rows + PREFIX
    return pl.pallas_call(
        functools.partial(attend_kernel, min(rows, 256)),
        grid=(pairs,),
        in_specs=ins,
        out_specs=[column(rows, 0), lse_spec],
        out_shape=[
            jax.ShapeDtypeStruct((rows, width), BF16),
            jax.ShapeDtypeStruct((pairs, 8, rows), F32),
        ],
        scratch_shapes=[pltpu.VMEM((size, PAIR + LABELS), BF16), pltpu.VMEM((PAIR, size), BF16)],
        compiler_params=pltpu.CompilerParams(vmem_limit_bytes=40 << 20),
        cost_estimate=pl.CostEstimate(
            flops=2 * 2 * rows * size * width, transcendentals=rows * size * width // HEAD,
            bytes_accessed=16 * rows * width,
        ),
        name="attend",
    )(qkv, qkv, qkv, kv_sib, kv_sib, pre[0], pre[1], *labels)


def attend_back(qkv, kv_sib, pre, labels, merged, lse, grad):
    rows, width = qkv.shape[0], qkv.shape[1] // 3
    pairs = width // PAIR
    column, ins, lse_spec = attention_specs(rows, pairs)
    size = 2 * rows + PREFIX
    shape = jax.ShapeDtypeStruct
    return pl.pallas_call(
        functools.partial(attend_back_kernel, min(rows, 256)),
        grid=(pairs,),
        in_specs=ins + [column(rows, 0), lse_spec, column(rows, 0)],
        out_specs=[column(rows, 0)] * 5 + [column(PREFIX, 0)] * 2,
        out_shape=[
            shape((rows, width), BF16),
            shape((rows, width), F32), shape((rows, width), F32),
            shape((rows, width), BF16), shape((rows, width), BF16),
            shape((PREFIX, width), F32), shape((PREFIX, width), F32),
        ],
        scratch_shapes=[
            pltpu.VMEM((size, PAIR + LABELS), BF16), pltpu.VMEM((size, PAIR), BF16),
            pltpu.VMEM((PAIR, size), BF16), pltpu.VMEM((size, PAIR), F32), pltpu.VMEM((size, PAIR), F32),
        ],
        compiler_params=pltpu.CompilerParams(vmem_limit_bytes=40 << 20),
        cost_estimate=pl.CostEstimate(
            flops=5 * 2 * rows * size * width, transcendentals=rows * size * width // HEAD,
            bytes_accessed=32 * rows * width,
        ),
        name="attend_back",
    )(qkv, qkv, qkv, kv_sib, kv_sib, pre[0], pre[1], *labels, merged, lse, grad)


def norm_stats(values):
    center = values - jnp.mean(values, axis=-1, keepdims=True)
    scale = lax.rsqrt(jnp.mean(center * center, axis=-1, keepdims=True) + 1e-05)
    return center * scale, scale


def norm_back(grad, gain, normed, scale):
    dn = grad * gain
    return scale * (
        dn
        - jnp.mean(dn, axis=-1, keepdims=True)
        - normed * jnp.mean(dn * normed, axis=-1, keepdims=True)
    )


def gelu_pair(u):
    cdf = 0.5 * (1.0 + lax.erf(u * 0.7071067811865476))
    pdf = jnp.exp(-0.5 * u * u) * 0.3989422804014327
    return (u * cdf).astype(BF16), (cdf + u * pdf).astype(BF16)


MESH = pl.DeviceIdType.MESH
ROWS = 256
CORE = 2 * ROWS
CHUNK = 128
PART = 64
STEPS = ROWS // CHUNK
QUARTER = D // 4
UNITS = D
TILE = 256
PAIRS = 4
KEYS = 2 * CORE + PREFIX
SEMS = 224


def gelu_both(u):
    size = jnp.abs(u) * 0.7071067811865476
    t = 1.0 / (1.0 + 0.3275911 * size)
    poly = t * (0.254829592 + t * (-0.284496736 + t * (1.421413741 + t * (-1.453152027 + t * 1.061405429))))
    bell = jnp.exp(-(size * size))
    tail = 0.5 * poly * bell
    cdf = jnp.where(u >= 0, 1.0 - tail, tail)
    return (u * cdf).astype(BF16), (cdf + u * (bell * 0.3989422804014327)).astype(BF16)


def norm_chunk(values):
    center = values - jnp.mean(values, axis=-1, keepdims=True)
    scale = lax.rsqrt(jnp.mean(center * center, axis=-1, keepdims=True) + 1e-05)
    return center * scale, scale


class Copies:
    def __init__(self, send, arrive, here):
        self.send, self.arrive, self.here = send, arrive, here
        self.remotes = self.locals = 0

    def remote(self, src, dst, device, number=None):
        if number is None:
            number = self.remotes
            self.remotes += 1
        copy = pltpu.make_async_remote_copy(
            src_ref=src, dst_ref=dst, send_sem=self.send.at[number], recv_sem=self.arrive.at[number],
            device_id=device, device_id_type=MESH,
        )
        return copy, number

    def local(self, src, dst, number=None):
        if number is None:
            number = self.locals
            self.locals += 1
        return pltpu.make_async_copy(src, dst, self.here.at[number])


def fused_kernel(
    dp,
    states, cotangent, segments, qkv, out_w, up_w, down_w, pre, pack,
    hidden, grads, pgrads, gup, gdown,
    xb, xg, cot, lab_q, lab_k, qw, ow, uw, dw, pw, pk,
    qs, kv, kvs, mg, lse, n1, r1, n2, r2, slopes,
    mid, acc, act, mrecv, fsnd, fin, fout, fret, gfirst, gm, gms, gout,
    keys, turned, vals, dk_acc, dv_acc, dq, dkv, dkv_send, dkv_recv, dxs, dxr, pacc, psib, pacross, psum, pdp,
    send_sem, arrive_sem, here_sem,
):
    core, z, place = lax.axis_index("section"), lax.axis_index("dp"), lax.axis_index("tensor")
    low, high = lax.rem(place, 2), place // 2
    across = place + 1 - 2 * low
    along = lax.rem(place + 2, 4)
    sib_dev = {"section": 1 - core}
    x_dev, y_dev = {"tensor": across}, {"tensor": along}
    diag_dev = {"section": 1 - core, "tensor": across}

    def dp_dev(step):
        return {"dp": z + step - 2 * step * lax.rem(z // step, 2)}

    dp_steps = []
    while (1 << len(dp_steps)) < dp:
        dp_steps.append(1 << len(dp_steps))
    z_dev = dp_dev(1)
    wires = Copies(send_sem, arrive_sem, here_sem)
    pending = []

    barrier = pltpu.get_barrier_semaphore()
    greeted = [sib_dev, x_dev, y_dev, diag_dev] + [dp_dev(s) for s in dp_steps]
    for device in greeted:
        pl.semaphore_signal(barrier, inc=1, device_id=device, device_id_type=MESH)
    pl.semaphore_wait(barrier, len(greeted))

    class Own:
        def __init__(self, layer, src, dst):
            self.layer = layer
            self.here = wires.local(src, dst)
            self.first = wires.remote(src, dst, sib_dev)[0]

        def start(self):
            @pl.when(core == self.layer)
            def _():
                self.here.start()
                self.first.start()

        def need(self):
            @pl.when(core == self.layer)
            def _():
                self.here.wait()

            @pl.when(core != self.layer)
            def _():
                self.first.wait_recv()

        def finish(self):
            @pl.when(core == self.layer)
            def _():
                self.first.wait_send()

    class Away:
        def __init__(self, layer, src, dst):
            self.layer = layer
            self.first = wires.remote(src, dst, sib_dev)[0]

        def start(self):
            @pl.when(core == self.layer)
            def _():
                self.first.start()

        def need(self):
            @pl.when(core != self.layer)
            def _():
                self.first.wait_recv()

        def finish(self):
            @pl.when(core == self.layer)
            def _():
                self.first.wait_send()

    class Direct:
        def __init__(self, layer, src, dst, dev):
            self.layer = layer
            self.over = wires.remote(src, dst, dev)[0]
            self.rest = wires.remote(dst, dst, sib_dev)[0]

        def start(self):
            @pl.when(core == self.layer)
            def _():
                self.over.start()

        def forward(self):
            @pl.when(core == self.layer)
            def _():
                self.over.wait_recv()
                self.rest.start()

        def need(self):
            @pl.when(core != self.layer)
            def _():
                self.rest.wait_recv()

        def finish(self):
            @pl.when(core == self.layer)
            def _():
                self.over.wait_send()
                self.rest.wait_send()

    class Shared:
        def __init__(self, layer, src, dst, mine, theirs, dev):
            self.layer = layer
            self.over = wires.remote(src.at[mine], dst.at[mine], dev)[0]
            self.dp, number = wires.remote(dst.at[mine], dst.at[mine], z_dev)
            self.dp_in = wires.remote(dst.at[theirs], dst.at[theirs], z_dev, number)[0]
            self.rest = wires.remote(dst.at[mine], dst.at[mine], sib_dev)[0]
            self.last = wires.remote(dst.at[theirs], dst.at[theirs], sib_dev)[0]

        def start(self):
            @pl.when(core == self.layer)
            def _():
                self.over.start()

        def forward(self):
            @pl.when(core == self.layer)
            def _():
                self.over.wait_recv()
                self.dp.start()
                self.rest.start()

        def forward_last(self):
            @pl.when(core == self.layer)
            def _():
                self.dp_in.wait_recv()
                self.last.start()

        def need(self):
            @pl.when(core != self.layer)
            def _():
                self.rest.wait_recv()
                self.last.wait_recv()

        def finish(self):
            @pl.when(core == self.layer)
            def _():
                for c in (self.over, self.dp, self.rest, self.last):
                    c.wait_send()

    odd = lax.rem(z, 2)

    def halves(size, pieces):
        places, at = [], 0
        for piece in pieces:
            places.append(
                tuple(pl.ds(pl.multiple_of(parity_z * (size // 2) + at, 16), piece) for parity_z in (odd, 1 - odd))
            )
            at += piece
        return places

    class Layer:
        def __init__(self, layer):
            self.heads_own = Own(layer, qkv, qw.at[layer, 0])
            self.small_own = [Own(layer, pre, pw.at[layer, 0]), Own(layer, pack, pk.at[layer, 0])]
            self.out_own = Own(layer, out_w, ow.at[layer, 0])
            self.units_own = [Away(layer, up_w, gup.at[layer, 0]), Away(layer, down_w, gdown.at[layer, 0])]
            if layer == 0:
                (mine, theirs), = halves(D, [D // 2])
                self.heads = [
                    Shared(layer, qkv.at[i], qw.at[layer, 1, i], mine, theirs, x_dev) for i in range(3)
                ]
            else:
                self.heads = [Direct(layer, qkv, qw.at[layer, 1], x_dev)]
            self.small = [Direct(layer, pre, pw.at[layer, 1], x_dev), Direct(layer, pack, pk.at[layer, 1], y_dev)]
            self.out_x = Direct(layer, out_w, ow.at[layer, 1], x_dev)
            (mine, theirs), = halves(QUARTER, [QUARTER // 2])
            self.out_y = [
                Shared(layer, out_w, ow.at[layer, 2], mine, theirs, y_dev),
                Shared(layer, ow.at[layer, 1], ow.at[layer, 3], mine, theirs, y_dev),
            ]
            self.units = [
                Shared(layer, src, dst.at[layer, 1], mine, theirs, y_dev)
                for src, dst, pieces in ((up_w, gup, [256, 256]), (down_w, gdown, [256, 128, 128]))
                for mine, theirs in halves(UNITS, pieces)
            ]

        def everything(self):
            return (
                [self.heads_own, self.out_own, self.out_x] + self.small_own + self.units_own + self.heads + self.small
                + self.out_y + self.units
            )

    layers = [Layer(0), Layer(1)]

    def each(items, action):
        for item in items:
            getattr(item, action)()

    loads = {}

    def load(layer, slot, array, when):
        spread, native, dst = ((gup, up_w, uw), (gdown, down_w, dw))[array]
        copy = wires.local(spread.at[layer, slot], dst.at[slot])
        loads[layer, slot, array, when] = copy
        if slot == 0:
            mine = wires.local(native, dst.at[0], wires.locals - 1)

            @pl.when(core == layer)
            def _():
                mine.start()

            @pl.when(core != layer)
            def _():
                copy.start()
        else:
            copy.start()

    def loaded(layer, slot, array, when):
        loads[layer, slot, array, when].wait()

    def chunk_rows(step):
        return pl.ds(step * CHUNK, CHUNK)

    class Tokens:
        def __init__(self, source, dest):
            self.near = [wires.local(source.at[low, chunk_rows(i)], dest.at[chunk_rows(i)]) for i in range(STEPS)]
            self.far = [
                wires.remote(source.at[1 - low, chunk_rows(i)], dest.at[chunk_rows(i)], x_dev)[0] for i in range(STEPS)
            ]

        def start(self):
            @pl.when(core == 0)
            def _():
                for c in self.near:
                    c.start()

            @pl.when(core == 1)
            def _():
                for c in self.far:
                    c.start()

        def wait(self, step):
            @pl.when(core == 0)
            def _():
                self.near[step].wait()

            @pl.when(core == 1)
            def _():
                self.far[step].wait_recv()

        def finish(self):
            @pl.when(core == 1)
            def _():
                for c in self.far:
                    c.wait_send()

    tokens = Tokens(states, xb.at[0])
    ends = Tokens(cotangent, cot)

    first = layers[0]
    tokens.start()
    each([first.heads_own] + first.small_own, "start")
    each(first.heads + first.small, "start")
    each([first.out_own] + first.units_own, "start")

    def send_chunk(src, dst, device):
        copy, _ = wires.remote(src, dst, device)
        copy.start()
        return copy

    gathers = {}

    def gather_x(layer, step):
        gathers[layer, step] = send_chunk(
            xb.at[layer, chunk_rows(step)], xg.at[chunk_rows(step)], y_dev
        )

    for step in range(STEPS):
        tokens.wait(step)
        gather_x(0, step)

    each(first.units[:2], "start")

    parity = low + core - 2 * low * core
    row = segments[pl.ds(low, 1), :]
    last = row[:, LEN - 1 :]

    def block_labels(block):
        ids = last - segments[pl.ds(low, 1), pl.ds(pl.multiple_of(block * ROWS, ROWS), ROWS)]
        numbers = lax.broadcasted_iota(jnp.int32, (LABELS, ROWS), 0)
        same = jnp.where(numbers == ids, 1.0, 0.0)
        return same.T, jnp.where(numbers <= 2 * SPAN, HIDDEN * (1.0 - same), 0.0).T

    for index, (h, p) in enumerate(((high, parity), (1 - high, parity), (high, 1 - parity), (1 - high, 1 - parity))):
        same, differ = block_labels(2 * h + p)
        if index < 2:
            lab_q[pl.ds(index * ROWS, ROWS), :] = same.astype(BF16)
        lab_k[pl.ds(index * ROWS, ROWS), :] = differ.astype(BF16)

    def project(layer, source, start, size, slots=(0, 1)):
        for slot in slots:
            columns = slice(slot * QUARTER, (slot + 1) * QUARTER)
            rows = pl.ds(start, size)
            qs[layer, rows, columns] = dot(source, qw[layer, slot, 0]).astype(BF16)
            kv[layer, rows, columns] = dot(source, qw[layer, slot, 1]).astype(BF16)
            kv[layer, rows, slice(CORE + columns.start, CORE + columns.stop)] = dot(
                source, qw[layer, slot, 2]
            ).astype(BF16)

    def lanes(index, base=0):
        return slice(base + index * PAIR, base + (index + 1) * PAIR)

    def fill_keys(layer):
        for p in range(PAIRS):
            keys[p, :CORE, :PAIR] = kv[layer, :, lanes(p)]
            keys[p, CORE : 2 * CORE, :PAIR] = kvs[layer, :, lanes(p)]
            keys[p, 2 * CORE :, :PAIR] = pw[layer, p // 2, 0, :, lanes(p % 2)]

    def pair_values(layer, p):
        return kv[layer, :, lanes(p, CORE)], kvs[layer, :, lanes(p, CORE)], pw[layer, p // 2, 1, :, lanes(p % 2)]

    def fill_turned(p, own, sib, prefix):
        turned[p, :, :CORE] = own.T
        turned[p, :, CORE : 2 * CORE] = sib.T
        turned[p, :, 2 * CORE :] = prefix.T

    def fill_forward(layer):
        fill_keys(layer)
        for p in range(PAIRS):
            fill_turned(p, *pair_values(layer, p))

    def fill_backward(layer):
        if layer == 0:
            fill_keys(layer)
        for p in range(PAIRS):
            own, sib, prefix = pair_values(layer, p)
            vals[p, :CORE, :] = own
            vals[p, CORE : 2 * CORE, :] = sib
            vals[p, 2 * CORE :, :] = prefix
            fill_turned(p, keys[p, :CORE, :PAIR], keys[p, CORE : 2 * CORE, :PAIR], keys[p, 2 * CORE :, :PAIR])

    for p in range(PAIRS):
        keys[p, : 2 * CORE, PAIR:] = lab_k[...]
        keys[p, 2 * CORE :, PAIR:] = jnp.zeros((PREFIX, LABELS), BF16)

    def both_heads(values):
        return jnp.concatenate([jnp.where(head_lanes(CHUNK, h), values, 0) for h in range(2)], 0)

    def score_chunk(layer, start, p):
        rows = pl.ds(start, CHUNK)
        queries = both_heads(qs[layer, rows, lanes(p)] * 0.125)
        label = lab_q[rows, :]
        return queries, dot_t(keys[p], jnp.concatenate([queries, jnp.concatenate([label, label], 0)], 1))

    def untangle(both):
        return jnp.concatenate([both[:HEAD, :CHUNK], both[HEAD:, CHUNK:]], 0).T

    def attend_chunks(layer, steps):
        blocks = [(p, start, action if p + 1 == PAIRS else None) for start, action in steps for p in range(PAIRS)]
        ahead = score_chunk(layer, blocks[0][1], 0)
        for index, (p, start, action) in enumerate(blocks):
            rows, at = pl.ds(start, CHUNK), start // CHUNK
            _, scores = ahead
            if index + 1 < len(blocks):
                ahead = score_chunk(layer, blocks[index + 1][1], blocks[index + 1][0])
            peak = jnp.max(scores, axis=0, keepdims=True)
            weights = jnp.exp(scores - peak)
            total = jnp.sum(weights, axis=0, keepdims=True)
            merged = dot(turned[p], weights.astype(BF16)) * (1.0 / total)
            lse[layer, p, at : at + 1, :] = peak + jnp.log(total)
            mg[layer, rows, lanes(p)] = untangle(merged).astype(BF16)
            if action is not None:
                action()

    def attend_chunks_back(layer, starts, fresh, done=None):
        def begin(p, start):
            rows = pl.ds(start, CHUNK)
            queries, scores = score_chunk(layer, start, p)
            grad_both = both_heads(gm[rows, lanes(p)])
            return queries, scores, grad_both, dot_t(vals[p], grad_both)

        blocks = [(p, start) for p in range(PAIRS) for start in starts]
        ahead = begin(*blocks[0])
        kept = []
        for index, (p, start) in enumerate(blocks):
            rows, at = pl.ds(start, CHUNK), start // CHUNK
            queries, scores, grad_both, grad_weights = ahead
            if index + 1 < len(blocks):
                ahead = begin(*blocks[index + 1])
            product = (gm[rows, lanes(p)].astype(F32) * mg[layer, rows, lanes(p)].astype(F32)).T
            delta = jnp.concatenate(
                [jnp.sum(product[h * HEAD : (h + 1) * HEAD], axis=0, keepdims=True) for h in range(2)], 1
            )
            weights = jnp.exp(scores - lse[layer, p, at : at + 1, :])
            grad_scores = (weights * (grad_weights - delta)).astype(BF16)
            dq[rows, lanes(p)] = (untangle(dot(turned[p], grad_scores)) * 0.125).astype(BF16)
            kept.append((weights.astype(BF16), grad_both, grad_scores, queries))
            if len(kept) == len(starts):
                joined = [jnp.concatenate([k[i] for k in kept], 1 - i % 2) for i in range(4)]
                dv_part, dk_part = dot(joined[0], joined[1]), dot(joined[2], joined[3])
                if fresh:
                    dv_acc[:, lanes(p)] = dv_part
                    dk_acc[:, lanes(p)] = dk_part
                else:
                    dv_acc[:, lanes(p)] += dv_part
                    dk_acc[:, lanes(p)] += dk_part
                kept = []
                if done is not None:
                    done(p)

    def vector(layer, index):
        return pk[layer, 0, index : index + 1, :]

    def keep_norm(store, scales, layer, rows, normed, scale):
        store[layer, rows, :] = normed.astype(BF16)
        scales[layer, rows, :] = jnp.broadcast_to(scale, (CHUNK, PAIR))

    def forward_attention(layer):
        this, later = layers[layer], layers[1]
        if layer == 0:
            this.heads_own.need()
            project(0, xb[0], 0, ROWS, (0,))
            each(this.heads + this.small, "forward")
            this.out_x.start()
            this.out_y[0].start()
            for step in range(STEPS):
                gathers[0, step].wait_recv()
                project(0, xg[chunk_rows(step), :], ROWS + step * CHUNK, CHUNK, (0,))
            each(this.units[:2], "forward")
            this.out_x.forward()
            this.out_y[1].start()
            each(later.heads + later.small + [later.out_x], "start")
            each(this.units[2:], "start")
            each(this.heads, "forward_last")
            each(this.heads + this.small_own + this.small, "need")
            project(0, xb[0], 0, ROWS, (1,))
            sent = [send_chunk(kv.at[0, :ROWS], kvs.at[0, :ROWS], sib_dev)]
            project(0, xg[...], ROWS, ROWS, (1,))
            sent.append(send_chunk(kv.at[0, ROWS:], kvs.at[0, ROWS:], sib_dev))
        else:
            each([this.heads_own] + this.heads + this.small_own + this.small, "need")
            project(1, xb[1], 0, ROWS)
            sent = [send_chunk(kv.at[1, :ROWS], kvs.at[1, :ROWS], sib_dev)]
            for step in range(STEPS):
                gathers[1, step].wait_recv()
                project(1, xg[chunk_rows(step), :], ROWS + step * CHUNK, CHUNK)
            sent.append(send_chunk(kv.at[1, ROWS:], kvs.at[1, ROWS:], sib_dev))
        for c in sent:
            c.wait_recv()
        fill_forward(layer)
        swaps, copies = [], []

        def swap(step):
            rows = pl.ds(ROWS + step * CHUNK, CHUNK)
            swaps.append(send_chunk(mg.at[layer, rows], mrecv.at[chunk_rows(step)], y_dev))

        def finish(step):
            swaps[step].wait_recv()
            rows = chunk_rows(step)
            parts = [mg[layer, rows, :QUARTER], mg[layer, rows, QUARTER:], mrecv[rows, :QUARTER], mrecv[rows, QUARTER:]]
            total = xb[layer, rows, :].astype(F32) + vector(layer, 3)
            for i, part in enumerate(parts):
                total = total + dot(part, ow[layer, i])
            normed, scale = norm_chunk(total)
            keep_norm(n1, r1, layer, rows, normed, scale)
            middle = normed * vector(layer, 1) + vector(layer, 4)
            mid[rows, :] = middle
            fsnd[rows, :] = middle.astype(BF16)
            copies.append(send_chunk(fsnd.at[rows], fin.at[rows], x_dev))

        def first_peer():
            swap(0)
            if layer == 0:
                each(this.out_y, "forward")
            else:
                ends.start()

        def first_own():
            if layer == 0:
                each(this.units[2:], "forward")

        def second_peer():
            swap(1)
            each(this.out_y, "forward_last")
            each([this.out_own, this.out_x] + this.out_y, "need")
            finish(0)

        def second_own():
            finish(1)
            if layer == 0:
                each(later.units[:2], "start")

        attend_chunks(
            layer, [(ROWS, first_peer), (0, first_own), (ROWS + CHUNK, second_peer), (CHUNK, second_own)]
        )
        each(this.units_own, "need")
        load(layer, 0, 0, 0)
        load(layer, 0, 1, 0)
        for c in sent + swaps:
            c.wait_send()

        def gathered():
            for step in range(STEPS):
                gathers[layer, step].wait_send()

        gathered()
        return copies

    def tiles(count, body):
        def two(j, _):
            body(2 * j, 0)
            return body(2 * j + 1, 0)

        lax.fori_loop(0, count // 2, two, 0)

    def feed_rows(layer, slot, source, start, store):
        size = source.shape[0]

        def up_tile(j, _):
            columns = pl.ds(pl.multiple_of(j * TILE, TILE), TILE)
            wide = pl.ds(pl.multiple_of(slot * UNITS + j * TILE, TILE), TILE)
            u = dot(source[...], uw[slot, :, columns]) + pk[layer, slot, 0:1, columns]
            store[:, columns], slopes[layer, pl.ds(start, size), wide] = gelu_both(u)
            return 0

        tiles(UNITS // TILE, up_tile)

    def feed_rows_back(layer, source, start, size):
        def tile(j, _):
            slot, units_at = j // 4, pl.ds(pl.multiple_of(lax.rem(j, 4) * TILE, TILE), TILE)
            wide = pl.ds(pl.multiple_of(j * TILE, TILE), TILE)
            u = dot_t(source[...], dw[slot, units_at, :]) * slopes[layer, pl.ds(start, size), wide].astype(F32)
            act[:size, wide] = u.astype(BF16)
            return 0

        tiles(2 * UNITS // TILE, tile)

    def feed_out(store, acts, back):
        def tile(j, _):
            columns = pl.ds(pl.multiple_of(j * TILE, TILE), TILE)
            if back:
                u = dot_t(acts[0][...], uw[0, columns, :]) + dot_t(acts[1][...], uw[1, columns, :])
            else:
                u = dot(acts[0][...], dw[0, :, columns]) + dot(acts[1][...], dw[1, :, columns])
            store[:, columns] = u.astype(store.dtype)
            return 0

        tiles(D // TILE, tile)

    def act_slots(size):
        return [act.at[pl.ds(0, size), pl.ds(slot * UNITS, UNITS)] for slot in range(2)]

    def feed_forward(layer, copies, finish, arrivals):
        this = layers[layer]
        mine = act_slots(ROWS)
        theirs = [[dkv.at[pl.ds(slot * ROWS + step * CHUNK, CHUNK)] for slot in range(2)] for step in range(STEPS)]

        def feed_peer(slot, step):
            feed_rows(layer, slot, fin.at[chunk_rows(step)], ROWS + step * CHUNK, theirs[step][slot])

        loaded(layer, 0, 0, 0)
        feed_rows(layer, 0, fsnd, 0, mine[0])
        for step in range(STEPS):
            copies[step].wait_recv()
            feed_peer(0, step)
            arrivals[step]()
        each(this.units[:2], "forward_last")
        each(this.units[:2], "need")
        load(layer, 1, 0, 0)
        loaded(layer, 1, 0, 0)
        for step in range(STEPS):
            feed_peer(1, step)
        each(this.units[2:], "forward_last")
        each(this.units[2:], "need")
        load(layer, 1, 1, 0)
        loaded(layer, 0, 1, 0)
        loaded(layer, 1, 1, 0)
        returned = []
        for step in range(STEPS):
            rows = chunk_rows(step)
            feed_out(fout.at[rows], theirs[step], False)
            returned.append(send_chunk(fout.at[rows], fret.at[rows], x_dev))
        feed_rows(layer, 1, fsnd, 0, mine[1])
        feed_out(acc, mine, False)
        arrivals[STEPS]()
        for c in copies:
            c.wait_send()
        for step in range(STEPS):
            returned[step].wait_recv()
            finish(step, chunk_rows(step), acc[chunk_rows(step), :] + fret[chunk_rows(step), :].astype(F32))
        for c in returned:
            c.wait_send()

    def feed_back(layer, copies, finish, between):
        feed_rows_back(layer, fsnd, 0, ROWS)
        feed_out(acc, act_slots(ROWS), True)
        returned = []
        per = len(copies) // STEPS
        for step in range(STEPS):
            rows = chunk_rows(step)
            for c in copies[step * per : (step + 1) * per]:
                c.wait_recv()
            feed_rows_back(layer, fin.at[rows], ROWS + step * CHUNK, CHUNK)
            feed_out(fout.at[rows], act_slots(CHUNK), True)
            returned.append(send_chunk(fout.at[rows], fret.at[rows], x_dev))
        between()
        for step in range(STEPS):
            returned[step].wait_recv()
            finish(step, chunk_rows(step), acc[chunk_rows(step), :] + fret[chunk_rows(step), :].astype(F32))
        for c in copies + returned:
            c.wait_send()

    deliveries = []
    later_deliveries = []

    def deliver(layer, source, dest, rows, now=False):
        far, number = wires.remote(source.at[rows], dest.at[low, rows], {"section": layer, "tensor": across})
        far_in, _ = wires.remote(source.at[rows], dest.at[1 - low, rows], {"section": layer, "tensor": across}, number)
        if layer == 0:
            near = wires.local(source.at[rows], dest.at[low, rows])
        else:
            near, _ = wires.remote(source.at[rows], dest.at[low, rows], sib_dev)

        def start():
            @pl.when(core == 0)
            def _():
                near.start()

            @pl.when(core == 1)
            def _():
                far.start()

        if now:
            start()
        else:
            later_deliveries.append(start)

        def sent():
            @pl.when(core == 0)
            def _():
                near.wait() if layer == 0 else near.wait_send()

            @pl.when(core == 1)
            def _():
                far.wait_send()

        def arrived():
            @pl.when(core == layer)
            def _():
                far_in.wait_recv()
                if layer == 1:
                    near.wait_recv()

        deliveries.append(arrived)
        return sent

    def start_back(layer, rows, grad):
        normed, scale = n2[layer, rows, :].astype(F32), r2[layer, rows, :1]
        value = norm_back(grad, vector(layer, 2), normed, scale)
        mid[rows, :] = value
        fsnd[rows, :] = value.astype(BF16)
        return send_chunk(fsnd.at[rows], fin.at[rows], x_dev)

    unsent = []
    back_copies = []

    def forward_finish(layer):
        def finish(step, rows, branch):
            normed, scale = norm_chunk(mid[rows, :] + branch + vector(layer, 5))
            keep_norm(n2, r2, layer, rows, normed, scale)
            xb[layer + 1, rows, :] = (normed * vector(layer, 2) + vector(layer, 6)).astype(BF16)
            if layer == 0:
                gather_x(1, step)
            unsent.append(deliver(layer, xb.at[layer + 1], hidden, rows))
            if layer == 1:
                ends.wait(step)
                back_copies.append(start_back(1, rows, cot[rows, :].astype(F32)))

        return finish

    second = layers[1]

    def first_arrivals():
        each(second.heads + second.small, "forward")
        second.out_x.forward()
        each(second.units[2:], "start")
        each(second.out_y, "start")

    def later_arrivals():
        each([second.heads_own] + second.small_own + [second.out_own] + second.units_own, "start")
        each(second.units[:2], "forward")

    def after_units():
        each(second.out_y, "forward")
        each(second.units[2:], "forward")

    copies = forward_attention(0)
    feed_forward(0, copies, forward_finish(0), [first_arrivals, later_arrivals, after_units])
    copies = forward_attention(1)
    feed_forward(1, copies, forward_finish(1), [lambda: None] * 3)

    grad_sent = []

    def backward(layer, copies):
        swaps = []

        def finish(step, rows, term):
            middle = mid[rows, :] + term
            first = norm_back(middle, vector(layer, 1), n1[layer, rows, :].astype(F32), r1[layer, rows, :1])
            gfirst[rows, :] = first
            low_first = first.astype(BF16)
            for i in range(4):
                part = dot_t(low_first, ow[layer, i]).astype(BF16)
                columns = slice((i % 2) * QUARTER, (i % 2 + 1) * QUARTER)
                if i < 2:
                    gm[rows, columns] = part
                else:
                    gms[rows, columns] = part
            swaps.append(send_chunk(gms.at[rows], gm.at[pl.ds(ROWS + step * CHUNK, CHUNK)], y_dev))

            attend_chunks_back(layer, [step * CHUNK], step == 0)

        def between():
            if layer == 1:
                for slot in range(2):
                    for array in range(2):
                        load(0, slot, array, 1)
            fill_backward(layer)

        feed_back(layer, copies, finish, between)
        for d in later_deliveries:
            d()
        later_deliveries.clear()
        for c in swaps:
            c.wait_recv()
        given = []

        def give(p):
            dkv_send[p, 0] = dk_acc[CORE : 2 * CORE, lanes(p)].astype(BF16)
            dkv_send[p, 1] = dv_acc[CORE : 2 * CORE, lanes(p)].astype(BF16)
            given.append(send_chunk(dkv_send.at[p], dkv_recv.at[layer, p], sib_dev))

        attend_chunks_back(layer, [ROWS, ROWS + CHUNK], False, give)
        pacc[layer, 0] = dk_acc[2 * CORE :, :]
        pacc[layer, 1] = dv_acc[2 * CORE :, :]
        if layer == 0:
            total = prefix_start()
        for p in range(PAIRS):
            given[p].wait_recv()
            dkv[:, lanes(p)] = (dk_acc[:CORE, lanes(p)] + dkv_recv[layer, p, 0].astype(F32)).astype(BF16)
            dkv[:, lanes(p, CORE)] = (dv_acc[:CORE, lanes(p)] + dkv_recv[layer, p, 1].astype(F32)).astype(BF16)

        def input_term(store, start, size):
            rows = pl.ds(start, size)

            def tile(j, _):
                features = pl.ds(pl.multiple_of(j * TILE, TILE), TILE)
                total = None
                for slot in range(2):
                    columns = slice(slot * QUARTER, (slot + 1) * QUARTER)
                    shifted = slice(CORE + slot * QUARTER, CORE + (slot + 1) * QUARTER)
                    for part, source in enumerate((dq[rows, columns], dkv[rows, columns], dkv[rows, shifted])):
                        term = dot_t(source, qw[layer, slot, part, features, :])
                        total = term if total is None else total + term
                store[:, features] = total.astype(store.dtype)
                return 0

            tiles(D // TILE, tile)

        returned = []
        for step in range(STEPS):
            input_term(dxs.at[chunk_rows(step)], ROWS + step * CHUNK, CHUNK)
            for part in range(CHUNK // PART):
                rows = pl.ds(step * CHUNK + part * PART, PART)
                returned.append(send_chunk(dxs.at[rows], dxr.at[rows], y_dev))
        if layer == 0:
            total.stage()
        input_term(acc, 0, ROWS)
        if layer == 1:
            for slot in range(2):
                for array in range(2):
                    loaded(0, slot, array, 1)
        else:
            total.stage()
        for sent in grad_sent:
            sent()
        grad_sent.clear()
        onward = []
        for step in range(ROWS // PART):
            rows = pl.ds(step * PART, PART)
            returned[step].wait_recv()
            value = gfirst[rows, :] + (acc[rows, :] + dxr[rows, :].astype(F32))
            gout[rows, :] = value
            grad_sent.append(deliver(layer, gout, grads, rows, layer == 0))
            if layer == 1:
                onward.append(start_back(0, rows, value.astype(BF16).astype(F32)))
            else:
                total.stage()
        for c in swaps + given + returned:
            c.wait_send()
        return onward

    class prefix_start:
        def __init__(self):
            self.sib = send_chunk(pacc.at[1 - core], psib, sib_dev)
            self.sent = [self.sib]
            self.at = 0

        def stage(self):
            if self.at > len(dp_steps) + 1:
                return
            if self.at == 0:
                self.sib.wait_recv()
                total = pacc[core] + psib[...]
                psum[0] = total[:, :, :QUARTER]
                pacross[0] = total[:, :, QUARTER:]
                self.next = send_chunk(pacross.at[0], pacross.at[1], x_dev)
                self.sent.append(self.next)
            else:
                self.next.wait_recv()
                arrived = pacross[1] if self.at == 1 else pdp[self.at - 2]
                psum[self.at] = psum[self.at - 1] + arrived
                if self.at <= len(dp_steps):
                    step = self.at - 1
                    self.next = send_chunk(psum.at[self.at], pdp.at[step], dp_dev(dp_steps[step]))
                    self.sent.append(self.next)
                else:
                    self.done = wires.local(psum.at[self.at], pgrads)
                    self.done.start()
            self.at += 1

        def finish(self):
            while self.at <= len(dp_steps) + 1:
                self.stage()
            for c in self.sent:
                c.wait_send()
            self.done.wait()

    holder = []
    start_class = prefix_start

    def prefix_start():
        holder.append(start_class())
        return holder[0]

    back_copies = backward(1, back_copies)
    backward(0, back_copies)
    holder[0].finish()
    for sent in unsent + grad_sent:
        sent()
    for arrived in deliveries:
        arrived()
    tokens.finish()
    ends.finish()
    for layer in layers:
        each(layer.everything(), "finish")


def fused(dp, states, cotangent, segments, qkv, out_w, up_w, down_w, pre, pack):
    shape = jax.ShapeDtypeStruct
    steps = dp.bit_length() - 1
    vmem = pltpu.VMEM
    scratch = [
        vmem((3, ROWS, D), BF16),
        vmem((ROWS, D), BF16),
        vmem((ROWS, D), BF16),
        vmem((CORE, LABELS), BF16), vmem((2 * CORE, LABELS), BF16),
        vmem((2, 2, 3, D, QUARTER), BF16),
        vmem((2, 4, QUARTER, D), BF16),
        vmem((2, D, UNITS), BF16), vmem((2, UNITS, D), BF16),
        vmem((2, 2, 2, PREFIX, QUARTER), BF16),
        vmem((2, 2, 8, D), F32),
        vmem((2, CORE, CORE), BF16), vmem((2, CORE, 2 * CORE), BF16), vmem((2, CORE, 2 * CORE), BF16),
        vmem((2, CORE, CORE), BF16), vmem((2, PAIRS, 8, 2 * CHUNK), F32),
        vmem((2, ROWS, D), BF16), vmem((2, ROWS, PAIR), F32),
        vmem((2, ROWS, D), BF16), vmem((2, ROWS, PAIR), F32),
        vmem((2, CORE, 2 * UNITS), BF16),
        vmem((ROWS, D), F32), vmem((ROWS, D), F32), vmem((ROWS, 2 * UNITS), BF16),
        vmem((ROWS, CORE), BF16),
        vmem((ROWS, D), BF16), vmem((ROWS, D), BF16), vmem((ROWS, D), BF16), vmem((ROWS, D), BF16),
        vmem((ROWS, D), F32),
        vmem((CORE, CORE), BF16), vmem((ROWS, CORE), BF16), vmem((ROWS, D), F32),
        vmem((PAIRS, KEYS, PAIR + LABELS), BF16), vmem((PAIRS, PAIR, KEYS), BF16), vmem((PAIRS, KEYS, PAIR), BF16),
        vmem((KEYS, CORE), F32), vmem((KEYS, CORE), F32),
        vmem((CORE, CORE), BF16), vmem((CORE, 2 * CORE), BF16), vmem((PAIRS, 2, CORE, PAIR), BF16),
        vmem((2, PAIRS, 2, CORE, PAIR), BF16),
        vmem((ROWS, D), BF16), vmem((ROWS, D), BF16),
        vmem((2, 2, PREFIX, CORE), F32), vmem((2, PREFIX, CORE), F32),
        vmem((2, 2, PREFIX, QUARTER), F32), vmem((steps + 2, 2, PREFIX, QUARTER), F32),
        vmem((max(steps, 1), 2, PREFIX, QUARTER), F32),
        pltpu.SemaphoreType.DMA((SEMS,)), pltpu.SemaphoreType.DMA((SEMS,)), pltpu.SemaphoreType.DMA((SEMS,)),
    ]
    anywhere = pl.BlockSpec(memory_space=pl.ANY)
    result = pl.pallas_call(
        functools.partial(fused_kernel, dp),
        out_shape=[
            shape((2, ROWS, D), BF16), shape((2, ROWS, D), F32), shape((2, PREFIX, QUARTER), F32),
            shape((2, 2, D, UNITS), BF16), shape((2, 2, UNITS, D), BF16),
        ],
        in_specs=[anywhere, anywhere, pl.BlockSpec(memory_space=pltpu.VMEM)] + [anywhere] * 6,
        out_specs=[anywhere] * 5,
        scratch_shapes=scratch,
        compiler_params=pltpu.CompilerParams(
            collective_id=0, has_side_effects=True, vmem_limit_bytes=63 << 20
        ),
        name="layers",
    )(states, cotangent, segments, qkv, out_w, up_w, down_w, pre, pack)
    return result[:3]


class Links:
    def __init__(self):
        self.core = lax.axis_index("section")
        self.place = lax.axis_index("tensor")
        self.size = lax.axis_size("tensor")
        self.low = self.place % 2
        self.high = self.place // 2
        self.group = self.size // 2

    def sibling(self, a, only=None):
        pairs = [(0, 1), (1, 0)] if only is None else [(only, 1 - only)]
        return lax.ppermute(a, "section", pairs)

    def across(self, a, only=None):
        if only is None:
            return lax.ppermute(a, "tensor", [(t, t ^ 1) for t in range(self.size)])
        pairs = [(only * self.size + t, only * self.size + (t ^ 1)) for t in range(self.size)]
        return lax.ppermute(a, ("section", "tensor"), pairs)

    def diagonal(self, a, source):
        pairs = [(source * self.size + t, (1 - source) * self.size + (t ^ 1)) for t in range(self.size)]
        return lax.ppermute(a, ("section", "tensor"), pairs)

    def from_ahead(self, a, by):
        g = self.group
        pairs = [(2 * ((h + by) % g) + p, 2 * h + p) for h in range(g) for p in range(2)]
        return lax.ppermute(a, "tensor", pairs)

    def gather(self, a):
        return [a] + [self.from_ahead(a, k) for k in range(1, self.group)]

    def scatter_sum(self, part_fn):
        arrived = [self.from_ahead(part_fn(k).astype(BF16), self.group - k) for k in range(1, self.group)]
        total = part_fn(0)
        for a in arrived:
            total = total + a.astype(F32)
        return total


def forward(links, x, weights, pre, labels):
    qkv_w, out_w, up_w, up_b, down_w, gains, shifts = weights
    width = out_w.shape[0]
    blocks = [dot(b, qkv_w).astype(BF16) for b in links.gather(x)]
    qkv = jnp.concatenate(blocks, 0)
    kv_sib = links.sibling(qkv[:, width:])
    merged, lse = attend(qkv, kv_sib, pre, labels)
    rows = x.shape[0]
    attended = links.scatter_sum(lambda k: dot(merged[k * rows : (k + 1) * rows], out_w)) + shifts[0]
    normed_first, scale_first = norm_stats(x.astype(F32) + attended)
    middle = normed_first * gains[0] + shifts[1]
    blocks = links.gather(middle.astype(BF16))
    pairs = [gelu_pair(dot(b, up_w) + up_b) for b in blocks]
    branch = links.scatter_sum(lambda k: dot(pairs[k][0], down_w)) + shifts[2]
    normed_last, scale_last = norm_stats(middle + branch)
    result = (normed_last * gains[1] + shifts[3]).astype(BF16)
    slopes = [p[1] for p in pairs]
    return result, (qkv, kv_sib, merged, lse, normed_first, scale_first, slopes, normed_last, scale_last)


def backward(links, grad, weights, pre, labels, kept):
    qkv_w, out_w, up_w, up_b, down_w, gains, shifts = weights
    qkv, kv_sib, merged, lse, normed_first, scale_first, slopes, normed_last, scale_last = kept
    rows = grad.shape[0]
    grad_second = norm_back(grad.astype(F32), gains[1], normed_last, scale_last)
    blocks = links.gather(grad_second.astype(BF16))
    hiddens = [
        (dot_t(b, down_w) * s.astype(F32)).astype(BF16) for b, s in zip(blocks, slopes, strict=True)
    ]
    grad_middle = grad_second + links.scatter_sum(lambda k: dot_t(hiddens[k], up_w))
    grad_first = norm_back(grad_middle, gains[0], normed_first, scale_first)
    blocks = links.gather(grad_first.astype(BF16))
    grad_merged = jnp.concatenate([dot_t(b, out_w).astype(BF16) for b in blocks], 0)
    dq, dko, dvo, dks, dvs, dkp, dvp = attend_back(qkv, kv_sib, pre, labels, merged, lse, grad_merged)
    arrived = links.sibling(jnp.concatenate([dks, dvs], 1)).astype(F32)
    width = out_w.shape[0]
    dk = (dko + arrived[:, :width]).astype(BF16)
    dv = (dvo + arrived[:, width:]).astype(BF16)
    dqkv = jnp.concatenate([dq, dk, dv], 1)
    grad_inputs = grad_first + links.scatter_sum(
        lambda k: dot_t(dqkv[k * rows : (k + 1) * rows], qkv_w)
    )
    return grad_inputs, jnp.stack([dkp, dvp])


def spread_weights(links, arrays):
    first = links.core == 0
    layers = ([], [])
    for layer in range(2):
        for a in arrays:
            other = links.across(a, layer)
            sib_a, sib_other = links.sibling(a, layer), links.sibling(other, layer)
            here = links.core == layer
            layers[layer].append((jnp.where(here, a, sib_a), jnp.where(here, other, sib_other)))
    return layers


def sum_over_dp(a):
    size = lax.axis_size("dp")
    step = 1
    if size & (size - 1):
        return lax.psum(a, "dp")
    while step < size:
        a = a + lax.ppermute(a, "dp", [(i, i ^ step) for i in range(size)])
        step *= 2
    return a


def plain(
    states, segment_ids, cotangent, qkv_weight, out_weight, up_weight, up_bias, down_weight,
    norm_gain, shift_vec, prefix,
):
    links = Links()
    first = links.core == 0
    low = links.low

    def arrange(both):
        mine = lax.dynamic_index_in_dim(both, low, 0, keepdims=False)
        other = lax.dynamic_index_in_dim(both, 1 - low, 0, keepdims=False)
        return jnp.where(first, mine, links.across(other, 1))

    x = arrange(states)
    grad = arrange(cotangent)

    segment = lax.dynamic_index_in_dim(segment_ids, low, 0, keepdims=False)
    classes = (segment[-1] - segment).reshape(links.group, 2, -1)
    classes = jnp.roll(classes, -links.high, 0)
    parity = jnp.where(first, low, 1 - low)
    own = lax.dynamic_index_in_dim(classes, parity, 1, keepdims=False).reshape(-1)
    sib = lax.dynamic_index_in_dim(classes, 1 - parity, 1, keepdims=False).reshape(-1)
    numbers = jnp.arange(LABELS)[None, :]
    label_q = (own[:, None] == numbers).astype(BF16)
    known = numbers <= 2 * SPAN
    label_o = jnp.where(known & (own[:, None] != numbers), HIDDEN, 0.0).astype(BF16)
    label_s = jnp.where(known & (sib[:, None] != numbers), HIDDEN, 0.0).astype(BF16)
    labels = (label_q, label_o, label_s)

    small = jnp.concatenate(
        [norm_gain[0], shift_vec[0]], 0
    )
    small_sib = links.sibling(small)
    layers = spread_weights(
        links,
        [jnp.transpose(qkv_weight[0], (1, 0, 2)), prefix[0], out_weight[0], up_weight[0], up_bias, down_weight[0]],
    )
    weights, prefixes = [], []
    for layer in range(2):
        qkv, pre, out, up, bias, down = layers[layer]
        vectors = jnp.where(links.core == layer, small, small_sib).astype(F32)
        weights.append((
            jnp.concatenate([p[i] for i in range(3) for p in qkv], 1),
            jnp.concatenate(out, 0),
            jnp.concatenate(up, 1),
            jnp.concatenate(bias, 1).astype(F32),
            jnp.concatenate(down, 0),
            vectors[:2],
            vectors[2:],
        ))
        prefixes.append(jnp.concatenate(pre, 2))

    y0, kept0 = forward(links, x, weights[0], prefixes[0], labels)
    y1, kept1 = forward(links, y0, weights[1], prefixes[1], labels)
    g1, p1 = backward(links, grad, weights[1], prefixes[1], labels, kept1)
    g0, p0 = backward(links, g1.astype(BF16), weights[0], prefixes[0], labels, kept0)

    def deliver(first_layer, second_layer, wire, dtype):
        near = jnp.where(first, first_layer.astype(dtype), links.sibling(second_layer.astype(wire), 0).astype(dtype))
        far0 = links.diagonal(first_layer.astype(wire), 1)
        far1 = links.across(second_layer.astype(wire), 1)
        far = jnp.where(first, far0, far1).astype(dtype)
        return jnp.stack([jnp.where(low == 0, near, far), jnp.where(low == 0, far, near)])

    hidden_out = deliver(y0, y1, BF16, BF16)
    input_grads = deliver(g0, g1, BF16, F32)

    total = jnp.where(first, p0, p1) + links.sibling(jnp.where(first, p1, p0))
    quarter = total.shape[-1] // 2
    total = total[..., :quarter] + links.across(total[..., quarter:])
    prefix_grads = sum_over_dp(total)
    return hidden_out[None], input_grads[None], prefix_grads[None]


def whole_kernel(
    states, segment_ids, cotangent, qkv_weight, out_weight, up_weight, up_bias, down_weight,
    norm_gain, shift_vec, prefix,
):
    pack = jnp.concatenate([up_bias, norm_gain[0], shift_vec[0], jnp.zeros_like(up_bias)], 0).astype(F32)
    results = fused(
        lax.axis_size("dp"), states, cotangent, segment_ids, jnp.transpose(qkv_weight[0], (1, 0, 2)),
        out_weight[0], up_weight[0], down_weight[0], prefix[0], pack,
    )
    return tuple(r[None] for r in results)


def fits(mesh):
    dp = mesh.shape["dp"]
    return mesh.shape["tensor"] == 4 and dp > 1 and dp & (dp - 1) == 0


def solution(mesh):
    placed = (
        P(None, ("dp", "tensor"), None),
        P(None, "dp"),
        P(None, ("dp", "tensor"), None),
        P("section", None, None, "tensor"),
        P("section", "tensor", None),
        P("section", None, "tensor"),
        P("section", "tensor"),
        P("section", "tensor", None),
        P("section", None, None),
        P("section", None, None),
        P("section", None, None, "tensor"),
    )
    return jax.shard_map(
        whole_kernel if fits(mesh) else plain,
        mesh=mesh,
        in_specs=placed,
        out_specs=(
            P("section", None, ("dp", "tensor"), None),
            P("section", None, ("dp", "tensor"), None),
            P("section", None, None, "tensor"),
        ),
        check_vma=False,
    )
```

```python
import functools

import jax
import jax.numpy as jnp
from jax import lax
from jax.experimental import pallas as pl
from jax.experimental.pallas import tpu as pltpu
from jax.sharding import PartitionSpec as P

D = 1024
HEAD = 64
PAIR = 2 * HEAD
PREFIX = 64
LEN = 1024
SPAN = LEN // 32
LABELS = 128
HIDDEN = -1e30
F32 = jnp.float32
BF16 = jnp.bfloat16


def dot(a, b):
    return jnp.dot(a, b, preferred_element_type=F32)


def dot_t(a, b):
    return lax.dot_general(a, b, (((1,), (1,)), ((), ())), preferred_element_type=F32)


def head_lanes(rows, head):
    lanes = lax.broadcasted_iota(jnp.int32, (rows, PAIR), 1)
    return (lanes >= head * HEAD) & (lanes < (head + 1) * HEAD)


def fill_keys(keys, own, sib, pre, own_lab, sib_lab):
    rows = own.shape[0]
    keys[:rows, :PAIR] = own[...]
    keys[rows : 2 * rows, :PAIR] = sib[...]
    keys[2 * rows :, :PAIR] = pre[...]
    keys[:rows, PAIR:] = own_lab[...]
    keys[rows : 2 * rows, PAIR:] = sib_lab[...]
    keys[2 * rows :, PAIR:] = jnp.zeros((PREFIX, LABELS), BF16)


def attend_kernel(block, q, ko, vo, ks, vs, kp, vp, lab_q, lab_o, lab_s, out, lse, keys, vals_t):
    rows = q.shape[0]
    fill_keys(keys, ko, ks, kp, lab_o, lab_s)
    vals_t[:, :rows] = vo[...].T
    vals_t[:, rows : 2 * rows] = vs[...].T
    vals_t[:, 2 * rows :] = vp[...].T
    for start in range(0, rows, block):
        part = pl.ds(start, block)
        query = q[part, :] * 0.125
        label = lab_q[part, :]
        results = []
        for head in range(2):
            mine = jnp.where(head_lanes(block, head), query, 0)
            scores = dot_t(keys[...], jnp.concatenate([mine, label], 1))
            peak = jnp.max(scores, axis=0, keepdims=True)
            weights = jnp.exp(scores - peak)
            total = jnp.sum(weights, axis=0, keepdims=True)
            merged = dot(vals_t[head * HEAD : (head + 1) * HEAD, :], weights.astype(BF16))
            results.append(merged / total)
            lse[0, head : head + 1, part] = peak + jnp.log(total)
        out[part, :] = jnp.concatenate(results, 0).T.astype(BF16)


def attend_back_kernel(
    block, q, ko, vo, ks, vs, kp, vp, lab_q, lab_o, lab_s, out, lse, grad,
    dq, dko, dvo, dks, dvs, dkp, dvp, keys, vals, keys_t, dk_sum, dv_sum,
):
    rows = q.shape[0]
    fill_keys(keys, ko, ks, kp, lab_o, lab_s)
    vals[:rows, :] = vo[...]
    vals[rows : 2 * rows, :] = vs[...]
    vals[2 * rows :, :] = vp[...]
    keys_t[:, :rows] = ko[...].T
    keys_t[:, rows : 2 * rows] = ks[...].T
    keys_t[:, 2 * rows :] = kp[...].T
    for start in range(0, rows, block):
        part = pl.ds(start, block)
        query = q[part, :] * 0.125
        label = lab_q[part, :]
        grad_part = grad[part, :]
        product = (grad_part.astype(F32) * out[part, :].astype(F32)).T
        queries, grads, weights_all, scores_all, results = [], [], [], [], []
        for head in range(2):
            span = slice(head * HEAD, (head + 1) * HEAD)
            mine = jnp.where(head_lanes(block, head), query, 0)
            mine_grad = jnp.where(head_lanes(block, head), grad_part, 0)
            scores = dot_t(keys[...], jnp.concatenate([mine, label], 1))
            weights = jnp.exp(scores - lse[0, head : head + 1, part])
            delta = jnp.sum(product[span], axis=0, keepdims=True)
            grad_scores = (weights * (dot_t(vals[...], mine_grad) - delta)).astype(BF16)
            results.append(dot(keys_t[span, :], grad_scores))
            queries.append(mine)
            grads.append(mine_grad)
            weights_all.append(weights.astype(BF16))
            scores_all.append(grad_scores)
        dq[part, :] = (jnp.concatenate(results, 0).T * 0.125).astype(BF16)
        dv_part = dot(jnp.concatenate(weights_all, 1), jnp.concatenate(grads, 0))
        dk_part = dot(jnp.concatenate(scores_all, 1), jnp.concatenate(queries, 0))
        if start == 0:
            dv_sum[...] = dv_part
            dk_sum[...] = dk_part
        else:
            dv_sum[...] += dv_part
            dk_sum[...] += dk_part
    dko[...] = dk_sum[:rows, :]
    dvo[...] = dv_sum[:rows, :]
    dks[...] = dk_sum[rows : 2 * rows, :].astype(BF16)
    dvs[...] = dv_sum[rows : 2 * rows, :].astype(BF16)
    dkp[...] = dk_sum[2 * rows :, :]
    dvp[...] = dv_sum[2 * rows :, :]


def attention_specs(rows, pairs):
    def column(height, offset):
        return pl.BlockSpec((height, PAIR), lambda p: (0, offset + p))

    labels = pl.BlockSpec((rows, LABELS), lambda p: (0, 0))
    ins = [
        column(rows, 0), column(rows, pairs), column(rows, 2 * pairs),
        column(rows, 0), column(rows, pairs),
        column(PREFIX, 0), column(PREFIX, 0),
        labels, labels, labels,
    ]
    return column, ins, pl.BlockSpec((1, 8, rows), lambda p: (p, 0, 0))


def attend(qkv, kv_sib, pre, labels):
    rows, width = qkv.shape[0], qkv.shape[1] // 3
    pairs = width // PAIR
    column, ins, lse_spec = attention_specs(rows, pairs)
    size = 2 * rows + PREFIX
    return pl.pallas_call(
        functools.partial(attend_kernel, min(rows, 256)),
        grid=(pairs,),
        in_specs=ins,
        out_specs=[column(rows, 0), lse_spec],
        out_shape=[
            jax.ShapeDtypeStruct((rows, width), BF16),
            jax.ShapeDtypeStruct((pairs, 8, rows), F32),
        ],
        scratch_shapes=[pltpu.VMEM((size, PAIR + LABELS), BF16), pltpu.VMEM((PAIR, size), BF16)],
        compiler_params=pltpu.CompilerParams(vmem_limit_bytes=40 << 20),
        cost_estimate=pl.CostEstimate(
            flops=2 * 2 * rows * size * width, transcendentals=rows * size * width // HEAD,
            bytes_accessed=16 * rows * width,
        ),
        name="attend",
    )(qkv, qkv, qkv, kv_sib, kv_sib, pre[0], pre[1], *labels)


def attend_back(qkv, kv_sib, pre, labels, merged, lse, grad):
    rows, width = qkv.shape[0], qkv.shape[1] // 3
    pairs = width // PAIR
    column, ins, lse_spec = attention_specs(rows, pairs)
    size = 2 * rows + PREFIX
    shape = jax.ShapeDtypeStruct
    return pl.pallas_call(
        functools.partial(attend_back_kernel, min(rows, 256)),
        grid=(pairs,),
        in_specs=ins + [column(rows, 0), lse_spec, column(rows, 0)],
        out_specs=[column(rows, 0)] * 5 + [column(PREFIX, 0)] * 2,
        out_shape=[
            shape((rows, width), BF16),
            shape((rows, width), F32), shape((rows, width), F32),
            shape((rows, width), BF16), shape((rows, width), BF16),
            shape((PREFIX, width), F32), shape((PREFIX, width), F32),
        ],
        scratch_shapes=[
            pltpu.VMEM((size, PAIR + LABELS), BF16), pltpu.VMEM((size, PAIR), BF16),
            pltpu.VMEM((PAIR, size), BF16), pltpu.VMEM((size, PAIR), F32), pltpu.VMEM((size, PAIR), F32),
        ],
        compiler_params=pltpu.CompilerParams(vmem_limit_bytes=40 << 20),
        cost_estimate=pl.CostEstimate(
            flops=5 * 2 * rows * size * width, transcendentals=rows * size * width // HEAD,
            bytes_accessed=32 * rows * width,
        ),
        name="attend_back",
    )(qkv, qkv, qkv, kv_sib, kv_sib, pre[0], pre[1], *labels, merged, lse, grad)


def norm_stats(values):
    center = values - jnp.mean(values, axis=-1, keepdims=True)
    scale = lax.rsqrt(jnp.mean(center * center, axis=-1, keepdims=True) + 1e-05)
    return center * scale, scale


def norm_back(grad, gain, normed, scale):
    dn = grad * gain
    return scale * (
        dn
        - jnp.mean(dn, axis=-1, keepdims=True)
        - normed * jnp.mean(dn * normed, axis=-1, keepdims=True)
    )


def gelu_pair(u):
    cdf = 0.5 * (1.0 + lax.erf(u * 0.7071067811865476))
    pdf = jnp.exp(-0.5 * u * u) * 0.3989422804014327
    return (u * cdf).astype(BF16), (cdf + u * pdf).astype(BF16)


MESH = pl.DeviceIdType.MESH
ROWS = 256
CORE = 2 * ROWS
CHUNK = 128
PART = 64
STEPS = ROWS // CHUNK
QUARTER = D // 4
UNITS = D
TILE = 256
PAIRS = 4
KEYS = 2 * CORE + PREFIX
SEMS = 224


def gelu_both(u):
    size = jnp.abs(u) * 0.7071067811865476
    t = 1.0 / (1.0 + 0.3275911 * size)
    poly = t * (0.254829592 + t * (-0.284496736 + t * (1.421413741 + t * (-1.453152027 + t * 1.061405429))))
    bell = jnp.exp(-(size * size))
    tail = 0.5 * poly * bell
    cdf = jnp.where(u >= 0, 1.0 - tail, tail)
    return (u * cdf).astype(BF16), (cdf + u * (bell * 0.3989422804014327)).astype(BF16)


def norm_chunk(values):
    center = values - jnp.mean(values, axis=-1, keepdims=True)
    scale = lax.rsqrt(jnp.mean(center * center, axis=-1, keepdims=True) + 1e-05)
    return center * scale, scale


class Copies:
    def __init__(self, send, arrive, here):
        self.send, self.arrive, self.here = send, arrive, here
        self.remotes = self.locals = 0

    def remote(self, src, dst, device, number=None):
        if number is None:
            number = self.remotes
            self.remotes += 1
        copy = pltpu.make_async_remote_copy(
            src_ref=src, dst_ref=dst, send_sem=self.send.at[number], recv_sem=self.arrive.at[number],
            device_id=device, device_id_type=MESH,
        )
        return copy, number

    def local(self, src, dst, number=None):
        if number is None:
            number = self.locals
            self.locals += 1
        return pltpu.make_async_copy(src, dst, self.here.at[number])


def fused_kernel(
    dp,
    states, cotangent, segments, qkv, out_w, up_w, down_w, pre, pack,
    hidden, grads, pgrads, gup, gdown,
    xb, xg, cot, lab_q, lab_k, qw, ow, uw, dw, pw, pk,
    qs, kv, kvs, mg, lse, n1, r1, n2, r2, slopes,
    mid, acc, act, mrecv, fsnd, fin, fout, fret, gfirst, gm, gms, gout,
    keys, turned, vals, dk_acc, dv_acc, dq, dkv, dkv_send, dkv_recv, dxs, dxr, pacc, psib, pacross, psum, pdp,
    send_sem, arrive_sem, here_sem,
):
    core, z, place = lax.axis_index("section"), lax.axis_index("dp"), lax.axis_index("tensor")
    low, high = lax.rem(place, 2), place // 2
    across = place + 1 - 2 * low
    along = lax.rem(place + 2, 4)
    sib_dev = {"section": 1 - core}
    x_dev, y_dev = {"tensor": across}, {"tensor": along}
    diag_dev = {"section": 1 - core, "tensor": across}

    def dp_dev(step):
        return {"dp": z + step - 2 * step * lax.rem(z // step, 2)}

    dp_steps = []
    while (1 << len(dp_steps)) < dp:
        dp_steps.append(1 << len(dp_steps))
    z_dev = dp_dev(1)
    wires = Copies(send_sem, arrive_sem, here_sem)
    pending = []

    barrier = pltpu.get_barrier_semaphore()
    greeted = [sib_dev, x_dev, y_dev, diag_dev] + [dp_dev(s) for s in dp_steps]
    for device in greeted:
        pl.semaphore_signal(barrier, inc=1, device_id=device, device_id_type=MESH)
    pl.semaphore_wait(barrier, len(greeted))

    class Own:
        def __init__(self, layer, src, dst):
            self.layer = layer
            self.here = wires.local(src, dst)
            self.first = wires.remote(src, dst, sib_dev)[0]

        def start(self):
            @pl.when(core == self.layer)
            def _():
                self.here.start()
                self.first.start()

        def need(self):
            @pl.when(core == self.layer)
            def _():
                self.here.wait()

            @pl.when(core != self.layer)
            def _():
                self.first.wait_recv()

        def finish(self):
            @pl.when(core == self.layer)
            def _():
                self.first.wait_send()

    class Away:
        def __init__(self, layer, src, dst):
            self.layer = layer
            self.first = wires.remote(src, dst, sib_dev)[0]

        def start(self):
            @pl.when(core == self.layer)
            def _():
                self.first.start()

        def need(self):
            @pl.when(core != self.layer)
            def _():
                self.first.wait_recv()

        def finish(self):
            @pl.when(core == self.layer)
            def _():
                self.first.wait_send()

    class Direct:
        def __init__(self, layer, src, dst, dev):
            self.layer = layer
            self.over = wires.remote(src, dst, dev)[0]
            self.rest = wires.remote(dst, dst, sib_dev)[0]

        def start(self):
            @pl.when(core == self.layer)
            def _():
                self.over.start()

        def forward(self):
            @pl.when(core == self.layer)
            def _():
                self.over.wait_recv()
                self.rest.start()

        def need(self):
            @pl.when(core != self.layer)
            def _():
                self.rest.wait_recv()

        def finish(self):
            @pl.when(core == self.layer)
            def _():
                self.over.wait_send()
                self.rest.wait_send()

    class Shared:
        def __init__(self, layer, src, dst, mine, theirs, dev):
            self.layer = layer
            self.over = wires.remote(src.at[mine], dst.at[mine], dev)[0]
            self.dp, number = wires.remote(dst.at[mine], dst.at[mine], z_dev)
            self.dp_in = wires.remote(dst.at[theirs], dst.at[theirs], z_dev, number)[0]
            self.rest = wires.remote(dst.at[mine], dst.at[mine], sib_dev)[0]
            self.last = wires.remote(dst.at[theirs], dst.at[theirs], sib_dev)[0]

        def start(self):
            @pl.when(core == self.layer)
            def _():
                self.over.start()

        def forward(self):
            @pl.when(core == self.layer)
            def _():
                self.over.wait_recv()
                self.dp.start()
                self.rest.start()

        def forward_last(self):
            @pl.when(core == self.layer)
            def _():
                self.dp_in.wait_recv()
                self.last.start()

        def need(self):
            @pl.when(core != self.layer)
            def _():
                self.rest.wait_recv()
                self.last.wait_recv()

        def finish(self):
            @pl.when(core == self.layer)
            def _():
                for c in (self.over, self.dp, self.rest, self.last):
                    c.wait_send()

    odd = lax.rem(z, 2)

    def halves(size, pieces):
        places, at = [], 0
        for piece in pieces:
            places.append(
                tuple(pl.ds(pl.multiple_of(parity_z * (size // 2) + at, 16), piece) for parity_z in (odd, 1 - odd))
            )
            at += piece
        return places

    class Layer:
        def __init__(self, layer):
            self.heads_own = Own(layer, qkv, qw.at[layer, 0])
            self.small_own = [Own(layer, pre, pw.at[layer, 0]), Own(layer, pack, pk.at[layer, 0])]
            self.out_own = Own(layer, out_w, ow.at[layer, 0])
            self.units_own = [Away(layer, up_w, gup.at[layer, 0]), Away(layer, down_w, gdown.at[layer, 0])]
            if layer == 0:
                (mine, theirs), = halves(D, [D // 2])
                self.heads = [
                    Shared(layer, qkv.at[i], qw.at[layer, 1, i], mine, theirs, x_dev) for i in range(3)
                ]
            else:
                self.heads = [Direct(layer, qkv, qw.at[layer, 1], x_dev)]
            self.small = [Direct(layer, pre, pw.at[layer, 1], x_dev), Direct(layer, pack, pk.at[layer, 1], y_dev)]
            self.out_x = Direct(layer, out_w, ow.at[layer, 1], x_dev)
            (mine, theirs), = halves(QUARTER, [QUARTER // 2])
            self.out_y = [
                Shared(layer, out_w, ow.at[layer, 2], mine, theirs, y_dev),
                Shared(layer, ow.at[layer, 1], ow.at[layer, 3], mine, theirs, y_dev),
            ]
            self.units = [
                Shared(layer, src, dst.at[layer, 1], mine, theirs, y_dev)
                for src, dst, pieces in ((up_w, gup, [256, 256]), (down_w, gdown, [256, 128, 128]))
                for mine, theirs in halves(UNITS, pieces)
            ]

        def everything(self):
            return (
                [self.heads_own, self.out_own, self.out_x] + self.small_own + self.units_own + self.heads + self.small
                + self.out_y + self.units
            )

    layers = [Layer(0), Layer(1)]

    def each(items, action):
        for item in items:
            getattr(item, action)()

    loads = {}

    def load(layer, slot, array, when):
        spread, native, dst = ((gup, up_w, uw), (gdown, down_w, dw))[array]
        copy = wires.local(spread.at[layer, slot], dst.at[slot])
        loads[layer, slot, array, when] = copy
        if slot == 0:
            mine = wires.local(native, dst.at[0], wires.locals - 1)

            @pl.when(core == layer)
            def _():
                mine.start()

            @pl.when(core != layer)
            def _():
                copy.start()
        else:
            copy.start()

    def loaded(layer, slot, array, when):
        loads[layer, slot, array, when].wait()

    def chunk_rows(step):
        return pl.ds(step * CHUNK, CHUNK)

    class Tokens:
        def __init__(self, source, dest):
            self.near = [wires.local(source.at[low, chunk_rows(i)], dest.at[chunk_rows(i)]) for i in range(STEPS)]
            self.far = [
                wires.remote(source.at[1 - low, chunk_rows(i)], dest.at[chunk_rows(i)], x_dev)[0] for i in range(STEPS)
            ]

        def start(self):
            @pl.when(core == 0)
            def _():
                for c in self.near:
                    c.start()

            @pl.when(core == 1)
            def _():
                for c in self.far:
                    c.start()

        def wait(self, step):
            @pl.when(core == 0)
            def _():
                self.near[step].wait()

            @pl.when(core == 1)
            def _():
                self.far[step].wait_recv()

        def finish(self):
            @pl.when(core == 1)
            def _():
                for c in self.far:
                    c.wait_send()

    tokens = Tokens(states, xb.at[0])
    ends = Tokens(cotangent, cot)

    first = layers[0]
    tokens.start()
    each([first.heads_own] + first.small_own, "start")
    each(first.heads + first.small, "start")
    each([first.out_own] + first.units_own, "start")

    def send_chunk(src, dst, device):
        copy, _ = wires.remote(src, dst, device)
        copy.start()
        return copy

    gathers = {}

    def gather_x(layer, step):
        gathers[layer, step] = send_chunk(
            xb.at[layer, chunk_rows(step)], xg.at[chunk_rows(step)], y_dev
        )

    for step in range(STEPS):
        tokens.wait(step)
        gather_x(0, step)

    each(first.units[:2], "start")

    parity = low + core - 2 * low * core
    row = segments[pl.ds(low, 1), :]
    last = row[:, LEN - 1 :]

    def block_labels(block):
        ids = last - segments[pl.ds(low, 1), pl.ds(pl.multiple_of(block * ROWS, ROWS), ROWS)]
        numbers = lax.broadcasted_iota(jnp.int32, (LABELS, ROWS), 0)
        same = jnp.where(numbers == ids, 1.0, 0.0)
        return same.T, jnp.where(numbers <= 2 * SPAN, HIDDEN * (1.0 - same), 0.0).T

    for index, (h, p) in enumerate(((high, parity), (1 - high, parity), (high, 1 - parity), (1 - high, 1 - parity))):
        same, differ = block_labels(2 * h + p)
        if index < 2:
            lab_q[pl.ds(index * ROWS, ROWS), :] = same.astype(BF16)
        lab_k[pl.ds(index * ROWS, ROWS), :] = differ.astype(BF16)

    def project(layer, source, start, size, slots=(0, 1)):
        for slot in slots:
            columns = slice(slot * QUARTER, (slot + 1) * QUARTER)
            rows = pl.ds(start, size)
            qs[layer, rows, columns] = dot(source, qw[layer, slot, 0]).astype(BF16)
            kv[layer, rows, columns] = dot(source, qw[layer, slot, 1]).astype(BF16)
            kv[layer, rows, slice(CORE + columns.start, CORE + columns.stop)] = dot(
                source, qw[layer, slot, 2]
            ).astype(BF16)

    def lanes(index, base=0):
        return slice(base + index * PAIR, base + (index + 1) * PAIR)

    def fill_keys(layer):
        for p in range(PAIRS):
            keys[p, :CORE, :PAIR] = kv[layer, :, lanes(p)]
            keys[p, CORE : 2 * CORE, :PAIR] = kvs[layer, :, lanes(p)]
            keys[p, 2 * CORE :, :PAIR] = pw[layer, p // 2, 0, :, lanes(p % 2)]

    def pair_values(layer, p):
        return kv[layer, :, lanes(p, CORE)], kvs[layer, :, lanes(p, CORE)], pw[layer, p // 2, 1, :, lanes(p % 2)]

    def fill_turned(p, own, sib, prefix):
        turned[p, :, :CORE] = own.T
        turned[p, :, CORE : 2 * CORE] = sib.T
        turned[p, :, 2 * CORE :] = prefix.T

    def fill_forward(layer):
        fill_keys(layer)
        for p in range(PAIRS):
            fill_turned(p, *pair_values(layer, p))

    def fill_backward(layer):
        if layer == 0:
            fill_keys(layer)
        for p in range(PAIRS):
            own, sib, prefix = pair_values(layer, p)
            vals[p, :CORE, :] = own
            vals[p, CORE : 2 * CORE, :] = sib
            vals[p, 2 * CORE :, :] = prefix
            fill_turned(p, keys[p, :CORE, :PAIR], keys[p, CORE : 2 * CORE, :PAIR], keys[p, 2 * CORE :, :PAIR])

    for p in range(PAIRS):
        keys[p, : 2 * CORE, PAIR:] = lab_k[...]
        keys[p, 2 * CORE :, PAIR:] = jnp.zeros((PREFIX, LABELS), BF16)

    def both_heads(values):
        return jnp.concatenate([jnp.where(head_lanes(CHUNK, h), values, 0) for h in range(2)], 0)

    def score_chunk(layer, start, p):
        rows = pl.ds(start, CHUNK)
        queries = both_heads(qs[layer, rows, lanes(p)] * 0.125)
        label = lab_q[rows, :]
        return queries, dot_t(keys[p], jnp.concatenate([queries, jnp.concatenate([label, label], 0)], 1))

    def untangle(both):
        return jnp.concatenate([both[:HEAD, :CHUNK], both[HEAD:, CHUNK:]], 0).T

    def attend_chunks(layer, steps):
        blocks = [(p, start, action if p + 1 == PAIRS else None) for start, action in steps for p in range(PAIRS)]
        ahead = score_chunk(layer, blocks[0][1], 0)
        for index, (p, start, action) in enumerate(blocks):
            rows, at = pl.ds(start, CHUNK), start // CHUNK
            _, scores = ahead
            if index + 1 < len(blocks):
                ahead = score_chunk(layer, blocks[index + 1][1], blocks[index + 1][0])
            peak = jnp.max(scores, axis=0, keepdims=True)
            weights = jnp.exp(scores - peak)
            total = jnp.sum(weights, axis=0, keepdims=True)
            merged = dot(turned[p], weights.astype(BF16)) * (1.0 / total)
            lse[layer, p, at : at + 1, :] = peak + jnp.log(total)
            mg[layer, rows, lanes(p)] = untangle(merged).astype(BF16)
            if action is not None:
                action()

    def attend_chunks_back(layer, starts, fresh, done=None):
        def begin(p, start):
            rows = pl.ds(start, CHUNK)
            queries, scores = score_chunk(layer, start, p)
            grad_both = both_heads(gm[rows, lanes(p)])
            return queries, scores, grad_both, dot_t(vals[p], grad_both)

        blocks = [(p, start) for p in range(PAIRS) for start in starts]
        ahead = begin(*blocks[0])
        kept = []
        for index, (p, start) in enumerate(blocks):
            rows, at = pl.ds(start, CHUNK), start // CHUNK
            queries, scores, grad_both, grad_weights = ahead
            if index + 1 < len(blocks):
                ahead = begin(*blocks[index + 1])
            product = (gm[rows, lanes(p)].astype(F32) * mg[layer, rows, lanes(p)].astype(F32)).T
            delta = jnp.concatenate(
                [jnp.sum(product[h * HEAD : (h + 1) * HEAD], axis=0, keepdims=True) for h in range(2)], 1
            )
            weights = jnp.exp(scores - lse[layer, p, at : at + 1, :])
            grad_scores = (weights * (grad_weights - delta)).astype(BF16)
            dq[rows, lanes(p)] = (untangle(dot(turned[p], grad_scores)) * 0.125).astype(BF16)
            kept.append((weights.astype(BF16), grad_both, grad_scores, queries))
            if len(kept) == len(starts):
                joined = [jnp.concatenate([k[i] for k in kept], 1 - i % 2) for i in range(4)]
                dv_part, dk_part = dot(joined[0], joined[1]), dot(joined[2], joined[3])
                if fresh:
                    dv_acc[:, lanes(p)] = dv_part
                    dk_acc[:, lanes(p)] = dk_part
                else:
                    dv_acc[:, lanes(p)] += dv_part
                    dk_acc[:, lanes(p)] += dk_part
                kept = []
                if done is not None:
                    done(p)

    def vector(layer, index):
        return pk[layer, 0, index : index + 1, :]

    def keep_norm(store, scales, layer, rows, normed, scale):
        store[layer, rows, :] = normed.astype(BF16)
        scales[layer, rows, :] = jnp.broadcast_to(scale, (CHUNK, PAIR))

    def forward_attention(layer):
        this, later = layers[layer], layers[1]
        if layer == 0:
            this.heads_own.need()
            project(0, xb[0], 0, ROWS, (0,))
            each(this.heads + this.small, "forward")
            this.out_x.start()
            this.out_y[0].start()
            for step in range(STEPS):
                gathers[0, step].wait_recv()
                project(0, xg[chunk_rows(step), :], ROWS + step * CHUNK, CHUNK, (0,))
            each(this.units[:2], "forward")
            this.out_x.forward()
            this.out_y[1].start()
            each(later.heads + later.small + [later.out_x], "start")
            each(this.units[2:], "start")
            each(this.heads, "forward_last")
            each(this.heads + this.small_own + this.small, "need")
            project(0, xb[0], 0, ROWS, (1,))
            sent = [send_chunk(kv.at[0, :ROWS], kvs.at[0, :ROWS], sib_dev)]
            project(0, xg[...], ROWS, ROWS, (1,))
            sent.append(send_chunk(kv.at[0, ROWS:], kvs.at[0, ROWS:], sib_dev))
        else:
            each([this.heads_own] + this.heads + this.small_own + this.small, "need")
            project(1, xb[1], 0, ROWS)
            sent = [send_chunk(kv.at[1, :ROWS], kvs.at[1, :ROWS], sib_dev)]
            for step in range(STEPS):
                gathers[1, step].wait_recv()
                project(1, xg[chunk_rows(step), :], ROWS + step * CHUNK, CHUNK)
            sent.append(send_chunk(kv.at[1, ROWS:], kvs.at[1, ROWS:], sib_dev))
        for c in sent:
            c.wait_recv()
        fill_forward(layer)
        swaps, copies = [], []

        def swap(step):
            rows = pl.ds(ROWS + step * CHUNK, CHUNK)
            swaps.append(send_chunk(mg.at[layer, rows], mrecv.at[chunk_rows(step)], y_dev))

        def finish(step):
            swaps[step].wait_recv()
            rows = chunk_rows(step)
            parts = [mg[layer, rows, :QUARTER], mg[layer, rows, QUARTER:], mrecv[rows, :QUARTER], mrecv[rows, QUARTER:]]
            total = xb[layer, rows, :].astype(F32) + vector(layer, 3)
            for i, part in enumerate(parts):
                total = total + dot(part, ow[layer, i])
            normed, scale = norm_chunk(total)
            keep_norm(n1, r1, layer, rows, normed, scale)
            middle = normed * vector(layer, 1) + vector(layer, 4)
            mid[rows, :] = middle
            fsnd[rows, :] = middle.astype(BF16)
            copies.append(send_chunk(fsnd.at[rows], fin.at[rows], x_dev))

        def first_peer():
            swap(0)
            if layer == 0:
                each(this.out_y, "forward")
            else:
                ends.start()

        def first_own():
            if layer == 0:
                this.units[2].forward()

        def second_peer():
            swap(1)
            each(this.out_y, "forward_last")
            each([this.out_own, this.out_x] + this.out_y, "need")
            finish(0)

        def second_own():
            finish(1)
            if layer == 0:
                each(this.units[3:], "forward")
                each(later.units[:2], "start")

        attend_chunks(
            layer, [(ROWS, first_peer), (0, first_own), (ROWS + CHUNK, second_peer), (CHUNK, second_own)]
        )
        each(this.units_own, "need")
        load(layer, 0, 0, 0)
        load(layer, 0, 1, 0)
        for c in sent + swaps:
            c.wait_send()

        def gathered():
            for step in range(STEPS):
                gathers[layer, step].wait_send()

        gathered()
        return copies

    def tiles(count, body):
        def two(j, _):
            body(2 * j, 0)
            return body(2 * j + 1, 0)

        lax.fori_loop(0, count // 2, two, 0)

    def feed_rows(layer, slot, source, start, store):
        size = source.shape[0]

        def up_tile(j, _):
            columns = pl.ds(pl.multiple_of(j * TILE, TILE), TILE)
            wide = pl.ds(pl.multiple_of(slot * UNITS + j * TILE, TILE), TILE)
            u = dot(source[...], uw[slot, :, columns]) + pk[layer, slot, 0:1, columns]
            store[:, columns], slopes[layer, pl.ds(start, size), wide] = gelu_both(u)
            return 0

        tiles(UNITS // TILE, up_tile)

    def feed_rows_back(layer, source, start, size):
        def tile(j, _):
            slot, units_at = j // 4, pl.ds(pl.multiple_of(lax.rem(j, 4) * TILE, TILE), TILE)
            wide = pl.ds(pl.multiple_of(j * TILE, TILE), TILE)
            u = dot_t(source[...], dw[slot, units_at, :]) * slopes[layer, pl.ds(start, size), wide].astype(F32)
            act[:size, wide] = u.astype(BF16)
            return 0

        tiles(2 * UNITS // TILE, tile)

    def feed_out(store, acts, back):
        def tile(j, _):
            columns = pl.ds(pl.multiple_of(j * TILE, TILE), TILE)
            if back:
                u = dot_t(acts[0][...], uw[0, columns, :]) + dot_t(acts[1][...], uw[1, columns, :])
            else:
                u = dot(acts[0][...], dw[0, :, columns]) + dot(acts[1][...], dw[1, :, columns])
            store[:, columns] = u.astype(store.dtype)
            return 0

        tiles(D // TILE, tile)

    def act_slots(size):
        return [act.at[pl.ds(0, size), pl.ds(slot * UNITS, UNITS)] for slot in range(2)]

    def feed_forward(layer, copies, finish, arrivals):
        this = layers[layer]
        mine = act_slots(ROWS)
        theirs = [[dkv.at[pl.ds(slot * ROWS + step * CHUNK, CHUNK)] for slot in range(2)] for step in range(STEPS)]

        def feed_peer(slot, step):
            feed_rows(layer, slot, fin.at[chunk_rows(step)], ROWS + step * CHUNK, theirs[step][slot])

        loaded(layer, 0, 0, 0)
        feed_rows(layer, 0, fsnd, 0, mine[0])
        for step in range(STEPS):
            copies[step].wait_recv()
            feed_peer(0, step)
            arrivals[step]()
        each(this.units[:2], "forward_last")
        each(this.units[:2], "need")
        load(layer, 1, 0, 0)
        loaded(layer, 1, 0, 0)
        for step in range(STEPS):
            feed_peer(1, step)
        each(this.units[2:], "forward_last")
        each(this.units[2:], "need")
        load(layer, 1, 1, 0)
        loaded(layer, 0, 1, 0)
        loaded(layer, 1, 1, 0)
        returned = []
        for step in range(STEPS):
            rows = chunk_rows(step)
            feed_out(fout.at[rows], theirs[step], False)
            returned.append(send_chunk(fout.at[rows], fret.at[rows], x_dev))
        feed_rows(layer, 1, fsnd, 0, mine[1])
        feed_out(acc, mine, False)
        arrivals[STEPS]()
        for c in copies:
            c.wait_send()
        for step in range(STEPS):
            returned[step].wait_recv()
            finish(step, chunk_rows(step), acc[chunk_rows(step), :] + fret[chunk_rows(step), :].astype(F32))
        for c in returned:
            c.wait_send()

    def feed_back(layer, copies, finish, between):
        feed_rows_back(layer, fsnd, 0, ROWS)
        feed_out(acc, act_slots(ROWS), True)
        returned = []
        per = len(copies) // STEPS
        for step in range(STEPS):
            rows = chunk_rows(step)
            for c in copies[step * per : (step + 1) * per]:
                c.wait_recv()
            feed_rows_back(layer, fin.at[rows], ROWS + step * CHUNK, CHUNK)
            feed_out(fout.at[rows], act_slots(CHUNK), True)
            returned.append(send_chunk(fout.at[rows], fret.at[rows], x_dev))
        between()
        for step in range(STEPS):
            returned[step].wait_recv()
            finish(step, chunk_rows(step), acc[chunk_rows(step), :] + fret[chunk_rows(step), :].astype(F32))
        for c in copies + returned:
            c.wait_send()

    deliveries = []
    later_deliveries = []

    def deliver(layer, source, dest, rows, now=False):
        far, number = wires.remote(source.at[rows], dest.at[low, rows], {"section": layer, "tensor": across})
        far_in, _ = wires.remote(source.at[rows], dest.at[1 - low, rows], {"section": layer, "tensor": across}, number)
        if layer == 0:
            near = wires.local(source.at[rows], dest.at[low, rows])
        else:
            near, _ = wires.remote(source.at[rows], dest.at[low, rows], sib_dev)

        def start():
            @pl.when(core == 0)
            def _():
                near.start()

            @pl.when(core == 1)
            def _():
                far.start()

        if now:
            start()
        else:
            later_deliveries.append(start)

        def sent():
            @pl.when(core == 0)
            def _():
                near.wait() if layer == 0 else near.wait_send()

            @pl.when(core == 1)
            def _():
                far.wait_send()

        def arrived():
            @pl.when(core == layer)
            def _():
                far_in.wait_recv()
                if layer == 1:
                    near.wait_recv()

        deliveries.append(arrived)
        return sent

    def start_back(layer, rows, grad):
        normed, scale = n2[layer, rows, :].astype(F32), r2[layer, rows, :1]
        value = norm_back(grad, vector(layer, 2), normed, scale)
        mid[rows, :] = value
        fsnd[rows, :] = value.astype(BF16)
        return send_chunk(fsnd.at[rows], fin.at[rows], x_dev)

    unsent = []
    back_copies = []

    def forward_finish(layer):
        def finish(step, rows, branch):
            normed, scale = norm_chunk(mid[rows, :] + branch + vector(layer, 5))
            keep_norm(n2, r2, layer, rows, normed, scale)
            xb[layer + 1, rows, :] = (normed * vector(layer, 2) + vector(layer, 6)).astype(BF16)
            if layer == 0:
                gather_x(1, step)
            unsent.append(deliver(layer, xb.at[layer + 1], hidden, rows))
            if layer == 1:
                ends.wait(step)
                back_copies.append(start_back(1, rows, cot[rows, :].astype(F32)))

        return finish

    second = layers[1]

    def first_arrivals():
        each(second.heads + second.small, "forward")
        second.out_x.forward()
        each(second.units[2:], "start")
        each(second.out_y, "start")

    def later_arrivals():
        each([second.heads_own] + second.small_own + [second.out_own] + second.units_own, "start")
        each(second.units[:2], "forward")

    def after_units():
        each(second.out_y, "forward")
        each(second.units[2:], "forward")

    copies = forward_attention(0)
    feed_forward(0, copies, forward_finish(0), [first_arrivals, later_arrivals, after_units])
    copies = forward_attention(1)
    feed_forward(1, copies, forward_finish(1), [lambda: None] * 3)

    grad_sent = []

    def backward(layer, copies):
        swaps = []

        def finish(step, rows, term):
            middle = mid[rows, :] + term
            first = norm_back(middle, vector(layer, 1), n1[layer, rows, :].astype(F32), r1[layer, rows, :1])
            gfirst[rows, :] = first
            low_first = first.astype(BF16)
            for i in range(4):
                part = dot_t(low_first, ow[layer, i]).astype(BF16)
                columns = slice((i % 2) * QUARTER, (i % 2 + 1) * QUARTER)
                if i < 2:
                    gm[rows, columns] = part
                else:
                    gms[rows, columns] = part
            swaps.append(send_chunk(gms.at[rows], gm.at[pl.ds(ROWS + step * CHUNK, CHUNK)], y_dev))

            attend_chunks_back(layer, [step * CHUNK], step == 0)

        def between():
            if layer == 1:
                for slot in range(2):
                    for array in range(2):
                        load(0, slot, array, 1)
            fill_backward(layer)

        feed_back(layer, copies, finish, between)
        for d in later_deliveries:
            d()
        later_deliveries.clear()
        for c in swaps:
            c.wait_recv()
        given = []

        def give(p):
            dkv_send[p, 0] = dk_acc[CORE : 2 * CORE, lanes(p)].astype(BF16)
            dkv_send[p, 1] = dv_acc[CORE : 2 * CORE, lanes(p)].astype(BF16)
            given.append(send_chunk(dkv_send.at[p], dkv_recv.at[layer, p], sib_dev))

        attend_chunks_back(layer, [ROWS, ROWS + CHUNK], False, give)
        pacc[layer, 0] = dk_acc[2 * CORE :, :]
        pacc[layer, 1] = dv_acc[2 * CORE :, :]
        if layer == 0:
            total = prefix_start()
        for p in range(PAIRS):
            given[p].wait_recv()
            dkv[:, lanes(p)] = (dk_acc[:CORE, lanes(p)] + dkv_recv[layer, p, 0].astype(F32)).astype(BF16)
            dkv[:, lanes(p, CORE)] = (dv_acc[:CORE, lanes(p)] + dkv_recv[layer, p, 1].astype(F32)).astype(BF16)

        def input_term(store, start, size):
            rows = pl.ds(start, size)

            def tile(j, _):
                features = pl.ds(pl.multiple_of(j * TILE, TILE), TILE)
                total = None
                for slot in range(2):
                    columns = slice(slot * QUARTER, (slot + 1) * QUARTER)
                    shifted = slice(CORE + slot * QUARTER, CORE + (slot + 1) * QUARTER)
                    for part, source in enumerate((dq[rows, columns], dkv[rows, columns], dkv[rows, shifted])):
                        term = dot_t(source, qw[layer, slot, part, features, :])
                        total = term if total is None else total + term
                store[:, features] = total.astype(store.dtype)
                return 0

            tiles(D // TILE, tile)

        returned = []
        for step in range(STEPS):
            input_term(dxs.at[chunk_rows(step)], ROWS + step * CHUNK, CHUNK)
            for part in range(CHUNK // PART):
                rows = pl.ds(step * CHUNK + part * PART, PART)
                returned.append(send_chunk(dxs.at[rows], dxr.at[rows], y_dev))
        if layer == 0:
            total.stage()
        input_term(acc, 0, ROWS)
        if layer == 1:
            for slot in range(2):
                for array in range(2):
                    loaded(0, slot, array, 1)
        else:
            total.stage()
        for sent in grad_sent:
            sent()
        grad_sent.clear()
        onward = []
        for step in range(ROWS // PART):
            rows = pl.ds(step * PART, PART)
            returned[step].wait_recv()
            value = gfirst[rows, :] + (acc[rows, :] + dxr[rows, :].astype(F32))
            gout[rows, :] = value
            grad_sent.append(deliver(layer, gout, grads, rows, layer == 0))
            if layer == 1:
                onward.append(start_back(0, rows, value.astype(BF16).astype(F32)))
            else:
                total.stage()
        for c in swaps + given + returned:
            c.wait_send()
        return onward

    class prefix_start:
        def __init__(self):
            self.sib = send_chunk(pacc.at[1 - core], psib, sib_dev)
            self.sent = [self.sib]
            self.at = 0

        def stage(self):
            if self.at > len(dp_steps) + 1:
                return
            if self.at == 0:
                self.sib.wait_recv()
                total = pacc[core] + psib[...]
                psum[0] = total[:, :, :QUARTER]
                pacross[0] = total[:, :, QUARTER:]
                self.next = send_chunk(pacross.at[0], pacross.at[1], x_dev)
                self.sent.append(self.next)
            else:
                self.next.wait_recv()
                arrived = pacross[1] if self.at == 1 else pdp[self.at - 2]
                psum[self.at] = psum[self.at - 1] + arrived
                if self.at <= len(dp_steps):
                    step = self.at - 1
                    self.next = send_chunk(psum.at[self.at], pdp.at[step], dp_dev(dp_steps[step]))
                    self.sent.append(self.next)
                else:
                    self.done = wires.local(psum.at[self.at], pgrads)
                    self.done.start()
            self.at += 1

        def finish(self):
            while self.at <= len(dp_steps) + 1:
                self.stage()
            for c in self.sent:
                c.wait_send()
            self.done.wait()

    holder = []
    start_class = prefix_start

    def prefix_start():
        holder.append(start_class())
        return holder[0]

    back_copies = backward(1, back_copies)
    backward(0, back_copies)
    holder[0].finish()
    for sent in unsent + grad_sent:
        sent()
    for arrived in deliveries:
        arrived()
    tokens.finish()
    ends.finish()
    for layer in layers:
        each(layer.everything(), "finish")


def fused(dp, states, cotangent, segments, qkv, out_w, up_w, down_w, pre, pack):
    shape = jax.ShapeDtypeStruct
    steps = dp.bit_length() - 1
    vmem = pltpu.VMEM
    scratch = [
        vmem((3, ROWS, D), BF16),
        vmem((ROWS, D), BF16),
        vmem((ROWS, D), BF16),
        vmem((CORE, LABELS), BF16), vmem((2 * CORE, LABELS), BF16),
        vmem((2, 2, 3, D, QUARTER), BF16),
        vmem((2, 4, QUARTER, D), BF16),
        vmem((2, D, UNITS), BF16), vmem((2, UNITS, D), BF16),
        vmem((2, 2, 2, PREFIX, QUARTER), BF16),
        vmem((2, 2, 8, D), F32),
        vmem((2, CORE, CORE), BF16), vmem((2, CORE, 2 * CORE), BF16), vmem((2, CORE, 2 * CORE), BF16),
        vmem((2, CORE, CORE), BF16), vmem((2, PAIRS, 8, 2 * CHUNK), F32),
        vmem((2, ROWS, D), BF16), vmem((2, ROWS, PAIR), F32),
        vmem((2, ROWS, D), BF16), vmem((2, ROWS, PAIR), F32),
        vmem((2, CORE, 2 * UNITS), BF16),
        vmem((ROWS, D), F32), vmem((ROWS, D), F32), vmem((ROWS, 2 * UNITS), BF16),
        vmem((ROWS, CORE), BF16),
        vmem((ROWS, D), BF16), vmem((ROWS, D), BF16), vmem((ROWS, D), BF16), vmem((ROWS, D), BF16),
        vmem((ROWS, D), F32),
        vmem((CORE, CORE), BF16), vmem((ROWS, CORE), BF16), vmem((ROWS, D), F32),
        vmem((PAIRS, KEYS, PAIR + LABELS), BF16), vmem((PAIRS, PAIR, KEYS), BF16), vmem((PAIRS, KEYS, PAIR), BF16),
        vmem((KEYS, CORE), F32), vmem((KEYS, CORE), F32),
        vmem((CORE, CORE), BF16), vmem((CORE, 2 * CORE), BF16), vmem((PAIRS, 2, CORE, PAIR), BF16),
        vmem((2, PAIRS, 2, CORE, PAIR), BF16),
        vmem((ROWS, D), BF16), vmem((ROWS, D), BF16),
        vmem((2, 2, PREFIX, CORE), F32), vmem((2, PREFIX, CORE), F32),
        vmem((2, 2, PREFIX, QUARTER), F32), vmem((steps + 2, 2, PREFIX, QUARTER), F32),
        vmem((max(steps, 1), 2, PREFIX, QUARTER), F32),
        pltpu.SemaphoreType.DMA((SEMS,)), pltpu.SemaphoreType.DMA((SEMS,)), pltpu.SemaphoreType.DMA((SEMS,)),
    ]
    anywhere = pl.BlockSpec(memory_space=pl.ANY)
    result = pl.pallas_call(
        functools.partial(fused_kernel, dp),
        out_shape=[
            shape((2, ROWS, D), BF16), shape((2, ROWS, D), F32), shape((2, PREFIX, QUARTER), F32),
            shape((2, 2, D, UNITS), BF16), shape((2, 2, UNITS, D), BF16),
        ],
        in_specs=[anywhere, anywhere, pl.BlockSpec(memory_space=pltpu.VMEM)] + [anywhere] * 6,
        out_specs=[anywhere] * 5,
        scratch_shapes=scratch,
        compiler_params=pltpu.CompilerParams(
            collective_id=0, has_side_effects=True, vmem_limit_bytes=63 << 20
        ),
        name="layers",
    )(states, cotangent, segments, qkv, out_w, up_w, down_w, pre, pack)
    return result[:3]


class Links:
    def __init__(self):
        self.core = lax.axis_index("section")
        self.place = lax.axis_index("tensor")
        self.size = lax.axis_size("tensor")
        self.low = self.place % 2
        self.high = self.place // 2
        self.group = self.size // 2

    def sibling(self, a, only=None):
        pairs = [(0, 1), (1, 0)] if only is None else [(only, 1 - only)]
        return lax.ppermute(a, "section", pairs)

    def across(self, a, only=None):
        if only is None:
            return lax.ppermute(a, "tensor", [(t, t ^ 1) for t in range(self.size)])
        pairs = [(only * self.size + t, only * self.size + (t ^ 1)) for t in range(self.size)]
        return lax.ppermute(a, ("section", "tensor"), pairs)

    def diagonal(self, a, source):
        pairs = [(source * self.size + t, (1 - source) * self.size + (t ^ 1)) for t in range(self.size)]
        return lax.ppermute(a, ("section", "tensor"), pairs)

    def from_ahead(self, a, by):
        g = self.group
        pairs = [(2 * ((h + by) % g) + p, 2 * h + p) for h in range(g) for p in range(2)]
        return lax.ppermute(a, "tensor", pairs)

    def gather(self, a):
        return [a] + [self.from_ahead(a, k) for k in range(1, self.group)]

    def scatter_sum(self, part_fn):
        arrived = [self.from_ahead(part_fn(k).astype(BF16), self.group - k) for k in range(1, self.group)]
        total = part_fn(0)
        for a in arrived:
            total = total + a.astype(F32)
        return total


def forward(links, x, weights, pre, labels):
    qkv_w, out_w, up_w, up_b, down_w, gains, shifts = weights
    width = out_w.shape[0]
    blocks = [dot(b, qkv_w).astype(BF16) for b in links.gather(x)]
    qkv = jnp.concatenate(blocks, 0)
    kv_sib = links.sibling(qkv[:, width:])
    merged, lse = attend(qkv, kv_sib, pre, labels)
    rows = x.shape[0]
    attended = links.scatter_sum(lambda k: dot(merged[k * rows : (k + 1) * rows], out_w)) + shifts[0]
    normed_first, scale_first = norm_stats(x.astype(F32) + attended)
    middle = normed_first * gains[0] + shifts[1]
    blocks = links.gather(middle.astype(BF16))
    pairs = [gelu_pair(dot(b, up_w) + up_b) for b in blocks]
    branch = links.scatter_sum(lambda k: dot(pairs[k][0], down_w)) + shifts[2]
    normed_last, scale_last = norm_stats(middle + branch)
    result = (normed_last * gains[1] + shifts[3]).astype(BF16)
    slopes = [p[1] for p in pairs]
    return result, (qkv, kv_sib, merged, lse, normed_first, scale_first, slopes, normed_last, scale_last)


def backward(links, grad, weights, pre, labels, kept):
    qkv_w, out_w, up_w, up_b, down_w, gains, shifts = weights
    qkv, kv_sib, merged, lse, normed_first, scale_first, slopes, normed_last, scale_last = kept
    rows = grad.shape[0]
    grad_second = norm_back(grad.astype(F32), gains[1], normed_last, scale_last)
    blocks = links.gather(grad_second.astype(BF16))
    hiddens = [
        (dot_t(b, down_w) * s.astype(F32)).astype(BF16) for b, s in zip(blocks, slopes, strict=True)
    ]
    grad_middle = grad_second + links.scatter_sum(lambda k: dot_t(hiddens[k], up_w))
    grad_first = norm_back(grad_middle, gains[0], normed_first, scale_first)
    blocks = links.gather(grad_first.astype(BF16))
    grad_merged = jnp.concatenate([dot_t(b, out_w).astype(BF16) for b in blocks], 0)
    dq, dko, dvo, dks, dvs, dkp, dvp = attend_back(qkv, kv_sib, pre, labels, merged, lse, grad_merged)
    arrived = links.sibling(jnp.concatenate([dks, dvs], 1)).astype(F32)
    width = out_w.shape[0]
    dk = (dko + arrived[:, :width]).astype(BF16)
    dv = (dvo + arrived[:, width:]).astype(BF16)
    dqkv = jnp.concatenate([dq, dk, dv], 1)
    grad_inputs = grad_first + links.scatter_sum(
        lambda k: dot_t(dqkv[k * rows : (k + 1) * rows], qkv_w)
    )
    return grad_inputs, jnp.stack([dkp, dvp])


def spread_weights(links, arrays):
    first = links.core == 0
    layers = ([], [])
    for layer in range(2):
        for a in arrays:
            other = links.across(a, layer)
            sib_a, sib_other = links.sibling(a, layer), links.sibling(other, layer)
            here = links.core == layer
            layers[layer].append((jnp.where(here, a, sib_a), jnp.where(here, other, sib_other)))
    return layers


def sum_over_dp(a):
    size = lax.axis_size("dp")
    step = 1
    if size & (size - 1):
        return lax.psum(a, "dp")
    while step < size:
        a = a + lax.ppermute(a, "dp", [(i, i ^ step) for i in range(size)])
        step *= 2
    return a


def plain(
    states, segment_ids, cotangent, qkv_weight, out_weight, up_weight, up_bias, down_weight,
    norm_gain, shift_vec, prefix,
):
    links = Links()
    first = links.core == 0
    low = links.low

    def arrange(both):
        mine = lax.dynamic_index_in_dim(both, low, 0, keepdims=False)
        other = lax.dynamic_index_in_dim(both, 1 - low, 0, keepdims=False)
        return jnp.where(first, mine, links.across(other, 1))

    x = arrange(states)
    grad = arrange(cotangent)

    segment = lax.dynamic_index_in_dim(segment_ids, low, 0, keepdims=False)
    classes = (segment[-1] - segment).reshape(links.group, 2, -1)
    classes = jnp.roll(classes, -links.high, 0)
    parity = jnp.where(first, low, 1 - low)
    own = lax.dynamic_index_in_dim(classes, parity, 1, keepdims=False).reshape(-1)
    sib = lax.dynamic_index_in_dim(classes, 1 - parity, 1, keepdims=False).reshape(-1)
    numbers = jnp.arange(LABELS)[None, :]
    label_q = (own[:, None] == numbers).astype(BF16)
    known = numbers <= 2 * SPAN
    label_o = jnp.where(known & (own[:, None] != numbers), HIDDEN, 0.0).astype(BF16)
    label_s = jnp.where(known & (sib[:, None] != numbers), HIDDEN, 0.0).astype(BF16)
    labels = (label_q, label_o, label_s)

    small = jnp.concatenate(
        [norm_gain[0], shift_vec[0]], 0
    )
    small_sib = links.sibling(small)
    layers = spread_weights(
        links,
        [jnp.transpose(qkv_weight[0], (1, 0, 2)), prefix[0], out_weight[0], up_weight[0], up_bias, down_weight[0]],
    )
    weights, prefixes = [], []
    for layer in range(2):
        qkv, pre, out, up, bias, down = layers[layer]
        vectors = jnp.where(links.core == layer, small, small_sib).astype(F32)
        weights.append((
            jnp.concatenate([p[i] for i in range(3) for p in qkv], 1),
            jnp.concatenate(out, 0),
            jnp.concatenate(up, 1),
            jnp.concatenate(bias, 1).astype(F32),
            jnp.concatenate(down, 0),
            vectors[:2],
            vectors[2:],
        ))
        prefixes.append(jnp.concatenate(pre, 2))

    y0, kept0 = forward(links, x, weights[0], prefixes[0], labels)
    y1, kept1 = forward(links, y0, weights[1], prefixes[1], labels)
    g1, p1 = backward(links, grad, weights[1], prefixes[1], labels, kept1)
    g0, p0 = backward(links, g1.astype(BF16), weights[0], prefixes[0], labels, kept0)

    def deliver(first_layer, second_layer, wire, dtype):
        near = jnp.where(first, first_layer.astype(dtype), links.sibling(second_layer.astype(wire), 0).astype(dtype))
        far0 = links.diagonal(first_layer.astype(wire), 1)
        far1 = links.across(second_layer.astype(wire), 1)
        far = jnp.where(first, far0, far1).astype(dtype)
        return jnp.stack([jnp.where(low == 0, near, far), jnp.where(low == 0, far, near)])

    hidden_out = deliver(y0, y1, BF16, BF16)
    input_grads = deliver(g0, g1, BF16, F32)

    total = jnp.where(first, p0, p1) + links.sibling(jnp.where(first, p1, p0))
    quarter = total.shape[-1] // 2
    total = total[..., :quarter] + links.across(total[..., quarter:])
    prefix_grads = sum_over_dp(total)
    return hidden_out[None], input_grads[None], prefix_grads[None]


def whole_kernel(
    states, segment_ids, cotangent, qkv_weight, out_weight, up_weight, up_bias, down_weight,
    norm_gain, shift_vec, prefix,
):
    pack = jnp.concatenate([up_bias, norm_gain[0], shift_vec[0], jnp.zeros_like(up_bias)], 0).astype(F32)
    results = fused(
        lax.axis_size("dp"), states, cotangent, segment_ids, jnp.transpose(qkv_weight[0], (1, 0, 2)),
        out_weight[0], up_weight[0], down_weight[0], prefix[0], pack,
    )
    return tuple(r[None] for r in results)


def fits(mesh):
    dp = mesh.shape["dp"]
    return mesh.shape["tensor"] == 4 and dp > 1 and dp & (dp - 1) == 0


def solution(mesh):
    placed = (
        P(None, ("dp", "tensor"), None),
        P(None, "dp"),
        P(None, ("dp", "tensor"), None),
        P("section", None, None, "tensor"),
        P("section", "tensor", None),
        P("section", None, "tensor"),
        P("section", "tensor"),
        P("section", "tensor", None),
        P("section", None, None),
        P("section", None, None),
        P("section", None, None, "tensor"),
    )
    return jax.shard_map(
        whole_kernel if fits(mesh) else plain,
        mesh=mesh,
        in_specs=placed,
        out_specs=(
            P("section", None, ("dp", "tensor"), None),
            P("section", None, ("dp", "tensor"), None),
            P("section", None, None, "tensor"),
        ),
        check_vma=False,
    )
```
